128 devices in a mesh: dp: 64 (over y, x_hi, z, core), tensor: 2 (over x_lo).
Axes of the slice: x: 4 (x_hi: 2, x_lo: 2; x = x_hi * 2 + x_lo), y: 4, z: 4, core: 2. Of those that a mesh axis runs over, the one named last changes fastest.
Arguments:
- tokens: bfloat16 [16384, 1536], P('dp'), may hold values from -6 to 6
- lengths: int32 [64, 4], P('dp'), may hold values from 1 to 128, 256 in all within a row
- keep_mask: int32 [16384], P('dp'), may hold values 0 or 1
- norm1_gain: bfloat16 [1536], replicated, may hold values from 0.099609375 to 1.8984375
- w_query: bfloat16 [1536, 1536], P(None, 'tensor'), may hold values from -0.15625 to 0.15625
- b_query: bfloat16 [12, 128], P('tensor'), may hold values from -3 to 3
- w_key: bfloat16 [1536, 256], P(None, 'tensor'), may hold values from -0.15625 to 0.15625
- b_key: bfloat16 [2, 128], P('tensor'), may hold values from -3 to 3
- w_value: bfloat16 [1536, 256], P(None, 'tensor'), may hold values from -0.15625 to 0.15625
- b_value: bfloat16 [2, 128], P('tensor'), may hold values from -3 to 3
- w_out: bfloat16 [1536, 1536], P('tensor'), may hold values from -0.625 to 0.625
- norm2_gain: bfloat16 [1536], replicated, may hold values from 0.099609375 to 1.8984375
- w_gate: bfloat16 [1536, 8960], P(None, 'tensor'), may hold values from -0.15625 to 0.15625
- w_up: bfloat16 [1536, 8960], P(None, 'tensor'), may hold values from -0.15625 to 0.15625
- w_down: bfloat16 [8960, 1536], P('tensor'), may hold values from -0.0625 to 0.0625
- cotangent: bfloat16 [16384, 1536], P('dp'), may hold values from -6 to 6
Outputs:
- layer_out: bfloat16 [16384, 1536], P('dp')
- d_input: bfloat16 [16384, 1536], P('dp')
- d_norm1_gain: float32 [1536], P('dp')
- d_query: float32 [1536, 1536], P('dp', 'tensor')
- d_bquery: float32 [12, 128], P('tensor')
- d_key: float32 [1536, 256], P('dp', 'tensor')
- d_bkey: float32 [2, 128], P('tensor')
- d_value: float32 [1536, 256], P('dp', 'tensor')
- d_bvalue: float32 [2, 128], P('tensor')
- d_out: float32 [1536, 1536], P('tensor', 'dp')
- d_norm2_gain: float32 [1536], P('dp')
- d_gate: float32 [1536, 8960], P('dp', 'tensor')
- d_up: float32 [1536, 8960], P('dp', 'tensor')
- d_down: float32 [8960, 1536], P('tensor', 'dp')
The draws below stay inside these ranges and needn't reach their ends.
Inputs may be any that keep to these rules, and one draw needn't show every extreme that they name: `lengths`: each row sums to 256, and its longest document has exactly 128 tokens.
All inputs are finite; a program needn't handle non-finite values. No bound on the sum of `keep_mask` on one device may be relied on, other than what follows from the above.
Results may differ from the reference program's by a relative error of at most 0.018.
Values sent between devices are 32-bit elements; how exact they have to be, the bound alone decides.
A program may use at most 320 MiB of HBM per device.

```python
import math
import jax
import jax.numpy as jnp
import numpy as np
from jax import lax

D = 1536
HEADS = 12
KV_HEADS = 2
HEAD_DIM = 128
FF = 8960
TOK_DEV = 256
DOCS = 4
TOKENS = 16384
N_DP = 64


def set_ends(entries, stream_key, least, high):
    longest = entries.shape.index(max(entries.shape))
    spots = []
    for shift in (0, 1):
        where = [jax.random.randint(jax.random.fold_in(stream_key, axis), (), 0, length) for axis, length in enumerate(entries.shape)]
        where[longest] = (where[longest] + shift) % entries.shape[longest]
        spots.append(tuple(where))
    return entries.at[spots[0]].set(least).at[spots[1]].set(high)


def block_scale(rng, shape, pieces, least, top_value):
    def one(dim, blocks):
        heights = jax.random.uniform(jax.random.fold_in(jax.random.fold_in(rng, 6), dim), (blocks,), jnp.float32, least / len(pieces), top_value / len(pieces))
        return jnp.repeat(jnp.exp(heights), shape[dim] // blocks).reshape((-1,) + (1,) * (len(shape) - dim - 1))

    gain = one(*pieces[0])
    for cut in pieces[1:]:
        gain = gain * one(*cut)
    return gain


def split_up(count, total, limit, lean):
    portions = [(1 << 20) // math.isqrt(rank ** lean) + 1 for rank in range(2, count + 1)]
    rest, holding = total - limit - (count - 1), [1] * (count - 1)
    while rest > 0:
        movable = [i for i in range(count - 1) if holding[i] < limit]
        pool, remaining = sum([portions[i] for i in movable]), rest
        for i in movable:
            extra = min(limit - holding[i], max(1, remaining * portions[i] // pool), rest)
            holding[i] = holding[i] + extra
            rest = rest - extra
    return np.array([limit] + holding)


def uneven_parts(own_key, count, total, most, skew):
    if count == 2:
        one = jax.random.randint(own_key, (), max(1, total - most), min(most, total - 1) + 1)
        return jnp.stack([one, total - one])
    tallies = jnp.asarray(split_up(count, total, most, skew), jnp.int32)
    couples = (count - 1) // 2
    giver, taker = tallies[1:1 + 2 * couples:2], tallies[2:2 + 2 * couples:2]
    room = jnp.minimum(giver - 1, most - taker)
    shifted = jax.random.randint(jax.random.fold_in(own_key, 1), (couples,), 0, 1 << 20) % (room + 1)
    tallies = tallies.at[1:1 + 2 * couples:2].set(giver - shifted).at[2:2 + 2 * couples:2].set(taker + shifted)
    return tallies[jax.random.permutation(jax.random.fold_in(own_key, 2), count)]


def normal_values(rng, extent, scale, limit, split=(), kind=jnp.bfloat16):
    entries = scale * jax.random.normal(rng, extent, jnp.float32)
    if split:
        entries = entries * block_scale(rng, extent, split, -0.22, 0.18)
    return jnp.clip(entries, -limit, limit).astype(kind)


def setup_inputs(seed: int = 0) -> dict:
    splits = jax.random.split(jax.random.key(seed), 17)
    return {
        "tokens": normal_values(splits[0], (TOKENS, D), 1.0, 6.0, ((0, 64),)),
        "lengths": jax.vmap(lambda own: uneven_parts(own, DOCS, TOK_DEV, TOK_DEV // 2, 2))(jax.random.split(splits[1], N_DP)).reshape((N_DP, DOCS)).astype(jnp.int32),
        "keep_mask": set_ends((jax.random.randint(splits[2], (TOKENS,), 0, 8) < 7).astype(jnp.int32), jax.random.fold_in(splits[2], 1), 0, 1),
        "norm1_gain": jnp.clip(1.0 + 0.18 * jax.random.normal(splits[3], (D,), jnp.float32), 0.099609375, 1.8984375).astype(jnp.bfloat16),
        "w_query": normal_values(splits[4], (D, HEADS * HEAD_DIM), D ** -0.5, 0.15625, ((1, 2),)),
        "b_query": normal_values(splits[5], (HEADS, HEAD_DIM), 0.5, 3.0, ((0, 2),)),
        "w_key": normal_values(splits[6], (D, KV_HEADS * HEAD_DIM), D ** -0.5, 0.15625, ((1, 2),)),
        "b_key": normal_values(splits[7], (KV_HEADS, HEAD_DIM), 0.5, 3.0, ((0, 2),)),
        "w_value": normal_values(splits[8], (D, KV_HEADS * HEAD_DIM), D ** -0.5, 0.15625, ((1, 2),)),
        "b_value": normal_values(splits[9], (KV_HEADS, HEAD_DIM), 0.5, 3.0, ((0, 2),)),
        "w_out": normal_values(splits[10], (HEADS * HEAD_DIM, D), (HEADS * HEAD_DIM // 16) ** -0.5, 0.625, ((0, 2),)),
        "norm2_gain": jnp.clip(1.0 + 0.18 * jax.random.normal(splits[11], (D,), jnp.float32), 0.099609375, 1.8984375).astype(jnp.bfloat16),
        "w_gate": normal_values(splits[12], (D, FF), D ** -0.5, 0.15625, ((1, 2),)),
        "w_up": normal_values(splits[13], (D, FF), D ** -0.5, 0.15625, ((1, 2),)),
        "w_down": normal_values(splits[14], (FF, D), FF ** -0.5, 0.0625, ((0, 2),)),
        "cotangent": normal_values(splits[15], (TOKENS, D), 1.0, 6.0, ((0, 64),)),
    }


EPS = 1e-06
ROPE_BASE = 10000.0
NEG_FILL = -1e+30

@jax.custom_vjp
def low(v):
    return lax.optimization_barrier(v.astype(jnp.bfloat16)).astype(jnp.float32)

@jax.custom_vjp
def low_back(v):
    return v

def low_keep(v):
    return (low(v), None)

def low_pass(kept, grad):
    return (grad,)

def back_keep(v):
    return (v, None)

def back_low(kept, grad):
    return (low(grad),)
low.defvjp(low_keep, low_pass)
low_back.defvjp(back_keep, back_low)

def rms_scale(values):
    return lax.rsqrt(lax.optimization_barrier(jnp.mean(values * values, axis=-1, keepdims=True)) + EPS)

def rotate(values):
    half_width = values.shape[-1] // 2
    return jnp.concatenate([-values[..., half_width:], values[..., :half_width]], axis=-1)

def tables(length_row, tok_count, width):
    positions = jnp.arange(tok_count, dtype=jnp.int32)
    doc_ends = jnp.cumsum(length_row).astype(jnp.int32)
    passed = (positions[:, None] >= doc_ends[None, :]).astype(jnp.int32)
    segment = lax.optimization_barrier(jnp.sum(passed, axis=1)).astype(jnp.int32)
    doc_place = positions - lax.optimization_barrier(jnp.sum(passed * length_row[None, :], axis=1)).astype(jnp.int32)
    inv_freq = ROPE_BASE ** (-jnp.arange(0, width, 2).astype(jnp.float32) / width)
    angles = doc_place.astype(jnp.float32)[:, None] * inv_freq[None, :]
    angles = jnp.concatenate([angles, angles], axis=1)
    return (segment, jnp.cos(angles), jnp.sin(angles))

def layer(input_rows, first_norm_gain, w_query, b_query, w_key, b_key, w_value, b_value, w_out, second_norm_gain, w_gate, w_up, w_down, allowed, cosine, sine_table):
    highest = lax.Precision.HIGHEST
    block_count, row_count = (allowed.shape[0], allowed.shape[1])
    group_count = HEADS // KV_HEADS
    first_normed = low(input_rows * rms_scale(input_rows) * first_norm_gain)
    q_pre = low_back(jnp.dot(first_normed, w_query, precision=highest) + b_query.reshape(-1))
    k_pre = low_back(jnp.dot(first_normed, w_key, precision=highest) + b_key.reshape(-1))
    v_low = low(low_back(jnp.dot(first_normed, w_value, precision=highest) + b_value.reshape(-1)))
    cos_h = cosine[:, :, None, :]
    sin_h = sine_table[:, :, None, :]
    q_four = q_pre.reshape(block_count, row_count, HEADS, HEAD_DIM)
    queries = low((q_four * cos_h + rotate(q_four) * sin_h) * HEAD_DIM ** (-0.5))
    queries = queries.reshape(block_count, row_count, KV_HEADS, group_count, HEAD_DIM)
    k_four = k_pre.reshape(block_count, row_count, KV_HEADS, HEAD_DIM)
    keys = low(k_four * cos_h + rotate(k_four) * sin_h)
    v_four = v_low.reshape(block_count, row_count, KV_HEADS, HEAD_DIM)
    raw_scores = low_back(jnp.einsum('ntkgd,nskd->nkgts', queries, keys, precision=highest))
    scores = jnp.where(allowed[:, None, None], raw_scores, NEG_FILL)
    row_top = lax.optimization_barrier(jnp.max(scores, axis=-1, keepdims=True))
    exp_scores = jnp.exp(scores - row_top)
    soft_low = low(exp_scores / lax.optimization_barrier(jnp.sum(exp_scores, axis=-1, keepdims=True)))
    attn_mix = jnp.einsum('nkgts,nskd->ntkgd', soft_low, v_four, precision=highest)
    attn_mix = low(low_back(attn_mix.reshape(block_count * row_count, HEADS * HEAD_DIM)))
    attn_branch = low_back(jnp.dot(attn_mix, w_out, precision=highest))
    residual_stream = input_rows + attn_branch
    second_normed = low(residual_stream * rms_scale(residual_stream) * second_norm_gain)
    gate_pre = low_back(jnp.dot(second_normed, w_gate, precision=highest))
    up_pre = low_back(jnp.dot(second_normed, w_up, precision=highest))
    hidden_low = low(jax.nn.silu(gate_pre) * up_pre)
    return residual_stream + low_back(jnp.dot(hidden_low, w_down, precision=highest))

def reference(tokens, lengths, keep_mask, norm1_gain, w_query, b_query, w_key, b_key, w_value, b_value, w_out, norm2_gain, w_gate, w_up, w_down, cotangent):
    segment, cosine, sine_table = jax.vmap(lambda length_row: tables(length_row, TOK_DEV, HEAD_DIM))(lengths)
    positions = jnp.arange(TOK_DEV, dtype=jnp.int32)
    keep_rows = keep_mask.reshape(N_DP, TOK_DEV)
    allowed = (segment[:, :, None] == segment[:, None, :]) & (positions[None, None, :] <= positions[None, :, None]) & ((keep_rows[:, None, :] == 1) | (positions[None, None, :] == positions[None, :, None]))
    floats = [item.astype(jnp.float32) for item in (tokens, norm1_gain, w_query, b_query, w_key, b_key, w_value, b_value, w_out, norm2_gain, w_gate, w_up, w_down)]

    def forward(*params):
        return layer(*params, allowed, cosine, sine_table)
    layer_out, pull_back = jax.vjp(forward, *floats)
    gradients = pull_back(cotangent.astype(jnp.float32))
    return (layer_out.astype(jnp.bfloat16), gradients[0].astype(jnp.bfloat16), gradients[1], gradients[2], gradients[3], gradients[4], gradients[5], gradients[6], gradients[7], gradients[8], gradients[9], gradients[10], gradients[11], gradients[12])
```

```python
import functools

import jax
import jax.numpy as jnp
from jax import lax
from jax.experimental import pallas as pl
from jax.experimental.pallas import tpu as pltpu
from jax.sharding import PartitionSpec as P

EPS = 1e-06
ROPE_BASE = 10000.0
NEG_FILL = -1e30
MESH = pl.DeviceIdType.MESH
BF = jnp.bfloat16
F32 = jnp.float32
VM = pltpu.VMEM

D = 1536
TOK = 256
HALF = 128
HEADS = 6
WIDTH = 128
QW = HEADS * WIDTH
FFL = 4480
FFW = 1152
OFFS = (0, 1152, 2304, 3328)

UW = 256
NU = 17
GATE_UNITS = 9
G_SLOTS = 8
R_SLOTS = 3
N_TICK = NU + 6


def coords():
    dp = lax.axis_index("dp")
    t = lax.axis_index("tensor")
    return dp // 16, lax.rem(dp // 8, 2), lax.rem(dp // 2, 4), lax.rem(dp, 2), t


def device(y, xh, z, c, t):
    return (((y * 2 + xh) * 4 + z) * 2 + c, t)


def device_x(y, x, z, c):
    return device(y, x // 2, z, c, lax.rem(x, 2))


def remote(src, dst, send, recv, to):
    return pltpu.make_async_remote_copy(
        src_ref=src, dst_ref=dst, send_sem=send, recv_sem=recv, device_id=to, device_id_type=MESH
    )


def greet(devices):
    barrier = pltpu.get_barrier_semaphore()
    for to in devices:
        pl.semaphore_signal(barrier, inc=1, device_id=to, device_id_type=MESH)
    pl.semaphore_wait(barrier, len(devices))


def dot(left, right):
    return jnp.dot(left, right, preferred_element_type=F32)


def dot_nt(left, right):
    return lax.dot_general(left, right, (((1,), (1,)), ((), ())), preferred_element_type=F32)


def dot_tn(left, right):
    return lax.dot_general(left, right, (((0,), (0,)), ((), ())), preferred_element_type=F32)


def rope(v, cosine, sine):
    return v * cosine + pltpu.roll(v, WIDTH // 2, 1) * sine


def rope_back(w, cosine, sine):
    return w * cosine + pltpu.roll(w * sine, WIDTH // 2, 1)


def mean_last(v):
    return jnp.mean(v, axis=-1, keepdims=True)


def front_kernel(
    tokens, cot, lengths, keep, inv_freq, g1, wq, bq, wk, bk, wv, bv, wo, g2,
    q_o, k_o, v_o, mask_o, cos_o, sin_o, h1_o, n2_o, n2t_o, dy_o, dyt_o, la_o, o2_o,
    n2f, dyf, n1f, n1r, of, orr, part, prec, ss, rs,
):
    y, xh, z, c, t = coords()
    x = 2 * xh + t
    right = device_x(y, lax.rem(x + 1, 4), z, c)
    left = device_x(y, lax.rem(x + 3, 4), z, c)
    core = device(y, xh, z, 1 - c, t)
    mate = device(y, xh, z, c, 1 - t)
    cross = device_x(y, 3 - x, z, c)
    greet((right, left, core))
    me = 2 * xh + c
    mine = pl.ds(pl.multiple_of(t * HALF, HALF), HALF)
    other = pl.ds(pl.multiple_of((1 - t) * HALF, HALF), HALF)

    def send(i, src, dst, to):
        copy = remote(src, dst, ss.at[i], rs.at[i], to)
        copy.start()
        return copy

    dyf[me] = cot[...].astype(F32)
    dy_cross = send(0, dyf.at[me, mine], dyf.at[me, mine], cross)
    dy_core = send(1, dyf.at[me], dyf.at[me], core)

    rows = lax.broadcasted_iota(jnp.int32, (TOK, TOK), 0)
    cols = lax.broadcasted_iota(jnp.int32, (TOK, TOK), 1)
    place = lax.broadcasted_iota(jnp.int32, (TOK, WIDTH), 0)
    row_id = place
    seg_r = jnp.zeros((TOK, TOK), jnp.int32)
    seg_c = jnp.zeros((TOK, TOK), jnp.int32)
    end = jnp.int32(0)
    for i in range(4):
        span = lengths[0, i]
        end = end + span
        seg_r = seg_r + (rows >= end).astype(jnp.int32)
        seg_c = seg_c + (cols >= end).astype(jnp.int32)
        place = place - jnp.where(row_id >= end, span, 0)
    allowed = (seg_r == seg_c) & (cols <= rows) & ((keep[...] == 1) | (cols == rows))
    mask_o[...] = allowed.astype(F32)
    angle = place.astype(F32) * inv_freq[...]
    lane = lax.broadcasted_iota(jnp.int32, (TOK, WIDTH), 1)
    cosine = jnp.cos(angle)
    sine = jnp.sin(angle) * jnp.where(lane < WIDTH // 2, -1.0, 1.0)
    cos_o[...] = cosine
    sin_o[...] = sine

    xf = tokens[...].astype(F32)
    r1 = lax.rsqrt(mean_last(xf * xf) + EPS)
    n1 = (xf * r1 * g1[...]).astype(BF)
    n1f[...] = n1.astype(F32)
    n1_core = send(2, n1f, n1r, core)
    kp = dot(n1, wk[...]) + bk[...]
    k_o[...] = rope(kp, cosine, sine).astype(BF)
    v_o[...] = (dot(n1, wv[...]) + bv[...]).astype(BF)
    for h in range(HEADS):
        at = slice(h * WIDTH, (h + 1) * WIDTH)
        qp = dot(n1, wq[:, at]) + bq[:, at]
        q_o[:, at] = (rope(qp, cosine, sine) * WIDTH**-0.5).astype(BF)

    def head(h, _):
        at = pl.ds(pl.multiple_of(h * WIDTH, WIDTH), WIDTH)
        s = jnp.where(mask_o[...] > 0.5, dot_nt(q_o[:, at], k_o[...]), NEG_FILL)
        e = jnp.exp(s - jnp.max(s, axis=-1, keepdims=True))
        soft = (e / jnp.sum(e, axis=-1, keepdims=True)).astype(BF)
        o = dot(soft, v_o[...]).astype(BF)
        o2_o[:TOK, at] = o
        of[:, at] = o.astype(F32)
        return 0

    lax.fori_loop(0, HEADS, head, 0)
    part[0] = dot(o2_o[other, :], wo[...])
    half = send(3, part.at[0], prec, mate)
    o_core = send(4, of, orr, core)
    part[1] = dot(o2_o[mine, :], wo[...])

    dy_cross.wait_recv()
    far = 2 * (1 - xh) + c
    dy_pass = send(5, dyf.at[far, other], dyf.at[far, other], mate)

    half.wait_recv()
    h1 = tokens[mine, :].astype(F32) + part[1] + prec[...]
    h1_o[...] = h1
    r2 = lax.rsqrt(mean_last(h1 * h1) + EPS)
    n2f[me, mine] = (h1 * r2 * g2[...]).astype(BF).astype(F32)

    own = n2f.at[me, mine]
    to_right = send(6, own, own, right)
    to_left = send(7, own, own, left)
    to_core = send(8, own, own, core)

    la_o[:, :TOK] = n1.T
    n1_core.wait_recv()
    la_o[:, TOK:] = n1r[...].astype(BF).T
    o_core.wait_recv()
    o2_o[TOK:, :] = orr[...].astype(BF)

    def dy_block(b):
        low = dyf[b].astype(BF)
        at = pl.ds(pl.multiple_of(b * TOK, TOK), TOK)
        dy_o[at, :] = low
        dyt_o[:, at] = low.T

    dy_block(me)
    dy_core.wait_recv()
    dy_block(2 * xh + 1 - c)

    def slot(xx):
        return n2f.at[2 * (xx // 2) + c, pl.ds(pl.multiple_of(lax.rem(xx, 2) * HALF, HALF), HALF)]

    def lower(ref):
        return ref.at[pl.ds(0, HALF // 2)]

    def upper(ref):
        return ref.at[pl.ds(HALF // 2, HALF // 2)]

    from_left = slot(lax.rem(x + 3, 4))
    from_right = slot(lax.rem(x + 1, 4))
    to_right.wait_recv()
    pass_right = send(9, lower(from_left), lower(from_left), right)
    core_left = send(10, from_left, from_left, core)
    to_left.wait_recv()
    pass_left = send(11, upper(from_right), upper(from_right), left)
    core_right = send(12, from_right, from_right, core)

    dy_pass.wait_recv()
    dy_far = send(13, dyf.at[far], dyf.at[far], core)
    dy_block(far)

    pass_right.wait_recv()
    pass_left.wait_recv()
    across = slot(lax.rem(x + 2, 4))
    core_across = send(14, across, across, core)
    dy_far.wait_recv()
    dy_block(2 * (1 - xh) + 1 - c)

    def n2_block(b):
        low = n2f[b].astype(BF)
        at = pl.ds(pl.multiple_of(b * TOK, TOK), TOK)
        n2_o[at, :] = low
        n2t_o[:, at] = low.T

    n2_block(me)
    n2_block(far)
    to_core.wait_recv()
    core_left.wait_recv()
    core_right.wait_recv()
    core_across.wait_recv()
    n2_block(2 * xh + 1 - c)
    n2_block(2 * (1 - xh) + 1 - c)
    for copy in (
        dy_cross, dy_core, n1_core, half, o_core, dy_pass, to_right, to_left, to_core,
        pass_right, core_left, pass_left, core_right, dy_far, core_across,
    ):
        copy.wait_send()


def front(*args):
    shape = jax.ShapeDtypeStruct
    whole = pl.BlockSpec(memory_space=VM)
    scalars = pl.BlockSpec(memory_space=pltpu.SMEM)
    return pl.pallas_call(
        front_kernel,
        name="front",
        out_shape=(
            shape((TOK, QW), BF), shape((TOK, WIDTH), BF), shape((TOK, WIDTH), BF),
            shape((TOK, TOK), F32), shape((TOK, WIDTH), F32), shape((TOK, WIDTH), F32),
            shape((HALF, D), F32),
            shape((4 * TOK, D), BF), shape((D, 4 * TOK), BF),
            shape((4 * TOK, D), BF), shape((D, 4 * TOK), BF),
            shape((D, 2 * TOK), BF), shape((2 * TOK, QW), BF),
        ),
        in_specs=[whole, whole, scalars] + [whole] * 11,
        out_specs=(whole,) * 13,
        scratch_shapes=[
            VM((4, TOK, D), F32), VM((4, TOK, D), F32),
            VM((TOK, D), F32), VM((TOK, D), F32),
            VM((TOK, QW), F32), VM((TOK, QW), F32),
            VM((2, HALF, D), F32), VM((HALF, D), F32),
            pltpu.SemaphoreType.DMA((15,)), pltpu.SemaphoreType.DMA((15,)),
        ],
        compiler_params=pltpu.CompilerParams(
            collective_id=1, has_side_effects=True, vmem_limit_bytes=60 * 2**20
        ),
    )(*args)


def ffn_kernel(n2, dy, wg_hbm, wu_hbm, wd_hbm, dgu_o, a_o, dn2_o, out_o, wg, wu, wd, sem):
    _, xh, _, c, _ = coords()
    me = 2 * xh + c
    start = pl.multiple_of((me * 9 - me // 3) * 128, 128)
    at = pl.ds(start, FFW)
    copies = [
        pltpu.make_async_copy(wg_hbm.at[:, at], wg, sem.at[0]),
        pltpu.make_async_copy(wu_hbm.at[:, at], wu, sem.at[1]),
        pltpu.make_async_copy(wd_hbm.at[at, :], wd, sem.at[2]),
    ]
    for copy in copies:
        copy.start()
    lane = lax.broadcasted_iota(jnp.int32, (1, FFW), 1)
    live = jnp.where((lane < 128) & (me == 3), 0.0, 1.0)
    for copy in copies:
        copy.wait()

    def block(i, _):
        rows = pl.ds(pl.multiple_of(i * TOK, TOK), TOK)
        g = dot(n2[rows, :], wg[...])
        u = dot(n2[rows, :], wu[...])
        sg = live / (1.0 + jnp.exp(-g))
        silu = g * sg
        a = (silu * u).astype(BF)
        a_o[rows, :] = a
        da = dot_nt(dy[rows, :], wd[...])
        dg = (da * u * sg * (1.0 + g * (1.0 - sg))).astype(BF)
        du = (da * silu).astype(BF)
        dgu_o[rows, :FFW] = dg
        dgu_o[rows, FFW:] = du
        dn2_o[rows, :] = dot_nt(dg, wg[...]) + dot_nt(du, wu[...])
        out_o[rows, :] = dot(a, wd[...])
        return 0

    lax.fori_loop(0, 4, block, 0)


def ffn(*args):
    shape = jax.ShapeDtypeStruct
    whole = pl.BlockSpec(memory_space=VM)
    hbm = pl.BlockSpec(memory_space=pl.ANY)
    return pl.pallas_call(
        ffn_kernel,
        name="ffn",
        out_shape=(
            shape((4 * TOK, 2 * FFW), BF), shape((4 * TOK, FFW), BF),
            shape((4 * TOK, D), F32), shape((4 * TOK, D), F32),
        ),
        in_specs=[whole, whole, hbm, hbm, hbm],
        out_specs=(whole,) * 4,
        scratch_shapes=[
            VM((D, FFW), BF), VM((D, FFW), BF), VM((FFW, D), BF), pltpu.SemaphoreType.DMA((3,)),
        ],
        compiler_params=pltpu.CompilerParams(vmem_limit_bytes=60 * 2**20),
    )(*args)


def back_kernel(
    n2t, dyt, dgu_h, a_h, dn2_h, out_h, la, o2, tokens, cot, h1, q, k, v, mask, cos, sin,
    g1, g2, wq, wk, wv, wo,
    gate_o, up_o, down_o, dq_o, dk_o, dv_o, dout_o, lout_o, din_o, small_o,
    F, G, R1, R2, RB, C, L, S1, S2, dhf, dhr, dh, lb, do, dqf, xqr, rq, dkvf, xkvr, rkv,
    dn1, dn1r, dir, lof, small, sb,
    ss, rs, fss, frs, credit, xss, xrs, free, lsem, bsem, sss, srs,
):
    y, xh, z, c, t = coords()
    x = 2 * xh + t
    me = 2 * xh + c
    by_y = tuple(device(lax.rem(y + i, 4), xh, z, c, t) for i in (1, 2, 3))
    by_z = tuple(device(y, xh, lax.rem(z + i, 4), c, t) for i in (1, 2, 3))
    ring = {"y": (by_y[0], by_y[2]), "z": (by_z[0], by_z[2])}
    right = device_x(y, lax.rem(x + 1, 4), z, c)
    left = device_x(y, lax.rem(x + 3, 4), z, c)
    core = device(y, xh, z, 1 - c, t)
    mate = device(y, xh, z, c, 1 - t)
    over = device(y, 1 - xh, z, c, t)
    over_core = device(y, 1 - xh, z, 1 - c, t)
    peers = (None, core, over, over_core)
    greet(by_y + by_z + (right, left, core, over, over_core))
    mine = pl.ds(pl.multiple_of(t * HALF, HALF), HALF)
    other = pl.ds(pl.multiple_of((1 - t) * HALF, HALF), HALF)

    def way(j, stage):
        axis = "y" if (j // 2 == 0) == (stage == 0) else "z"
        return axis, (y if axis == "y" else z), (1 if j % 2 == 0 else -1)

    def chunk(g, j, stage, i):
        jx, jc = j // 2, j % 2
        if stage == 0:
            return G.at[g, i, 0, :, jc] if jx == 0 else G.at[g, :, 1, i, jc]
        return G.at[g, y, 0, i, jc] if jx == 0 else G.at[g, i, 1, z, jc]

    def step_copy(u, s, j):
        stage, n = (0, s) if s <= 3 else (1, s - 3)
        axis, p, d = way(j, stage)
        g, r = lax.rem(u, G_SLOTS), lax.rem(u, R_SLOTS)
        return remote(
            chunk(g, j, stage, lax.rem(p - d * n + 8, 4)),
            (R2 if stage else R1).at[r, n - 1, j],
            ss.at[r, s - 1, j],
            rs.at[r, s - 1, j],
            ring[axis][0 if d == 1 else 1],
        )

    def last_copy(u, n):
        px = 1 - xh if n & 2 else xh
        pc = 1 - c if n & 1 else c
        return remote(
            G.at[lax.rem(u, G_SLOTS), y, px, z, pc],
            F.at[me, u],
            fss.at[u, n - 1],
            frs.at[u, n - 1],
            peers[n],
        )

    def load(u, act):
        r = lax.rem(u, 2)

        @pl.when(u < 9)
        def _():
            at = pl.ds(pl.multiple_of(u * UW, UW), UW)
            act(pltpu.make_async_copy(dgu_h.at[:, at], RB.at[r], bsem.at[r]))

        @pl.when((u >= 9) & (u < 13))
        def _():
            at = pl.ds(pl.multiple_of((u - 9) * UW, UW), UW)
            act(pltpu.make_async_copy(a_h.at[:, at], RB.at[r], bsem.at[r]))

        @pl.when(u == 13)
        def _():
            act(pltpu.make_async_copy(a_h.at[:, pl.ds(1024, 128)], RB.at[r, :, pl.ds(0, 128)], bsem.at[r]))

    def product(g, left_ref, rhs, w, o0):
        def body(i, _):
            lhs = left_ref[pl.ds(pl.multiple_of(i * 384, 384), 384), :]
            G[g, i, :, :, :, :, o0 : o0 + w] = dot(lhs, rhs).reshape(2, 4, 2, 24, w)
            return 0

        lax.fori_loop(0, 4, body, 0)

    def grads(u):
        g = lax.rem(u, G_SLOTS)

        @pl.when(u >= G_SLOTS)
        def _():
            for n in range(1, 4):
                last_copy(u - G_SLOTS, n).wait_send()

        load(u, lambda copy: copy.wait())

        @pl.when(u < 9)
        def _():
            product(g, n2t, RB[lax.rem(u, 2)], UW, 0)

        @pl.when((u >= 9) & (u < 13))
        def _():
            product(g, dyt, RB[lax.rem(u, 2)], UW, 0)

        @pl.when(u == 13)
        def _():
            product(g, dyt, RB[1, :, 0:128], 128, 0)
            product(g, la, rkv[...], 128, 128)

        @pl.when(u >= 14)
        def _():
            product(g, lb, rq[:, pl.ds(pl.multiple_of((u - 14) * UW, UW), UW)], UW, 0)

        load(u + 2, lambda copy: copy.start())

    def xcopy(i, src, dst, to):
        return remote(src, dst, xss.at[i], xrs.at[i], to)

    def core_copies(base, src):
        return [
            xcopy(base + b, src.at[pl.ds(pl.multiple_of((2 * b + 1 - c) * TOK, TOK), TOK)], C.at[b], core)
            for b in range(2)
        ]

    def local_copies(src):
        return [
            pltpu.make_async_copy(
                src.at[pl.ds(pl.multiple_of((2 * b + c) * TOK, TOK), TOK)], L.at[b], lsem.at[b]
            )
            for b in range(2)
        ]

    def lrow(xx, lo, n):
        return L.at[xx // 2, pl.ds(pl.multiple_of(lax.rem(xx, 2) * HALF + lo, 64), n)]

    x1, x2, x3 = lax.rem(x + 1, 4), lax.rem(x + 2, 4), lax.rem(x + 3, 4)

    def ring1(base):
        return [
            xcopy(base + 2, lrow(x2, 0, 64), S1.at[0], right),
            xcopy(base + 3, lrow(x2, 64, 64), S1.at[1], left),
        ]

    def ring2(base):
        return [
            xcopy(base + 4, lrow(x1, 0, HALF), S2.at[0], right),
            xcopy(base + 5, lrow(x3, 0, HALF), S2.at[1], left),
        ]

    def x_begin(base, src, first):
        if not first:
            pl.semaphore_wait(free.at[0], 1)
        for copy in core_copies(base, src) + local_copies(src):
            copy.start()

    def x_ring1(base, src, first):
        for copy in core_copies(base, src) + local_copies(src):
            copy.wait()

        def add(i, _):
            at = pl.ds(pl.multiple_of(i * 64, 64), 64)
            for b in range(2):
                L[b, at] = L[b, at] + C[b, at]
            return 0

        lax.fori_loop(0, TOK // 64, add, 0)
        if first:
            pl.semaphore_signal(free.at[0], inc=1, device_id=core, device_id_type=MESH)
        else:
            pl.semaphore_wait(free.at[1], 1)
            pl.semaphore_wait(free.at[2], 1)
        for copy in ring1(base):
            copy.start()

    def x_ring2(base):
        for copy in ring1(base):
            copy.wait()
        low, high = lrow(x1, 0, 64), lrow(x3, 64, 64)
        low[...] = low[...] + S1[0]
        high[...] = high[...] + S1[1]
        for copy in ring2(base):
            copy.start()

    def x_end(base, first):
        for copy in ring2(base):
            copy.wait()
        total = lrow(x, 0, HALF)[...] + S2[0] + S2[1]
        if first:
            pl.semaphore_signal(free.at[1], inc=1, device_id=right, device_id_type=MESH)
            pl.semaphore_signal(free.at[2], inc=1, device_id=left, device_id_type=MESH)
        return total

    dh_copy = xcopy(12, dhf.at[mine], dhf.at[mine], mate)
    dh_core = xcopy(13, dhf, dhr, core)
    q_core = xcopy(14, dqf, xqr, core)
    kv_core = xcopy(15, dkvf, xkvr, core)
    dn1_copy = xcopy(16, dn1.at[other], dn1r, mate)
    lo_copy = xcopy(17, lof.at[mine], lof.at[mine], mate)
    di_copy = xcopy(18, dn1.at[mine], dir, mate)

    def second_norm():
        dn2 = x_end(0, True)
        hh = h1[...]
        r2 = lax.rsqrt(mean_last(hh * hh) + EPS)
        normed = hh * r2
        e = dn2 * g2[...]
        grad = cot[mine, :].astype(F32) + r2 * (e - normed * mean_last(e * normed))
        dh[...] = grad
        dhf[mine, :] = grad.astype(BF).astype(F32)
        dh_copy.start()
        small[...] = jnp.zeros_like(small)
        small[0:1, :] = jnp.sum(dn2 * normed, axis=0, keepdims=True)

    def mix_grad():
        dh_copy.wait()
        dh_core.start()
        do[...] = dot_nt(dhf[...].astype(BF), wo[...]).astype(BF)
        dkvf[...] = jnp.zeros_like(dkvf)

    def heads(lo, hi):
        def body(h, _):
            at = pl.ds(pl.multiple_of(h * WIDTH, WIDTH), WIDTH)
            qh, doh = q[:, at], do[:, at]
            s = jnp.where(mask[...] > 0.5, dot_nt(qh, k[...]), NEG_FILL)
            e = jnp.exp(s - jnp.max(s, axis=-1, keepdims=True))
            soft = e / jnp.sum(e, axis=-1, keepdims=True)
            dp = dot_nt(doh, v[...])
            dz = (soft * (dp - jnp.sum(soft * dp, axis=-1, keepdims=True))).astype(BF)
            dq = dot(dz, k[...]) * WIDTH**-0.5
            dqf[:, at] = rope_back(dq, cos[...], sin[...]).astype(BF).astype(F32)
            dkvf[0] = dkvf[0] + dot_tn(dz, qh)
            dkvf[1] = dkvf[1] + dot_tn(soft.astype(BF), doh)
            return 0

        lax.fori_loop(lo, hi, body, 0)

    def head_end():
        dkvf[0] = rope_back(dkvf[0], cos[...], sin[...]).astype(BF).astype(F32)
        dkvf[1] = dkvf[1].astype(BF).astype(F32)
        q_core.start()
        kv_core.start()
        small[2:3, 0:QW] = jnp.sum(dqf[...], axis=0, keepdims=True)
        small[2:3, QW : QW + WIDTH] = jnp.sum(dkvf[0], axis=0, keepdims=True)
        small[2:3, QW + WIDTH : QW + 2 * WIDTH] = jnp.sum(dkvf[1], axis=0, keepdims=True)

    def input_grad():
        dn1[...] = (
            dot_nt(dqf[...].astype(BF), wq[...])
            + dot_nt(dkvf[0].astype(BF), wk[...])
            + dot_nt(dkvf[1].astype(BF), wv[...])
        )
        xf = tokens[...].astype(F32)
        normed = xf * lax.rsqrt(mean_last(xf * xf) + EPS)
        small[1:2, :] = jnp.sum(dn1[...] * normed, axis=0, keepdims=True)
        dn1_copy.start()

    def exchange_end():
        q_core.wait()
        kv_core.wait()
        dh_core.wait()
        rkv[:TOK, :] = dkvf[c].astype(BF)
        rkv[TOK:, :] = xkvr[c].astype(BF)

        @pl.when(c == 0)
        def _():
            rq[:TOK, :] = dqf[...].astype(BF)
            rq[TOK:, :] = xqr[...].astype(BF)
            lb[...] = la[...]

        @pl.when(c == 1)
        def _():
            rq[...] = o2[...]
            lb[:, :TOK] = dhf[...].astype(BF).T
            lb[:, TOK:] = dhr[...].astype(BF).T

    def layer_end():
        lof[mine, :] = (h1[...] + x_end(6, False)).astype(BF).astype(F32)
        lo_copy.start()

    def input_end():
        dn1_copy.wait()
        total = dn1[mine, :] + dn1r[...]
        xf = tokens[mine, :].astype(F32)
        r1 = lax.rsqrt(mean_last(xf * xf) + EPS)
        normed = xf * r1
        e = total * g1[...]
        grad = dh[...] + r1 * (e - normed * mean_last(e * normed))
        dn1[mine, :] = grad.astype(BF).astype(F32)
        di_copy.start()

    def small_copy(i, slot, to):
        return remote(small, sb.at[slot], sss.at[i], srs.at[i], to)

    pair = [small_copy(i, i, to) for i, to in enumerate((mate, core, over))]
    quad_y = [small_copy(3 + i, 3 + y, by_y[i]) for i in range(3)]
    quad_z = [small_copy(6 + i, 7 + z, by_z[i]) for i in range(3)]

    def small_add(i):
        pair[i].wait()
        got = sb[i]
        if i == 0:
            got = jnp.where(lax.broadcasted_iota(jnp.int32, got.shape, 0) < 2, got, 0.0)
        small[...] = small[...] + got

    def small_quad(copies, base, p):
        for copy in copies:
            copy.wait()
        sb[base + p] = small[...]
        small[...] = ((sb[base] + sb[base + 1]) + sb[base + 2]) + sb[base + 3]

    def start(copies):
        for copy in copies:
            copy.start()

    extras = {
        0: [lambda: x_begin(0, dn2_h, True)],
        1: [lambda: x_ring1(0, dn2_h, True)],
        3: [lambda: x_ring2(0)],
        5: [second_norm, lambda: x_begin(6, out_h, False)],
        6: [lambda: x_ring1(6, out_h, False)],
        7: [mix_grad],
        8: [lambda: heads(0, 3)],
        9: [lambda: heads(3, 6), head_end],
        10: [input_grad, lambda: start(pair[:1]), lambda: x_ring2(6)],
        11: [exchange_end, lambda: small_add(0), lambda: start(pair[1:2])],
        12: [layer_end, lambda: small_add(1), lambda: start(pair[2:])],
        13: [input_end, lambda: small_add(2), lambda: start(quad_y)],
        14: [lambda: small_quad(quad_y, 3, y), lambda: start(quad_z)],
        15: [lambda: small_quad(quad_z, 7, z)],
    }

    load(jnp.int32(0), lambda copy: copy.start())
    load(jnp.int32(1), lambda copy: copy.start())
    grads(jnp.int32(0))

    def tick(n, _):
        @pl.when((n >= R_SLOTS) & (n <= NU + 4))
        def _():
            for i in range(4):
                pl.semaphore_wait(credit.at[i], 1)

        @pl.when(n < NU)
        def _():
            for j in range(4):
                step_copy(n, 1, j).start()

        for s in range(1, 7):
            u = n - s
            stage, m = (0, s) if s <= 3 else (1, s - 3)

            @pl.when((u >= 0) & (u < NU))
            def _():
                g, r = lax.rem(u, G_SLOTS), lax.rem(u, R_SLOTS)
                for j in range(4):
                    copy = step_copy(u, s, j)
                    copy.wait_recv()
                    _, p, d = way(j, stage)
                    at = chunk(g, j, stage, lax.rem(p - d * (m + 1) + 8, 4))
                    at[...] = at[...] + (R2 if stage else R1)[r, m - 1, j]
                    if s < 6:
                        step_copy(u, s + 1, j).start()
                    copy.wait_send()
                if s == 6:
                    for i in range(1, 4):
                        last_copy(u, i).start()
                    F[me, u] = G[g, y, xh, z, c]

        @pl.when((n >= 1) & (n <= NU + 5 - R_SLOTS))
        def _():
            for i, to in enumerate((ring["y"][1], ring["y"][0], ring["z"][1], ring["z"][0])):
                pl.semaphore_signal(credit.at[i], inc=1, device_id=to, device_id_type=MESH)

        @pl.when(n + 1 < NU)
        def _():
            grads(n + 1)

        for when, steps in extras.items():

            @pl.when(n == when)
            def _():
                for step in steps:
                    step()

        return 0

    lax.fori_loop(0, N_TICK, tick, 0)

    lo_copy.wait()
    lout_o[...] = lof[...].astype(BF)
    di_copy.wait()
    din_o[mine, :] = dn1[mine, :].astype(BF)
    din_o[other, :] = dir[...].astype(BF)
    small_o[...] = small[...]

    def finish(u, _):
        for n in range(1, 4):
            last_copy(u, n).wait_recv()

            @pl.when(u >= NU - G_SLOTS)
            def _():
                last_copy(u, n).wait_send()

        return 0

    lax.fori_loop(0, NU, finish, 0)

    def tile(i, col):
        return F[i, col // UW, :, col % UW : col % UW + 128]

    for m, out in enumerate((gate_o, up_o, down_o)):
        for i in range(4):
            for n in range(1 if i == 3 else 0, 9):
                out[:, OFFS[i] + 128 * n : OFFS[i] + 128 * (n + 1)] = tile(i, m * FFW + 128 * n)
    base = 3 * FFW
    dk_o[...] = tile(0, base) + tile(2, base)
    dv_o[...] = tile(1, base) + tile(3, base)
    for n in range(HEADS):
        at = slice(128 * n, 128 * (n + 1))
        col = base + 128 * (n + 1)
        dq_o[:, at] = tile(0, col) + tile(2, col)
        dout_o[:, at] = tile(1, col) + tile(3, col)


def back(*args):
    shape = jax.ShapeDtypeStruct
    whole = pl.BlockSpec(memory_space=VM)
    hbm = pl.BlockSpec(memory_space=pl.ANY)
    dma = pltpu.SemaphoreType.DMA
    regular = pltpu.SemaphoreType.REGULAR
    return pl.pallas_call(
        back_kernel,
        name="back",
        out_shape=(
            shape((24, FFL), F32), shape((24, FFL), F32), shape((24, FFL), F32),
            shape((24, QW), F32), shape((24, WIDTH), F32), shape((24, WIDTH), F32), shape((24, QW), F32),
            shape((TOK, D), BF), shape((TOK, D), BF), shape((8, D), F32),
        ),
        in_specs=[whole, whole] + [hbm] * 4 + [whole] * 17,
        out_specs=(whole,) * 10,
        scratch_shapes=[
            VM((4, NU, 24, UW), F32),
            VM((G_SLOTS, 4, 2, 4, 2, 24, UW), F32),
            VM((R_SLOTS, 3, 4, 4, 24, UW), F32),
            VM((R_SLOTS, 3, 4, 24, UW), F32),
            VM((2, 4 * TOK, UW), BF),
            VM((2, TOK, D), F32), VM((2, TOK, D), F32),
            VM((2, HALF // 2, D), F32), VM((2, HALF, D), F32),
            VM((TOK, D), F32), VM((TOK, D), F32), VM((HALF, D), F32), VM((D, 2 * TOK), BF),
            VM((TOK, QW), BF), VM((TOK, QW), F32), VM((TOK, QW), F32), VM((2 * TOK, QW), BF),
            VM((2, TOK, WIDTH), F32), VM((2, TOK, WIDTH), F32), VM((2 * TOK, WIDTH), BF),
            VM((TOK, D), F32), VM((HALF, D), F32), VM((HALF, D), F32), VM((TOK, D), F32),
            VM((8, D), F32), VM((11, 8, D), F32),
            dma((R_SLOTS, 6, 4)), dma((R_SLOTS, 6, 4)), dma((NU, 3)), dma((NU, 3)),
            regular((4,)), dma((19,)), dma((19,)), regular((3,)), dma((2,)), dma((2,)),
            dma((9,)), dma((9,)),
        ],
        compiler_params=pltpu.CompilerParams(
            collective_id=2, has_side_effects=True, vmem_limit_bytes=63 * 2**20
        ),
    )(*args)


def on_device(
    tokens, lengths, keep_mask, norm1_gain, w_query, b_query, w_key, b_key, w_value, b_value,
    w_out, norm2_gain, w_gate, w_up, w_down, cotangent,
):
    inv_freq = ROPE_BASE ** (-jnp.arange(0, WIDTH, 2).astype(F32) / WIDTH)
    inv_freq = jnp.concatenate([inv_freq, inv_freq])[None, :]
    g1 = norm1_gain.astype(F32)[None, :]
    g2 = norm2_gain.astype(F32)[None, :]

    def bias(b):
        return b.astype(F32).reshape(1, -1)

    q, k, v, mask, cos, sin, h1, n2, n2t, dy, dyt, la, o2 = front(
        tokens, cotangent, lengths, keep_mask[None, :], inv_freq, g1, w_query, bias(b_query),
        w_key, bias(b_key), w_value, bias(b_value), w_out, g2,
    )
    dgu, a, dn2_part, out_part = ffn(n2, dy, w_gate, w_up, w_down)
    gate, up, down, dq, dk, dv, dout, layer_out, d_input, small = back(
        n2t, dyt, dgu, a, dn2_part, out_part, la, o2, tokens, cotangent, h1, q, k, v, mask, cos, sin,
        g1, g2, w_query, w_key, w_value, w_out,
    )
    mine = lax.dynamic_slice(small, (0, lax.axis_index("dp") * 24), (8, 24))
    biases = small[2]
    return (
        layer_out,
        d_input,
        mine[1],
        dq,
        biases[:QW].reshape(HEADS, WIDTH),
        dk,
        biases[QW : QW + WIDTH][None, :],
        dv,
        biases[QW + WIDTH : QW + 2 * WIDTH][None, :],
        dout.T,
        mine[0],
        gate,
        up,
        down.T,
    )


def solution(mesh):
    placed = (
        P("dp", None), P("dp", None), P("dp"), P(), P(None, "tensor"), P("tensor", None),
        P(None, "tensor"), P("tensor", None), P(None, "tensor"), P("tensor", None),
        P("tensor", None), P(), P(None, "tensor"), P(None, "tensor"), P("tensor", None), P("dp", None),
    )
    return jax.shard_map(
        on_device,
        mesh=mesh,
        in_specs=placed,
        out_specs=(
            P("dp", None), P("dp", None), P("dp"), P("dp", "tensor"), P("tensor", None),
            P("dp", "tensor"), P("tensor", None), P("dp", "tensor"), P("tensor", None),
            P("tensor", "dp"), P("dp"), P("dp", "tensor"), P("dp", "tensor"), P("tensor", "dp"),
        ),
        check_vma=False,
    )
```

```python
import math

import jax
import jax.numpy as jnp
from jax import lax
from jax.experimental import pallas as pl
from jax.experimental.pallas import tpu as pltpu
from jax.sharding import PartitionSpec as P

EPS = 1e-06
ROPE_BASE = 10000.0
NEG_FILL = -1e30
MESH = pl.DeviceIdType.MESH
BF = jnp.bfloat16
F32 = jnp.float32
VM = pltpu.VMEM

D = 1536
TOK = 256
HALF = 128
HEADS = 6
WIDTH = 128
QW = HEADS * WIDTH
FFL = 4480
FFW = 1152
OFFS = (0, 1152, 2304, 3328)

UW = 256
NU = 17
GATE_UNITS = 9
G_SLOTS = 7
R_SLOTS = 3
N_TICK = NU + 4


def coords():
    dp = lax.axis_index("dp")
    t = lax.axis_index("tensor")
    return dp // 16, lax.rem(dp // 8, 2), lax.rem(dp // 2, 4), lax.rem(dp, 2), t


def device(y, xh, z, c, t):
    return (((y * 2 + xh) * 4 + z) * 2 + c, t)


def device_x(y, x, z, c):
    return device(y, x // 2, z, c, lax.rem(x, 2))


def remote(src, dst, send, recv, to):
    return pltpu.make_async_remote_copy(
        src_ref=src, dst_ref=dst, send_sem=send, recv_sem=recv, device_id=to, device_id_type=MESH
    )


def greet(devices):
    barrier = pltpu.get_barrier_semaphore()
    for to in devices:
        pl.semaphore_signal(barrier, inc=1, device_id=to, device_id_type=MESH)
    pl.semaphore_wait(barrier, len(devices))


def dot(left, right):
    return jnp.dot(left, right, preferred_element_type=F32)


def dot_nt(left, right):
    return lax.dot_general(left, right, (((1,), (1,)), ((), ())), preferred_element_type=F32)


def dot_tn(left, right):
    return lax.dot_general(left, right, (((0,), (0,)), ((), ())), preferred_element_type=F32)


def rope(v, cosine, sine):
    return v * cosine + pltpu.roll(v, WIDTH // 2, 1) * sine


def rope_back(w, cosine, sine):
    return w * cosine + pltpu.roll(w * sine, WIDTH // 2, 1)


def mean_last(v):
    return jnp.mean(v, axis=-1, keepdims=True)


def front_kernel(
    tokens, cot, lengths, keep, g1, wq, bq, wk, bk, wv, bv, wo, g2, wg_h, wu_h, wd_h,
    q_o, k_o, v_o, mask_o, cos_o, sin_o, h1_o, la_o, o2_o,
    n2t_h, dyt_h, dgu_h, a_h, dn2_h, out_h,
    n2f, dyf, n1f, n1r, of, orr, part, prec, wg, wu, wd, n2t_s, dyt_s, dgu_s, a_s, dn2_s, out_s,
    ss, rs, wsem, osem, tsem,
):
    y, xh, z, c, t = coords()
    x = 2 * xh + t
    x1, x2, x3 = lax.rem(x + 1, 4), lax.rem(x + 2, 4), lax.rem(x + 3, 4)
    right = device_x(y, x1, z, c)
    left = device_x(y, x3, z, c)
    core = device(y, xh, z, 1 - c, t)
    mate = device(y, xh, z, c, 1 - t)
    cross = device_x(y, 3 - x, z, c)
    greet((right, left, core))
    mine = pl.ds(pl.multiple_of(t * HALF, HALF), HALF)
    other = pl.ds(pl.multiple_of((1 - t) * HALF, HALF), HALF)

    def send(i, src, dst, to):
        copy = remote(src, dst, ss.at[i], rs.at[i], to)
        copy.start()
        return copy

    near = pl.ds(2 * xh, 2)
    far = pl.ds(2 * (1 - xh), 2)
    dyf[near, c] = cot[...].astype(F32).reshape(2, HALF, D)
    dy_cross = send(0, dyf.at[near, c], dyf.at[near, c], cross)
    dy_core = send(1, dyf.at[near, c], dyf.at[near, c], core)

    me = 2 * xh + c
    hidden = pl.ds(pl.multiple_of((me * 9 - me // 3) * 128, 128), FFW)
    loads = [
        pltpu.make_async_copy(wg_h.at[:, hidden], wg, wsem.at[0]),
        pltpu.make_async_copy(wu_h.at[:, hidden], wu, wsem.at[1]),
        pltpu.make_async_copy(wd_h.at[hidden, :], wd, wsem.at[2]),
    ]
    for copy in loads:
        copy.start()

    rows = lax.broadcasted_iota(jnp.int32, (TOK, TOK), 0)
    cols = lax.broadcasted_iota(jnp.int32, (TOK, TOK), 1)
    row_id = lax.broadcasted_iota(jnp.int32, (TOK, WIDTH), 0)
    place = row_id
    seg_r = jnp.zeros((TOK, TOK), jnp.int32)
    seg_c = jnp.zeros((TOK, TOK), jnp.int32)
    end = jnp.int32(0)
    for i in range(4):
        span = lengths[0, i]
        end = end + span
        seg_r = seg_r + (rows >= end).astype(jnp.int32)
        seg_c = seg_c + (cols >= end).astype(jnp.int32)
        place = place - jnp.where(row_id >= end, span, 0)
    allowed = (seg_r == seg_c) & (cols <= rows) & ((keep[...] == 1) | (cols == rows))
    mask_o[...] = allowed.astype(F32)
    lane = lax.broadcasted_iota(jnp.int32, (TOK, WIDTH), 1)
    first = lane < WIDTH // 2
    step = jnp.where(first, lane, lane - WIDTH // 2).astype(F32)
    angle = place.astype(F32) * jnp.exp(step * (-2.0 * math.log(ROPE_BASE) / WIDTH))
    cosine = jnp.cos(angle)
    sine = jnp.sin(angle) * jnp.where(first, -1.0, 1.0)
    cos_o[...] = cosine
    sin_o[...] = sine

    xf = tokens[...].astype(F32)
    r1 = lax.rsqrt(mean_last(xf * xf) + EPS)
    n1 = (xf * r1 * g1[...].astype(F32)).astype(BF)
    n1f[...] = n1.astype(F32)
    n1_core = send(2, n1f, n1r, core)
    kp = dot(n1, wk[...]) + bk[...].astype(F32)
    k_o[...] = rope(kp, cosine, sine).astype(BF)
    v_o[...] = (dot(n1, wv[...]) + bv[...].astype(F32)).astype(BF)
    bias = bq[...].astype(F32)
    for h in range(HEADS):
        at = slice(h * WIDTH, (h + 1) * WIDTH)
        qp = dot(n1, wq[:, at]) + bias[h : h + 1]
        q_o[:, at] = (rope(qp, cosine, sine) * WIDTH**-0.5).astype(BF)

    def head(h, _):
        at = pl.ds(pl.multiple_of(h * WIDTH, WIDTH), WIDTH)
        s = jnp.where(mask_o[...] > 0.5, dot_nt(q_o[:, at], k_o[...]), NEG_FILL)
        e = jnp.exp(s - jnp.max(s, axis=-1, keepdims=True))
        soft = (e / jnp.sum(e, axis=-1, keepdims=True)).astype(BF)
        o = dot(soft, v_o[...]).astype(BF)
        o2_o[:TOK, at] = o
        of[:, at] = o.astype(F32)
        return 0

    lax.fori_loop(0, HEADS, head, 0)
    part[0] = dot(o2_o[other, :], wo[...])
    half = send(3, part.at[0], prec, mate)
    o_core = send(4, of, orr, core)
    part[1] = dot(o2_o[mine, :], wo[...])
    la_o[:, :TOK] = n1.T
    n1_core.wait_recv()
    la_o[:, TOK:] = n1r[...].astype(BF).T
    o_core.wait_recv()
    o2_o[TOK:, :] = orr[...].astype(BF)

    half.wait_recv()
    h1 = tokens[mine, :].astype(F32) + part[1] + prec[...]
    h1_o[...] = h1
    r2 = lax.rsqrt(mean_last(h1 * h1) + EPS)
    n2f[x, c] = (h1 * r2 * g2[...].astype(F32)).astype(BF).astype(F32)

    def pass_on(i, xx, to, lo=0, n=HALF):
        at = n2f.at[xx, c, pl.ds(lo, n)]
        return send(i, at, at, to)

    to_right = pass_on(5, x, right)
    to_left = pass_on(6, x, left)
    to_core = pass_on(7, x, core)

    unit = lax.broadcasted_iota(jnp.int32, (1, FFW), 1)
    live = jnp.where((unit < 128) & (me == 3), 0.0, 1.0)

    def tokens_of(xx):
        return pl.ds(pl.multiple_of(xx * TOK, TOK), TOK)

    def results(n, xx):
        slot, at = n % 2, tokens_of(xx)
        return [
            pltpu.make_async_copy(src, dst, osem.at[slot, i])
            for i, (src, dst) in enumerate((
                (n2t_s.at[slot], n2t_h.at[:, at]),
                (dgu_s.at[slot], dgu_h.at[at]),
                (a_s.at[slot], a_h.at[at]),
                (dn2_s.at[slot], dn2_h.at[xx]),
                (out_s.at[slot], out_h.at[xx]),
            ))
        ]

    order = (x, x3, x1, x2)

    def feed(n):
        xx, slot = order[n], n % 2
        if n >= 2:
            for copy in results(n - 2, order[n - 2]):
                copy.wait()
        here = n2f[xx].reshape(TOK, D).astype(BF)
        g = dot(here, wg[...])
        u = dot(here, wu[...])
        n2t_s[slot] = here.T
        sg = live / (1.0 + jnp.exp(-g))
        silu = g * sg
        a = (silu * u).astype(BF)
        a_s[slot] = a
        out_s[slot] = dot(a, wd[...]).reshape(2, HALF, D)
        da = dot_nt(dyf[xx].reshape(TOK, D).astype(BF), wd[...])
        dg = (da * u * sg * (1.0 + g * (1.0 - sg))).astype(BF)
        du = (da * silu).astype(BF)
        dgu_s[slot, :, :FFW] = dg
        dgu_s[slot, :, FFW:] = du
        dn2_s[slot] = (dot_nt(dg, wg[...]) + dot_nt(du, wu[...])).reshape(2, HALF, D)
        for copy in results(n, xx):
            copy.start()

    def turned(n, xx):
        return pltpu.make_async_copy(dyt_s.at[n % 2], dyt_h.at[:, tokens_of(xx)], tsem.at[n % 2])

    around = (x, 2 * xh + 1 - t, x2, 3 - x)

    def turn(n):
        xx = around[n]
        if n >= 2:
            turned(n - 2, around[n - 2]).wait()
        dyt_s[n % 2] = dyf[xx].reshape(TOK, D).astype(BF).T
        turned(n, xx).start()

    dy_core.wait_recv()
    to_core.wait_recv()
    for copy in loads:
        copy.wait()
    feed(0)
    turn(0)
    turn(1)
    dy_cross.wait_recv()
    dy_far = send(8, dyf.at[far, c], dyf.at[far, c], core)

    to_right.wait_recv()
    pass_right = pass_on(9, x3, right, 0, HALF // 2)
    core_left = pass_on(10, x3, core)
    to_left.wait_recv()
    pass_left = pass_on(11, x1, left, HALF // 2, HALF // 2)
    core_right = pass_on(12, x1, core)
    dy_far.wait_recv()
    core_left.wait_recv()
    feed(1)
    pass_right.wait_recv()
    pass_left.wait_recv()
    core_across = pass_on(13, x2, core)
    core_right.wait_recv()
    feed(2)
    turn(2)
    turn(3)
    core_across.wait_recv()
    feed(3)
    for n in (2, 3):
        turned(n, around[n]).wait()
        for copy in results(n, order[n]):
            copy.wait()
    for copy in (
        dy_cross, dy_core, n1_core, half, o_core, to_right, to_left, to_core,
        dy_far, pass_right, core_left, pass_left, core_right, core_across,
    ):
        copy.wait_send()


def front(*args):
    shape = jax.ShapeDtypeStruct
    whole = pl.BlockSpec(memory_space=VM)
    scalars = pl.BlockSpec(memory_space=pltpu.SMEM)
    hbm = pl.BlockSpec(memory_space=pl.ANY)
    dma = pltpu.SemaphoreType.DMA
    return pl.pallas_call(
        front_kernel,
        name="front",
        out_shape=(
            shape((TOK, QW), BF), shape((TOK, WIDTH), BF), shape((TOK, WIDTH), BF),
            shape((TOK, TOK), F32), shape((TOK, WIDTH), F32), shape((TOK, WIDTH), F32),
            shape((HALF, D), F32), shape((D, 2 * TOK), BF), shape((2 * TOK, QW), BF),
            shape((D, 4 * TOK), BF), shape((D, 4 * TOK), BF),
            shape((4 * TOK, 2 * FFW), BF), shape((4 * TOK, FFW), BF),
            shape((4, 2, HALF, D), F32), shape((4, 2, HALF, D), F32),
        ),
        in_specs=[whole, whole, scalars] + [whole] * 10 + [hbm] * 3,
        out_specs=(whole,) * 9 + (hbm,) * 6,
        scratch_shapes=[
            VM((4, 2, HALF, D), F32), VM((4, 2, HALF, D), F32),
            VM((TOK, D), F32), VM((TOK, D), F32),
            VM((TOK, QW), F32), VM((TOK, QW), F32),
            VM((2, HALF, D), F32), VM((HALF, D), F32),
            VM((D, FFW), BF), VM((D, FFW), BF), VM((FFW, D), BF),
            VM((2, D, TOK), BF), VM((2, D, TOK), BF),
            VM((2, TOK, 2 * FFW), BF), VM((2, TOK, FFW), BF),
            VM((2, 2, HALF, D), F32), VM((2, 2, HALF, D), F32),
            dma((14,)), dma((14,)), dma((3,)), dma((2, 5)), dma((2,)),
        ],
        compiler_params=pltpu.CompilerParams(
            collective_id=1, has_side_effects=True, vmem_limit_bytes=63 * 2**20
        ),
    )(*args)


def back_kernel(
    n2t, dyt, dgu_h, a_h, dn2_h, out_h, la, o2, tokens, cot, h1, q, k, v, mask, cos, sin,
    g1, g2, wq, wk, wv, wo,
    gate_o, up_o, down_o, dq_o, dk_o, dv_o, dout_o, lout_o, din_o, small_o,
    F, G, R1, R2, R3, R4, RB, C, L, S1, S2, dhf, dhr, dh, lb, do, dqf, xqr, rq, dkvf, xkvr, rkv,
    dn1, dn1r, dir, lof, small, sb,
    ss, rs, fss, frs, credit, xss, xrs, free, lsem, bsem, sss, srs,
):
    y, xh, z, c, t = coords()
    x = 2 * xh + t
    me = 2 * xh + c
    by_y = tuple(device(lax.rem(y + i, 4), xh, z, c, t) for i in (1, 2, 3))
    by_z = tuple(device(y, xh, lax.rem(z + i, 4), c, t) for i in (1, 2, 3))
    ring = {"y": (by_y[0], by_y[2]), "z": (by_z[0], by_z[2])}
    right = device_x(y, lax.rem(x + 1, 4), z, c)
    left = device_x(y, lax.rem(x + 3, 4), z, c)
    core = device(y, xh, z, 1 - c, t)
    mate = device(y, xh, z, c, 1 - t)
    over = device(y, 1 - xh, z, c, t)
    over_core = device(y, 1 - xh, z, 1 - c, t)
    peers = (None, core, over, over_core)
    greet(by_y + by_z + (right, left, core, over, over_core))
    mine = pl.ds(pl.multiple_of(t * HALF, HALF), HALF)
    other = pl.ds(pl.multiple_of((1 - t) * HALF, HALF), HALF)

    R = (R1, R2, R3, R4)

    def axis(j, s):
        return ("y", y) if (j == 0) == (s <= 2) else ("z", z)

    def part(g, j, s, i, way):
        own = z if j else y
        if s == 1:
            return G.at[g, j, i, way]
        if s == 2:
            return G.at[g, j, i]
        return G.at[g, j, own, way, i] if s == 3 else G.at[g, j, own, :, i]

    def step_copy(u, s, j, way):
        name, p = axis(j, s)
        g, r = lax.rem(u, G_SLOTS), lax.rem(u, R_SLOTS)
        to = lax.rem(p + (2 if s % 2 else (3 if way else 1)), 4)
        return remote(
            part(g, j, s, to, way),
            R[s - 1].at[r, j, way],
            ss.at[r, s - 1, j, way],
            rs.at[r, s - 1, j, way],
            ring[name][way],
        )

    def total(u, px, pc):
        return G.at[lax.rem(u, G_SLOTS), px, jnp.where(px == 0, y, z), pc, jnp.where(px == 0, z, y)]

    def last_copy(u, n):
        px = 1 - xh if n & 2 else xh
        pc = 1 - c if n & 1 else c
        return remote(total(u, px, pc), F.at[me, u], fss.at[u, n - 1], frs.at[u, n - 1], peers[n])

    def advance(u, s):
        g, r = lax.rem(u, G_SLOTS), lax.rem(u, R_SLOTS)
        for j in range(2):
            _, p = axis(j, s)
            for way in range(2):
                step_copy(u, s, j, way).wait_recv()
                if s % 2:
                    at = part(g, j, s, lax.rem(p + (3 if way else 1), 4), way)
                    at[...] = at[...] + R[s - 1][r, j, way]
                    step_copy(u, s + 1, j, way).start()
            if s % 2 == 0:
                at = part(g, j, s, p, 0)
                at[...] = at[...] + R[s - 1][r, j, 0] + R[s - 1][r, j, 1]
                if s == 2:
                    for way in range(2):
                        step_copy(u, 3, j, way).start()
            for way in range(2):
                step_copy(u, s, j, way).wait_send()
        if s == 4:
            for n in range(1, 4):
                last_copy(u, n).start()
            F[me, u] = total(u, xh, c)[...]

    def load(u, act):
        r = lax.rem(u, 2)

        @pl.when(u < 9)
        def _():
            at = pl.ds(pl.multiple_of(u * UW, UW), UW)
            act(pltpu.make_async_copy(dgu_h.at[:, at], RB.at[r], bsem.at[r]))

        @pl.when((u >= 9) & (u < 13))
        def _():
            at = pl.ds(pl.multiple_of((u - 9) * UW, UW), UW)
            act(pltpu.make_async_copy(a_h.at[:, at], RB.at[r], bsem.at[r]))

        @pl.when(u == 13)
        def _():
            act(pltpu.make_async_copy(a_h.at[:, pl.ds(1024, 128)], RB.at[r, :, pl.ds(0, 128)], bsem.at[r]))

    def product(g, left_ref, rhs, w, o0):
        def body(i, _):
            lhs = left_ref[pl.ds(pl.multiple_of(i * 384, 384), 384), :]
            res = dot(lhs, rhs).reshape(2, 4, 2, 24, w)
            for zz in range(4):
                for cc in range(2):
                    G[g, 0, i, cc, zz, :, o0 : o0 + w] = res[0, zz, cc]
                    G[g, 1, zz, cc, i, :, o0 : o0 + w] = res[1, zz, cc]
            return 0

        lax.fori_loop(0, 4, body, 0)

    def grads(u):
        g = lax.rem(u, G_SLOTS)

        @pl.when(u >= G_SLOTS)
        def _():
            for n in range(1, 4):
                last_copy(u - G_SLOTS, n).wait_send()

        load(u, lambda copy: copy.wait())

        @pl.when(u < 9)
        def _():
            product(g, n2t, RB[lax.rem(u, 2)], UW, 0)

        @pl.when((u >= 9) & (u < 13))
        def _():
            product(g, dyt, RB[lax.rem(u, 2)], UW, 0)

        @pl.when(u == 13)
        def _():
            product(g, dyt, RB[1, :, 0:128], 128, 0)
            product(g, la, rkv[...], 128, 128)

        @pl.when(u >= 14)
        def _():
            product(g, lb, rq[:, pl.ds(pl.multiple_of((u - 14) * UW, UW), UW)], UW, 0)

        load(u + 2, lambda copy: copy.start())

    def xcopy(i, src, dst, to):
        return remote(src, dst, xss.at[i], xrs.at[i], to)

    def core_copy(base, src):
        return xcopy(base, src.at[:, 1 - c], C, core)

    def local_copy(src):
        return pltpu.make_async_copy(src.at[:, c], L, lsem.at[0])

    def lrow(xx, lo, n):
        return L.at[xx, pl.ds(lo, n)]

    x1, x2, x3 = lax.rem(x + 1, 4), lax.rem(x + 2, 4), lax.rem(x + 3, 4)

    def ring1(base):
        return [
            xcopy(base + 2, lrow(x2, 0, 64), S1.at[0], right),
            xcopy(base + 3, lrow(x2, 64, 64), S1.at[1], left),
        ]

    def ring2(base):
        return [
            xcopy(base + 4, lrow(x1, 0, HALF), S2.at[0], right),
            xcopy(base + 5, lrow(x3, 0, HALF), S2.at[1], left),
        ]

    def x_begin(base, src, first):
        if not first:
            pl.semaphore_wait(free.at[0], 1)
        core_copy(base, src).start()
        local_copy(src).start()

    def x_ring1(base, src, first):
        core_copy(base, src).wait()
        local_copy(src).wait()

        def add(i, _):
            L[i] = L[i] + C[i]
            return 0

        lax.fori_loop(0, 4, add, 0)
        if first:
            pl.semaphore_signal(free.at[0], inc=1, device_id=core, device_id_type=MESH)
        else:
            pl.semaphore_wait(free.at[1], 1)
            pl.semaphore_wait(free.at[2], 1)
        for copy in ring1(base):
            copy.start()

    def x_ring2(base):
        for copy in ring1(base):
            copy.wait()
        low, high = lrow(x1, 0, 64), lrow(x3, 64, 64)
        low[...] = low[...] + S1[0]
        high[...] = high[...] + S1[1]
        for copy in ring2(base):
            copy.start()

    def x_end(base, first):
        for copy in ring2(base):
            copy.wait()
        total = lrow(x, 0, HALF)[...] + S2[0] + S2[1]
        if first:
            pl.semaphore_signal(free.at[1], inc=1, device_id=right, device_id_type=MESH)
            pl.semaphore_signal(free.at[2], inc=1, device_id=left, device_id_type=MESH)
        return total

    dh_copy = xcopy(12, dhf.at[mine], dhf.at[mine], mate)
    dh_core = xcopy(13, dhf, dhr, core)
    q_core = xcopy(14, dqf, xqr, core)
    kv_core = xcopy(15, dkvf, xkvr, core)
    dn1_copy = xcopy(16, dn1.at[other], dn1r, mate)
    lo_copy = xcopy(17, lof.at[mine], lof.at[mine], mate)
    di_copy = xcopy(18, dn1.at[mine], dir, mate)

    def second_norm():
        dn2 = x_end(0, True)
        hh = h1[...]
        r2 = lax.rsqrt(mean_last(hh * hh) + EPS)
        normed = hh * r2
        e = dn2 * g2[...].astype(F32)
        grad = cot[mine, :].astype(F32) + r2 * (e - normed * mean_last(e * normed))
        dh[...] = grad
        dhf[mine, :] = grad.astype(BF).astype(F32)
        dh_copy.start()
        small[...] = jnp.zeros_like(small)
        small[0:1, :] = jnp.sum(dn2 * normed, axis=0, keepdims=True)

    def mix_grad():
        dh_copy.wait()
        dh_core.start()
        do[...] = dot_nt(dhf[...].astype(BF), wo[...]).astype(BF)
        dkvf[...] = jnp.zeros_like(dkvf)

    def heads(lo, hi):
        def body(h, _):
            at = pl.ds(pl.multiple_of(h * WIDTH, WIDTH), WIDTH)
            qh, doh = q[:, at], do[:, at]
            s = jnp.where(mask[...] > 0.5, dot_nt(qh, k[...]), NEG_FILL)
            e = jnp.exp(s - jnp.max(s, axis=-1, keepdims=True))
            soft = e / jnp.sum(e, axis=-1, keepdims=True)
            dp = dot_nt(doh, v[...])
            dz = (soft * (dp - jnp.sum(soft * dp, axis=-1, keepdims=True))).astype(BF)
            dq = dot(dz, k[...]) * WIDTH**-0.5
            dqf[:, at] = rope_back(dq, cos[...], sin[...]).astype(BF).astype(F32)
            dkvf[0] = dkvf[0] + dot_tn(dz, qh)
            dkvf[1] = dkvf[1] + dot_tn(soft.astype(BF), doh)
            return 0

        lax.fori_loop(lo, hi, body, 0)

    def head_end():
        dkvf[0] = rope_back(dkvf[0], cos[...], sin[...]).astype(BF).astype(F32)
        dkvf[1] = dkvf[1].astype(BF).astype(F32)
        q_core.start()
        kv_core.start()
        small[2:3, 0:QW] = jnp.sum(dqf[...], axis=0, keepdims=True)
        small[2:3, QW : QW + WIDTH] = jnp.sum(dkvf[0], axis=0, keepdims=True)
        small[2:3, QW + WIDTH : QW + 2 * WIDTH] = jnp.sum(dkvf[1], axis=0, keepdims=True)

    def input_grad():
        dn1[...] = (
            dot_nt(dqf[...].astype(BF), wq[...])
            + dot_nt(dkvf[0].astype(BF), wk[...])
            + dot_nt(dkvf[1].astype(BF), wv[...])
        )
        xf = tokens[...].astype(F32)
        normed = xf * lax.rsqrt(mean_last(xf * xf) + EPS)
        small[1:2, :] = jnp.sum(dn1[...] * normed, axis=0, keepdims=True)
        small_mate.start()
        dn1_copy.start()

    def exchange_end():
        q_core.wait()
        kv_core.wait()
        dh_core.wait()
        rkv[:TOK, :] = dkvf[c].astype(BF)
        rkv[TOK:, :] = xkvr[c].astype(BF)

        @pl.when(c == 0)
        def _():
            rq[:TOK, :] = dqf[...].astype(BF)
            rq[TOK:, :] = xqr[...].astype(BF)
            lb[...] = la[...]

        @pl.when(c == 1)
        def _():
            rq[...] = o2[...]
            lb[:, :TOK] = dhf[...].astype(BF).T
            lb[:, TOK:] = dhr[...].astype(BF).T

    def layer_end():
        lof[mine, :] = (h1[...] + x_end(6, False)).astype(BF).astype(F32)
        lo_copy.start()

    def input_end():
        dn1_copy.wait()
        total = dn1[mine, :] + dn1r[...]
        xf = tokens[mine, :].astype(F32)
        r1 = lax.rsqrt(mean_last(xf * xf) + EPS)
        normed = xf * r1
        e = total * g1[...].astype(F32)
        grad = dh[...] + r1 * (e - normed * mean_last(e * normed))
        dn1[mine, :] = grad.astype(BF).astype(F32)
        di_copy.start()

    def small_copy(i, slot, to):
        return remote(small, sb.at[slot], sss.at[i], srs.at[i], to)

    small_mate = small_copy(0, 0, mate)
    quad_y = [small_copy(1 + i, 1 + y, by_y[i]) for i in range(3)]
    quad_z = [small_copy(4 + i, 5 + z, by_z[i]) for i in range(3)]
    quad_x = [small_copy(6 + i, 9 + me, peers[i]) for i in range(1, 4)]

    def small_add():
        small_mate.wait()
        gains = lax.broadcasted_iota(jnp.int32, small.shape, 0) < 2
        small[...] = small[...] + jnp.where(gains, sb[0], 0.0)

    def small_quad(copies, base, p):
        for copy in copies:
            copy.wait()
        sb[base + p] = small[...]
        small[...] = ((sb[base] + sb[base + 1]) + sb[base + 2]) + sb[base + 3]

    def start(copies):
        for copy in copies:
            copy.start()

    extras = {
        0: [lambda: x_begin(0, dn2_h, True)],
        1: [lambda: x_ring1(0, dn2_h, True)],
        3: [lambda: x_ring2(0)],
        5: [second_norm, lambda: x_begin(6, out_h, False)],
        7: [mix_grad, lambda: x_ring1(6, out_h, False)],
        8: [lambda: heads(0, 3)],
        9: [lambda: heads(3, 6), head_end, lambda: x_ring2(6)],
        10: [exchange_end],
        11: [input_grad],
        12: [small_add, lambda: start(quad_y)],
        13: [layer_end],
        14: [input_end, lambda: small_quad(quad_y, 1, y), lambda: start(quad_z)],
        16: [lambda: small_quad(quad_z, 5, z), lambda: start(quad_x)],
    }

    load(jnp.int32(0), lambda copy: copy.start())
    load(jnp.int32(1), lambda copy: copy.start())
    grads(jnp.int32(0))

    def tick(n, _):
        @pl.when((n >= R_SLOTS) & (n <= NU + 2))
        def _():
            for i in range(4):
                pl.semaphore_wait(credit.at[i], 1)

        @pl.when(n < NU)
        def _():
            for j in range(2):
                for way in range(2):
                    step_copy(n, 1, j, way).start()

        for s in range(1, 5):
            u = n - s

            @pl.when((u >= 0) & (u < NU))
            def _():
                advance(u, s)

        @pl.when((n >= 1) & (n <= NU + 3 - R_SLOTS))
        def _():
            for i, to in enumerate((ring["y"][1], ring["y"][0], ring["z"][1], ring["z"][0])):
                pl.semaphore_signal(credit.at[i], inc=1, device_id=to, device_id_type=MESH)

        @pl.when(n + 1 < NU)
        def _():
            grads(n + 1)

        for when, steps in extras.items():

            @pl.when(n == when)
            def _():
                for step in steps:
                    step()

        return 0

    lax.fori_loop(0, N_TICK, tick, 0)

    lo_copy.wait()
    lout_o[...] = lof[...].astype(BF)
    di_copy.wait()
    din_o[mine, :] = dn1[mine, :].astype(BF)
    din_o[other, :] = dir[...].astype(BF)
    small_quad(quad_x, 9, me)
    small_o[...] = small[...]

    def finish(u, _):
        for n in range(1, 4):
            last_copy(u, n).wait_recv()

            @pl.when(u >= NU - G_SLOTS)
            def _():
                last_copy(u, n).wait_send()

        return 0

    lax.fori_loop(0, NU, finish, 0)

    def tile(i, col):
        return F[i, col // UW, :, col % UW : col % UW + 128]

    for m, out in enumerate((gate_o, up_o, down_o)):
        for i in range(4):
            for n in range(1 if i == 3 else 0, 9):
                out[:, OFFS[i] + 128 * n : OFFS[i] + 128 * (n + 1)] = tile(i, m * FFW + 128 * n)
    base = 3 * FFW
    dk_o[...] = tile(0, base) + tile(2, base)
    dv_o[...] = tile(1, base) + tile(3, base)
    for n in range(HEADS):
        at = slice(128 * n, 128 * (n + 1))
        col = base + 128 * (n + 1)
        dq_o[:, at] = tile(0, col) + tile(2, col)
        dout_o[:, at] = tile(1, col) + tile(3, col)


def back(*args):
    shape = jax.ShapeDtypeStruct
    whole = pl.BlockSpec(memory_space=VM)
    hbm = pl.BlockSpec(memory_space=pl.ANY)
    dma = pltpu.SemaphoreType.DMA
    regular = pltpu.SemaphoreType.REGULAR
    return pl.pallas_call(
        back_kernel,
        name="back",
        out_shape=(
            shape((24, FFL), F32), shape((24, FFL), F32), shape((24, FFL), F32),
            shape((24, QW), F32), shape((24, WIDTH), F32), shape((24, WIDTH), F32), shape((24, QW), F32),
            shape((TOK, D), BF), shape((TOK, D), BF), shape((8, D), F32),
        ),
        in_specs=[whole, whole] + [hbm] * 4 + [whole] * 17,
        out_specs=(whole,) * 10,
        scratch_shapes=[
            VM((4, NU, 24, UW), F32),
            VM((G_SLOTS, 2, 4, 2, 4, 24, UW), F32),
            VM((R_SLOTS, 2, 2, 4, 24, UW), F32), VM((R_SLOTS, 2, 2, 2, 4, 24, UW), F32),
            VM((R_SLOTS, 2, 2, 24, UW), F32), VM((R_SLOTS, 2, 2, 2, 24, UW), F32),
            VM((2, 4 * TOK, UW), BF),
            VM((4, HALF, D), F32), VM((4, HALF, D), F32),
            VM((2, HALF // 2, D), F32), VM((2, HALF, D), F32),
            VM((TOK, D), F32), VM((TOK, D), F32), VM((HALF, D), F32), VM((D, 2 * TOK), BF),
            VM((TOK, QW), BF), VM((TOK, QW), F32), VM((TOK, QW), F32), VM((2 * TOK, QW), BF),
            VM((2, TOK, WIDTH), F32), VM((2, TOK, WIDTH), F32), VM((2 * TOK, WIDTH), BF),
            VM((TOK, D), F32), VM((HALF, D), F32), VM((HALF, D), F32), VM((TOK, D), F32),
            VM((8, D), F32), VM((13, 8, D), F32),
            dma((R_SLOTS, 4, 2, 2)), dma((R_SLOTS, 4, 2, 2)), dma((NU, 3)), dma((NU, 3)),
            regular((4,)), dma((19,)), dma((19,)), regular((3,)), dma((1,)), dma((2,)),
            dma((10,)), dma((10,)),
        ],
        compiler_params=pltpu.CompilerParams(
            collective_id=2, has_side_effects=True, vmem_limit_bytes=63 * 2**20
        ),
    )(*args)


def on_device(
    tokens, lengths, keep_mask, norm1_gain, w_query, b_query, w_key, b_key, w_value, b_value,
    w_out, norm2_gain, w_gate, w_up, w_down, cotangent,
):
    g1 = norm1_gain[None, :]
    g2 = norm2_gain[None, :]
    q, k, v, mask, cos, sin, h1, la, o2, n2t, dyt, dgu, a, dn2_part, out_part = front(
        tokens, cotangent, lengths, keep_mask[None, :], g1, w_query, b_query, w_key, b_key,
        w_value, b_value, w_out, g2, w_gate, w_up, w_down,
    )
    gate, up, down, dq, dk, dv, dout, layer_out, d_input, small = back(
        n2t, dyt, dgu, a, dn2_part, out_part, la, o2, tokens, cotangent, h1, q, k, v, mask, cos, sin,
        g1, g2, w_query, w_key, w_value, w_out,
    )
    mine = lax.dynamic_slice(small, (0, lax.axis_index("dp") * 24), (8, 24))
    biases = small[2]
    return (
        layer_out,
        d_input,
        mine[1],
        dq,
        biases[:QW].reshape(HEADS, WIDTH),
        dk,
        biases[QW : QW + WIDTH][None, :],
        dv,
        biases[QW + WIDTH : QW + 2 * WIDTH][None, :],
        dout.T,
        mine[0],
        gate,
        up,
        down.T,
    )


def solution(mesh):
    placed = (
        P("dp", None), P("dp", None), P("dp"), P(), P(None, "tensor"), P("tensor", None),
        P(None, "tensor"), P("tensor", None), P(None, "tensor"), P("tensor", None),
        P("tensor", None), P(), P(None, "tensor"), P(None, "tensor"), P("tensor", None), P("dp", None),
    )
    return jax.shard_map(
        on_device,
        mesh=mesh,
        in_specs=placed,
        out_specs=(
            P("dp", None), P("dp", None), P("dp"), P("dp", "tensor"), P("tensor", None),
            P("dp", "tensor"), P("tensor", None), P("dp", "tensor"), P("tensor", None),
            P("tensor", "dp"), P("dp"), P("dp", "tensor"), P("dp", "tensor"), P("tensor", "dp"),
        ),
        check_vma=False,
    )
```

```python
import math

import jax
import jax.numpy as jnp
from jax import lax
from jax.experimental import pallas as pl
from jax.experimental.pallas import tpu as pltpu
from jax.sharding import PartitionSpec as P

EPS = 1e-06
ROPE_BASE = 10000.0
NEG_FILL = -1e30
MESH = pl.DeviceIdType.MESH
BF = jnp.bfloat16
F32 = jnp.float32
VM = pltpu.VMEM

D = 1536
TOK = 256
HALF = 128
SUB = 64
HEADS = 6
WIDTH = 128
QW = HEADS * WIDTH
FFL = 4480
FFW = 1152
OFFS = (0, 1152, 2304, 3328)

UW = 256
NU = 17
GATE_UNITS = 9
G_SLOTS = 7
R_SLOTS = 3
N_TICK = NU + 4


def coords():
    dp = lax.axis_index("dp")
    t = lax.axis_index("tensor")
    return dp // 16, lax.rem(dp // 8, 2), lax.rem(dp // 2, 4), lax.rem(dp, 2), t


def device(y, xh, z, c, t):
    return (((y * 2 + xh) * 4 + z) * 2 + c, t)


def device_x(y, x, z, c):
    return device(y, x // 2, z, c, lax.rem(x, 2))


def remote(src, dst, send, recv, to):
    return pltpu.make_async_remote_copy(
        src_ref=src, dst_ref=dst, send_sem=send, recv_sem=recv, device_id=to, device_id_type=MESH
    )


def greet(devices):
    barrier = pltpu.get_barrier_semaphore()
    for to in devices:
        pl.semaphore_signal(barrier, inc=1, device_id=to, device_id_type=MESH)
    pl.semaphore_wait(barrier, len(devices))


def dot(left, right):
    return jnp.dot(left, right, preferred_element_type=F32)


def dot_nt(left, right):
    return lax.dot_general(left, right, (((1,), (1,)), ((), ())), preferred_element_type=F32)


def dot_tn(left, right):
    return lax.dot_general(left, right, (((0,), (0,)), ((), ())), preferred_element_type=F32)


def rope(v, cosine, sine):
    return v * cosine + pltpu.roll(v, WIDTH // 2, 1) * sine


def rope_back(w, cosine, sine):
    return w * cosine + pltpu.roll(w * sine, WIDTH // 2, 1)


def mean_last(v):
    return jnp.mean(v, axis=-1, keepdims=True)


def front_kernel(
    lengths, keep, g1, bq, bk, bv, g2, tokens_h, cot_h, wq_h, wk_h, wv_h, wo_h, wg_h, wu_h, wd_h,
    q_h, k_h, v_h, mask_h, cos_h, sin_h, h1_h, la_h, o2_h, n2t_h, dyt_h, dgu_h, a_h, dn2_h, out_h,
    tokens, cot, wq, wk, wv, wo, wg, wu, wd, q_o, k_o, v_o, mask_o, cos_o, sin_o, h1_o, la_o, o2_o,
    n2f, dyf, n1f, n1r, of, orr, part, prec, n2t_s, dyt_s, dgu_s, a_s, dn2_s, out_s,
    ss, rs, isem, ksem, osem, psem, tsem,
):
    y, xh, z, c, t = coords()
    x = 2 * xh + t
    x1, x2, x3 = lax.rem(x + 1, 4), lax.rem(x + 2, 4), lax.rem(x + 3, 4)
    right = device_x(y, x1, z, c)
    left = device_x(y, x3, z, c)
    core = device(y, xh, z, 1 - c, t)
    mate = device(y, xh, z, c, 1 - t)
    cross = device_x(y, 3 - x, z, c)
    me = 2 * xh + c
    hidden = pl.ds(pl.multiple_of((me * 9 - me // 3) * 128, 128), FFW)
    fetches = [
        pltpu.make_async_copy(src, dst, isem.at[i])
        for i, (src, dst) in enumerate((
            (cot_h, cot), (tokens_h, tokens), (wk_h, wk), (wv_h, wv), (wq_h, wq), (wo_h, wo),
            (wg_h.at[:, hidden], wg), (wu_h.at[:, hidden], wu), (wd_h.at[hidden, :], wd),
        ))
    ]
    for copy in fetches[:6]:
        copy.start()
    greet((right, left, core))
    mine = pl.ds(pl.multiple_of(t * HALF, HALF), HALF)
    other = pl.ds(pl.multiple_of((1 - t) * HALF, HALF), HALF)
    sent = []

    def send(src, dst, to):
        i = len(sent)
        copy = remote(src, dst, ss.at[i], rs.at[i], to)
        copy.start()
        sent.append(copy)
        return copy

    kept = []

    def keep_copy(src, dst):
        copy = pltpu.make_async_copy(src, dst, ksem.at[len(kept)])
        copy.start()
        kept.append(copy)

    near = pl.ds(2 * xh, 2)
    fetches[0].wait()
    dyf[near, c] = cot[...].astype(F32).reshape(2, HALF, D)
    dy_own = send(dyf.at[x, c], dyf.at[x, c], cross)
    x_mate = 2 * xh + 1 - t
    dy_core = send(dyf.at[near, c], dyf.at[near, c], core)

    rows = lax.broadcasted_iota(jnp.int32, (TOK, TOK), 0)
    cols = lax.broadcasted_iota(jnp.int32, (TOK, TOK), 1)
    row_id = lax.broadcasted_iota(jnp.int32, (TOK, WIDTH), 0)
    place = row_id
    seg_r = jnp.zeros((TOK, TOK), jnp.int32)
    seg_c = jnp.zeros((TOK, TOK), jnp.int32)
    end = jnp.int32(0)
    for i in range(4):
        span = lengths[0, i]
        end = end + span
        seg_r = seg_r + (rows >= end).astype(jnp.int32)
        seg_c = seg_c + (cols >= end).astype(jnp.int32)
        place = place - jnp.where(row_id >= end, span, 0)
    allowed = (seg_r == seg_c) & (cols <= rows) & ((keep[...][None, :] == 1) | (cols == rows))
    mask_o[...] = allowed.astype(F32)
    lane = lax.broadcasted_iota(jnp.int32, (TOK, WIDTH), 1)
    first = lane < WIDTH // 2
    step = jnp.where(first, lane, lane - WIDTH // 2).astype(F32)
    angle = place.astype(F32) * jnp.exp(step * (-2.0 * math.log(ROPE_BASE) / WIDTH))
    cosine = jnp.cos(angle)
    sine = jnp.sin(angle) * jnp.where(first, -1.0, 1.0)
    cos_o[...] = cosine
    sin_o[...] = sine

    fetches[1].wait()
    xf = tokens[...].astype(F32)
    r1 = lax.rsqrt(mean_last(xf * xf) + EPS)
    n1 = (xf * r1 * g1[...].astype(F32)[None, :]).astype(BF)
    n1f[...] = n1.astype(F32)
    n1_core = send(n1f, n1r, core)
    for copy in fetches[2:6]:
        copy.wait()
    for copy in fetches[6:]:
        copy.start()
    kp = dot(n1, wk[...]) + bk[...].astype(F32)
    k_o[...] = rope(kp, cosine, sine).astype(BF)
    v_o[...] = (dot(n1, wv[...]) + bv[...].astype(F32)).astype(BF)
    bias = bq[...].astype(F32)
    for h in range(HEADS):
        at = slice(h * WIDTH, (h + 1) * WIDTH)
        qp = dot(n1, wq[:, at]) + bias[h : h + 1]
        q_o[:, at] = (rope(qp, cosine, sine) * WIDTH**-0.5).astype(BF)

    def head(h, _):
        at = pl.ds(pl.multiple_of(h * WIDTH, WIDTH), WIDTH)
        s = jnp.where(mask_o[...] > 0.5, dot_nt(q_o[:, at], k_o[...]), NEG_FILL)
        e = jnp.exp(s - jnp.max(s, axis=-1, keepdims=True))
        soft = (e / jnp.sum(e, axis=-1, keepdims=True)).astype(BF)
        o = dot(soft, v_o[...]).astype(BF)
        o2_o[:TOK, at] = o
        of[:, at] = o.astype(F32)
        return 0

    lax.fori_loop(0, HEADS, head, 0)

    def quarter(n):
        return pl.ds(n * SUB, SUB)

    part[0] = dot(o2_o[other, :], wo[...])
    halves = [send(part.at[0, quarter(n)], prec.at[quarter(n)], mate) for n in range(2)]
    o_core = send(of, orr, core)
    part[1] = dot(o2_o[mine, :], wo[...])

    order = (
        ((x, 0, HALF),),
        ((x3, 0, SUB), (x1, 0, SUB)),
        ((x3, SUB, SUB), (x1, SUB, SUB)),
        ((x2, 0, HALF),),
    )

    def pieces(n):
        out, at = [], 0
        for xx, lo, size in order[n]:
            for cc in range(2):
                out.append((at, size, xx, cc, lo))
                at += size
        return out

    def gather(ref, n):
        if len(order[n]) == 1:
            return ref[order[n][0][0]].reshape(TOK, D).astype(BF)
        return jnp.concatenate([ref[xx, cc, lo : lo + size] for _, size, xx, cc, lo in pieces(n)], axis=0).astype(BF)

    def turned(n):
        return pltpu.make_async_copy(dyt_s.at[n % 2], dyt_h.at[:, pl.ds(n * TOK, TOK)], tsem.at[n % 2])

    def turn(n):
        if n >= 2:
            turned(n - 2).wait()
        dyt_s[n % 2] = gather(dyf, n).T
        turned(n).start()

    for src, dst in ((q_o, q_h), (k_o, k_h), (v_o, v_h), (mask_o, mask_h), (cos_o, cos_h), (sin_o, sin_h)):
        keep_copy(src, dst)
    la_o[:, :TOK] = n1.T
    n1_core.wait_recv()
    la_o[:, TOK:] = n1r[...].astype(BF).T
    keep_copy(la_o, la_h)
    o_core.wait_recv()
    o2_o[TOK:, :] = orr[...].astype(BF)
    keep_copy(o2_o, o2_h)
    dy_core.wait_recv()
    turn(0)

    def pass_on(xx, to, lo, size):
        at = n2f.at[xx, c, pl.ds(lo, size)]
        return send(at, at, to)

    to_right, to_left, to_core = [], [], []
    for n in range(2):
        halves[n].wait_recv()
        at = quarter(n)
        own = tokens[pl.ds(pl.multiple_of(t * HALF + n * SUB, SUB), SUB), :].astype(F32)
        h1 = own + part[1, at] + prec[at]
        h1_o[at] = h1
        r2 = lax.rsqrt(mean_last(h1 * h1) + EPS)
        n2f[x, c, at] = (h1 * r2 * g2[...].astype(F32)[None, :]).astype(BF).astype(F32)
        to_right.append(pass_on(x, right, n * SUB, SUB))
        to_left.append(pass_on(x, left, n * SUB, SUB))
        to_core.append(pass_on(x, core, n * SUB, SUB))
    keep_copy(h1_o, h1_h)

    unit = lax.broadcasted_iota(jnp.int32, (1, FFW), 1)
    live = jnp.where((unit < 128) & (me == 3), 0.0, 1.0)

    def results(n):
        slot, at = n % 2, pl.ds(n * TOK, TOK)
        moves = [(n2t_s.at[slot], n2t_h.at[:, at]), (dgu_s.at[slot], dgu_h.at[at]), (a_s.at[slot], a_h.at[at])]
        copies = [pltpu.make_async_copy(src, dst, osem.at[slot, i]) for i, (src, dst) in enumerate(moves)]
        for b, (staged, dst) in enumerate(((dn2_s, dn2_h), (out_s, out_h))):
            for i, (row, size, xx, cc, lo) in enumerate(pieces(n)):
                copies.append(
                    pltpu.make_async_copy(
                        staged.at[slot, pl.ds(row, size)], dst.at[xx, cc, pl.ds(lo, size)], psem.at[slot, b, i]
                    )
                )
        return copies

    def feed(n):
        slot = n % 2
        here = gather(n2f, n)
        g = dot(here, wg[...])
        u = dot(here, wu[...])
        if n >= 2:
            for copy in results(n - 2):
                copy.wait()
        n2t_s[slot] = here.T
        sg = live / (1.0 + jnp.exp(-g))
        silu = g * sg
        a = (silu * u).astype(BF)
        a_s[slot] = a
        out_s[slot] = dot(a, wd[...])
        da = dot_nt(gather(dyf, n), wd[...])
        dg = (da * u * sg * (1.0 + g * (1.0 - sg))).astype(BF)
        du = (da * silu).astype(BF)
        dgu_s[slot, :, :FFW] = dg
        dgu_s[slot, :, FFW:] = du
        dn2_s[slot] = dot_nt(dg, wg[...]) + dot_nt(du, wu[...])
        for copy in results(n):
            copy.start()

    passed, core_side, core_across = [], [], []

    dy_mate = send(dyf.at[x_mate, c], dyf.at[x_mate, c], cross)

    def step_one(n):
        to_right[n].wait_recv()
        passed.append(pass_on(x3, right, n * SUB, SUB // 2))
        core_side.append(pass_on(x3, core, n * SUB, SUB))
        to_left[n].wait_recv()
        passed.append(pass_on(x1, left, n * SUB + SUB // 2, SUB // 2))
        core_side.append(pass_on(x1, core, n * SUB, SUB))

    def step_two(n):
        for copy in passed[2 * n : 2 * n + 2]:
            copy.wait_recv()
        core_across.append(pass_on(x2, core, n * SUB, SUB))

    for copy in to_core:
        copy.wait_recv()
    for copy in fetches[6:]:
        copy.wait()
    feed(0)
    step_one(0)
    dy_own.wait_recv()
    dy_side = send(dyf.at[3 - x, c], dyf.at[3 - x, c], core)
    dy_side.wait_recv()
    turn(1)
    for copy in core_side:
        copy.wait_recv()
    feed(1)
    step_one(1)
    turn(2)
    for copy in core_side[2:]:
        copy.wait_recv()
    feed(2)
    step_two(0)
    dy_mate.wait_recv()
    dy_across = send(dyf.at[x2, c], dyf.at[x2, c], core)
    step_two(1)
    dy_across.wait_recv()
    turn(3)
    for copy in core_across:
        copy.wait_recv()
    feed(3)
    for n in (2, 3):
        turned(n).wait()
        for copy in results(n):
            copy.wait()
    for copy in kept:
        copy.wait()
    for copy in sent:
        copy.wait_send()


def front(*args):
    shape = jax.ShapeDtypeStruct
    whole = pl.BlockSpec(memory_space=VM)
    scalars = pl.BlockSpec(memory_space=pltpu.SMEM)
    hbm = pl.BlockSpec(memory_space=pl.ANY)
    dma = pltpu.SemaphoreType.DMA
    return pl.pallas_call(
        front_kernel,
        name="front",
        out_shape=(
            shape((TOK, QW), BF), shape((TOK, WIDTH), BF), shape((TOK, WIDTH), BF),
            shape((TOK, TOK), F32), shape((TOK, WIDTH), F32), shape((TOK, WIDTH), F32),
            shape((HALF, D), F32), shape((D, 2 * TOK), BF), shape((2 * TOK, QW), BF),
            shape((D, 4 * TOK), BF), shape((D, 4 * TOK), BF),
            shape((4 * TOK, 2 * FFW), BF), shape((4 * TOK, FFW), BF),
            shape((4, 2, HALF, D), F32), shape((4, 2, HALF, D), F32),
        ),
        in_specs=[scalars] + [whole] * 6 + [hbm] * 9,
        out_specs=(hbm,) * 15,
        scratch_shapes=[
            VM((TOK, D), BF), VM((TOK, D), BF),
            VM((D, QW), BF), VM((D, WIDTH), BF), VM((D, WIDTH), BF), VM((QW, D), BF),
            VM((D, FFW), BF), VM((D, FFW), BF), VM((FFW, D), BF),
            VM((TOK, QW), BF), VM((TOK, WIDTH), BF), VM((TOK, WIDTH), BF),
            VM((TOK, TOK), F32), VM((TOK, WIDTH), F32), VM((TOK, WIDTH), F32),
            VM((HALF, D), F32), VM((D, 2 * TOK), BF), VM((2 * TOK, QW), BF),
            VM((4, 2, HALF, D), F32), VM((4, 2, HALF, D), F32),
            VM((TOK, D), F32), VM((TOK, D), F32),
            VM((TOK, QW), F32), VM((TOK, QW), F32),
            VM((2, HALF, D), F32), VM((HALF, D), F32),
            VM((2, D, TOK), BF), VM((2, D, TOK), BF),
            VM((2, TOK, 2 * FFW), BF), VM((2, TOK, FFW), BF),
            VM((2, TOK, D), F32), VM((2, TOK, D), F32),
            dma((32,)), dma((32,)), dma((9,)), dma((9,)), dma((2, 3)), dma((2, 2, 4)), dma((2,)),
        ],
        compiler_params=pltpu.CompilerParams(
            collective_id=1, has_side_effects=True, vmem_limit_bytes=63 * 2**20
        ),
    )(*args)


def back_kernel(
    dgu_h, a_h, dn2_h, out_h, g1, g2, n2t_h, dyt_h, la_h, o2_h, tokens_h, cot_h, h1_h, q_h, k_h, v_h,
    mask_h, cos_h, sin_h, wq_h, wk_h, wv_h, wo_h,
    F_o, lout_o, din_o, small_o,
    n2t, dyt, la, o2, tokens, cot, h1, q, k, v, mask, cos, sin, wq, wk, wv, wo,
    F, G, R1, R2, R3, R4, RB, C, L, S1, S2, dhf, dhr, dh, lb, do, dqf, xqr, rq, dkvf, xkvr, rkv,
    dn1, dn1r, dir, lof, small, sb,
    ss, rs, fss, frs, credit, xss, xrs, free, lsem, bsem, sss, srs, isem,
):
    fetches = [
        pltpu.make_async_copy(src, dst, isem.at[i])
        for i, (src, dst) in enumerate((
            (n2t_h, n2t), (dyt_h, dyt), (cot_h, cot), (h1_h, h1), (wo_h, wo), (q_h, q), (k_h, k), (v_h, v),
            (mask_h, mask), (cos_h, cos), (sin_h, sin), (tokens_h, tokens), (wq_h, wq), (wk_h, wk),
            (wv_h, wv), (la_h, la), (o2_h, o2),
        ))
    ]
    for copy in fetches[:1]:
        copy.start()
    y, xh, z, c, t = coords()
    x = 2 * xh + t
    me = 2 * xh + c
    by_y = tuple(device(lax.rem(y + i, 4), xh, z, c, t) for i in (1, 2, 3))
    by_z = tuple(device(y, xh, lax.rem(z + i, 4), c, t) for i in (1, 2, 3))
    ring = {"y": (by_y[0], by_y[2]), "z": (by_z[0], by_z[2])}
    right = device_x(y, lax.rem(x + 1, 4), z, c)
    left = device_x(y, lax.rem(x + 3, 4), z, c)
    core = device(y, xh, z, 1 - c, t)
    mate = device(y, xh, z, c, 1 - t)
    over = device(y, 1 - xh, z, c, t)
    over_core = device(y, 1 - xh, z, 1 - c, t)
    peers = (None, core, over, over_core)
    greet(by_y + by_z + (right, left, core, over, over_core))
    mine = pl.ds(pl.multiple_of(t * HALF, HALF), HALF)
    other = pl.ds(pl.multiple_of((1 - t) * HALF, HALF), HALF)

    R = (R1, R2, R3, R4)

    def axis(j, s):
        return ("y", y) if (j == 0) == (s <= 2) else ("z", z)

    def part(g, j, s, i, way):
        own = z if j else y
        if s == 1:
            return G.at[g, j, i, way]
        if s == 2:
            return G.at[g, j, i]
        return G.at[g, j, own, way, i] if s == 3 else G.at[g, j, own, :, i]

    def step_copy(u, s, j, way):
        name, p = axis(j, s)
        g, r = lax.rem(u, G_SLOTS), lax.rem(u, R_SLOTS)
        to = lax.rem(p + (2 if s % 2 else (3 if way else 1)), 4)
        return remote(
            part(g, j, s, to, way),
            R[s - 1].at[r, j, way],
            ss.at[r, s - 1, j, way],
            rs.at[r, s - 1, j, way],
            ring[name][way],
        )

    def total(u, px, pc):
        return G.at[lax.rem(u, G_SLOTS), px, jnp.where(px == 0, y, z), pc, jnp.where(px == 0, z, y)]

    def last_copy(u, n):
        px = 1 - xh if n & 2 else xh
        pc = 1 - c if n & 1 else c
        return remote(total(u, px, pc), F.at[me, u], fss.at[u, n - 1], frs.at[u, n - 1], peers[n])

    def advance(u, s):
        g, r = lax.rem(u, G_SLOTS), lax.rem(u, R_SLOTS)
        for j in range(2):
            _, p = axis(j, s)
            for way in range(2):
                step_copy(u, s, j, way).wait_recv()
                if s % 2:
                    at = part(g, j, s, lax.rem(p + (3 if way else 1), 4), way)
                    at[...] = at[...] + R[s - 1][r, j, way]
                    step_copy(u, s + 1, j, way).start()
            if s % 2 == 0:
                at = part(g, j, s, p, 0)
                at[...] = at[...] + R[s - 1][r, j, 0] + R[s - 1][r, j, 1]
                if s == 2:
                    for way in range(2):
                        step_copy(u, 3, j, way).start()
            for way in range(2):
                step_copy(u, s, j, way).wait_send()
        if s == 4:
            for n in range(1, 4):
                last_copy(u, n).start()
            F[me, u] = total(u, xh, c)[...]

    def load(u, act):
        r = lax.rem(u, 2)

        @pl.when(u < 9)
        def _():
            at = pl.ds(pl.multiple_of(u * UW, UW), UW)
            act(pltpu.make_async_copy(dgu_h.at[:, at], RB.at[r], bsem.at[r]))

        @pl.when((u >= 9) & (u < 13))
        def _():
            at = pl.ds(pl.multiple_of((u - 9) * UW, UW), UW)
            act(pltpu.make_async_copy(a_h.at[:, at], RB.at[r], bsem.at[r]))

        @pl.when(u == 13)
        def _():
            act(pltpu.make_async_copy(a_h.at[:, pl.ds(1024, 128)], RB.at[r, :, pl.ds(0, 128)], bsem.at[r]))

    def product(g, left_ref, rhs, w, o0):
        def body(i, _):
            lhs = left_ref[pl.ds(pl.multiple_of(i * 384, 384), 384), :]
            res = dot(lhs, rhs).reshape(2, 4, 2, 24, w)
            for zz in range(4):
                for cc in range(2):
                    G[g, 0, i, cc, zz, :, o0 : o0 + w] = res[0, zz, cc]
                    G[g, 1, zz, cc, i, :, o0 : o0 + w] = res[1, zz, cc]
            return 0

        lax.fori_loop(0, 4, body, 0)

    def grads(u):
        g = lax.rem(u, G_SLOTS)

        @pl.when(u >= G_SLOTS)
        def _():
            for n in range(1, 4):
                last_copy(u - G_SLOTS, n).wait_send()

        load(u, lambda copy: copy.wait())

        @pl.when(u < 9)
        def _():
            product(g, n2t, RB[lax.rem(u, 2)], UW, 0)

        @pl.when((u >= 9) & (u < 13))
        def _():
            product(g, dyt, RB[lax.rem(u, 2)], UW, 0)

        @pl.when(u == 13)
        def _():
            product(g, dyt, RB[1, :, 0:128], 128, 0)
            product(g, la, rkv[...], 128, 128)

        @pl.when(u >= 14)
        def _():
            product(g, lb, rq[:, pl.ds(pl.multiple_of((u - 14) * UW, UW), UW)], UW, 0)

        load(u + 2, lambda copy: copy.start())

    def xcopy(i, src, dst, to):
        return remote(src, dst, xss.at[i], xrs.at[i], to)

    def core_copy(base, src):
        return xcopy(base, src.at[:, 1 - c], C, core)

    def local_copy(src):
        return pltpu.make_async_copy(src.at[:, c], L, lsem.at[0])

    def lrow(xx, lo, n):
        return L.at[xx, pl.ds(lo, n)]

    x1, x2, x3 = lax.rem(x + 1, 4), lax.rem(x + 2, 4), lax.rem(x + 3, 4)

    def ring1(base):
        return [
            xcopy(base + 2, lrow(x2, 0, 64), S1.at[0], right),
            xcopy(base + 3, lrow(x2, 64, 64), S1.at[1], left),
        ]

    def ring2(base):
        return [
            xcopy(base + 4, lrow(x1, 0, HALF), S2.at[0], right),
            xcopy(base + 5, lrow(x3, 0, HALF), S2.at[1], left),
        ]

    def x_begin(base, src, first):
        if not first:
            pl.semaphore_wait(free.at[0], 1)
        core_copy(base, src).start()
        local_copy(src).start()

    def x_ring1(base, src, first):
        core_copy(base, src).wait()
        local_copy(src).wait()

        def add(i, _):
            L[i] = L[i] + C[i]
            return 0

        lax.fori_loop(0, 4, add, 0)
        if first:
            pl.semaphore_signal(free.at[0], inc=1, device_id=core, device_id_type=MESH)
        else:
            pl.semaphore_wait(free.at[1], 1)
            pl.semaphore_wait(free.at[2], 1)
        for copy in ring1(base):
            copy.start()

    def x_ring2(base):
        for copy in ring1(base):
            copy.wait()
        low, high = lrow(x1, 0, 64), lrow(x3, 64, 64)
        low[...] = low[...] + S1[0]
        high[...] = high[...] + S1[1]
        for copy in ring2(base):
            copy.start()

    def x_end(base, first):
        for copy in ring2(base):
            copy.wait()
        total = lrow(x, 0, HALF)[...] + S2[0] + S2[1]
        if first:
            pl.semaphore_signal(free.at[1], inc=1, device_id=right, device_id_type=MESH)
            pl.semaphore_signal(free.at[2], inc=1, device_id=left, device_id_type=MESH)
        return total

    dh_copy = xcopy(12, dhf.at[mine], dhf.at[mine], mate)
    dh_core = xcopy(13, dhf, dhr, core)
    q_core = xcopy(14, dqf, xqr, core)
    kv_core = xcopy(15, dkvf, xkvr, core)
    dn1_copy = xcopy(16, dn1.at[other], dn1r, mate)
    lo_copy = xcopy(17, lof.at[mine], lof.at[mine], mate)
    di_copy = xcopy(18, dn1.at[mine], dir, mate)

    def second_norm():
        dn2 = x_end(0, True)
        hh = h1[...]
        r2 = lax.rsqrt(mean_last(hh * hh) + EPS)
        normed = hh * r2
        e = dn2 * g2[...].astype(F32)[None, :]
        grad = cot[mine, :].astype(F32) + r2 * (e - normed * mean_last(e * normed))
        dh[...] = grad
        dhf[mine, :] = grad.astype(BF).astype(F32)
        dh_copy.start()
        small[...] = jnp.zeros_like(small)
        small[0:1, :] = jnp.sum(dn2 * normed, axis=0, keepdims=True)

    def mix_grad():
        dh_copy.wait()
        dh_core.start()
        do[...] = dot_nt(dhf[...].astype(BF), wo[...]).astype(BF)
        dkvf[...] = jnp.zeros_like(dkvf)

    def heads(lo, hi):
        def body(h, _):
            at = pl.ds(pl.multiple_of(h * WIDTH, WIDTH), WIDTH)
            qh, doh = q[:, at], do[:, at]
            s = jnp.where(mask[...] > 0.5, dot_nt(qh, k[...]), NEG_FILL)
            e = jnp.exp(s - jnp.max(s, axis=-1, keepdims=True))
            soft = e / jnp.sum(e, axis=-1, keepdims=True)
            dp = dot_nt(doh, v[...])
            dz = (soft * (dp - jnp.sum(soft * dp, axis=-1, keepdims=True))).astype(BF)
            dq = dot(dz, k[...]) * WIDTH**-0.5
            dqf[:, at] = rope_back(dq, cos[...], sin[...]).astype(BF).astype(F32)
            dkvf[0] = dkvf[0] + dot_tn(dz, qh)
            dkvf[1] = dkvf[1] + dot_tn(soft.astype(BF), doh)
            return 0

        lax.fori_loop(lo, hi, body, 0)

    def head_end():
        dkvf[0] = rope_back(dkvf[0], cos[...], sin[...]).astype(BF).astype(F32)
        dkvf[1] = dkvf[1].astype(BF).astype(F32)
        q_core.start()
        kv_core.start()
        small[2:3, 0:QW] = jnp.sum(dqf[...], axis=0, keepdims=True)
        small[2:3, QW : QW + WIDTH] = jnp.sum(dkvf[0], axis=0, keepdims=True)
        small[2:3, QW + WIDTH : QW + 2 * WIDTH] = jnp.sum(dkvf[1], axis=0, keepdims=True)

    def input_grad():
        dn1[...] = (
            dot_nt(dqf[...].astype(BF), wq[...])
            + dot_nt(dkvf[0].astype(BF), wk[...])
            + dot_nt(dkvf[1].astype(BF), wv[...])
        )
        xf = tokens[...].astype(F32)
        normed = xf * lax.rsqrt(mean_last(xf * xf) + EPS)
        small[1:2, :] = jnp.sum(dn1[...] * normed, axis=0, keepdims=True)
        small_mate.start()
        dn1_copy.start()

    def exchange_end():
        q_core.wait()
        kv_core.wait()
        dh_core.wait()
        rkv[:TOK, :] = dkvf[c].astype(BF)
        rkv[TOK:, :] = xkvr[c].astype(BF)

        @pl.when(c == 0)
        def _():
            rq[:TOK, :] = dqf[...].astype(BF)
            rq[TOK:, :] = xqr[...].astype(BF)
            lb[...] = la[...]

        @pl.when(c == 1)
        def _():
            rq[...] = o2[...]
            lb[:, :TOK] = dhf[...].astype(BF).T
            lb[:, TOK:] = dhr[...].astype(BF).T

    def layer_end():
        lof[mine, :] = (h1[...] + x_end(6, False)).astype(BF).astype(F32)
        lo_copy.start()

    def input_end():
        dn1_copy.wait()
        total = dn1[mine, :] + dn1r[...]
        xf = tokens[mine, :].astype(F32)
        r1 = lax.rsqrt(mean_last(xf * xf) + EPS)
        normed = xf * r1
        e = total * g1[...].astype(F32)[None, :]
        grad = dh[...] + r1 * (e - normed * mean_last(e * normed))
        dn1[mine, :] = grad.astype(BF).astype(F32)
        di_copy.start()

    def small_copy(i, slot, to):
        return remote(small, sb.at[slot], sss.at[i], srs.at[i], to)

    small_mate = small_copy(0, 0, mate)
    quad_y = [small_copy(1 + i, 1 + y, by_y[i]) for i in range(3)]
    quad_z = [small_copy(4 + i, 5 + z, by_z[i]) for i in range(3)]
    quad_x = [small_copy(6 + i, 9 + me, peers[i]) for i in range(1, 4)]

    def small_add():
        small_mate.wait()
        gains = lax.broadcasted_iota(jnp.int32, small.shape, 0) < 2
        small[...] = small[...] + jnp.where(gains, sb[0], 0.0)

    def small_quad(copies, base, p):
        for copy in copies:
            copy.wait()
        sb[base + p] = small[...]
        small[...] = ((sb[base] + sb[base + 1]) + sb[base + 2]) + sb[base + 3]

    def start(copies):
        for copy in copies:
            copy.start()

    def fetched():
        for copy in fetches[1:]:
            copy.wait()

    extras = {
        0: [lambda: x_begin(0, dn2_h, True)],
        1: [lambda: x_ring1(0, dn2_h, True), fetched],
        3: [lambda: x_ring2(0)],
        5: [second_norm, lambda: x_begin(6, out_h, False)],
        7: [mix_grad, lambda: x_ring1(6, out_h, False)],
        8: [lambda: heads(0, 3)],
        9: [lambda: heads(3, 6), head_end, lambda: x_ring2(6)],
        10: [exchange_end],
        11: [input_grad],
        12: [small_add, lambda: start(quad_y)],
        13: [layer_end],
        14: [input_end, lambda: small_quad(quad_y, 1, y), lambda: start(quad_z)],
        16: [lambda: small_quad(quad_z, 5, z), lambda: start(quad_x)],
    }

    load(jnp.int32(0), lambda copy: copy.start())
    load(jnp.int32(1), lambda copy: copy.start())
    start(fetches[1:])
    fetches[0].wait()
    grads(jnp.int32(0))

    def tick(n, _):
        @pl.when((n >= R_SLOTS) & (n <= NU + 2))
        def _():
            for i in range(4):
                pl.semaphore_wait(credit.at[i], 1)

        @pl.when(n < NU)
        def _():
            for j in range(2):
                for way in range(2):
                    step_copy(n, 1, j, way).start()

        for s in range(1, 5):
            u = n - s

            @pl.when((u >= 0) & (u < NU))
            def _():
                advance(u, s)

        @pl.when((n >= 1) & (n <= NU + 3 - R_SLOTS))
        def _():
            for i, to in enumerate((ring["y"][1], ring["y"][0], ring["z"][1], ring["z"][0])):
                pl.semaphore_signal(credit.at[i], inc=1, device_id=to, device_id_type=MESH)

        @pl.when(n + 1 < NU)
        def _():
            grads(n + 1)

        for when, steps in extras.items():

            @pl.when(n == when)
            def _():
                for step in steps:
                    step()

        return 0

    lax.fori_loop(0, N_TICK, tick, 0)

    lo_copy.wait()
    lout_o[...] = lof[...].astype(BF)
    di_copy.wait()
    din_o[mine, :] = dn1[mine, :].astype(BF)
    din_o[other, :] = dir[...].astype(BF)
    small_quad(quad_x, 9, me)
    small_o[...] = small[...]

    def finish(u, _):
        for n in range(1, 4):
            last_copy(u, n).wait_recv()

            @pl.when(u >= NU - G_SLOTS)
            def _():
                last_copy(u, n).wait_send()

        return 0

    lax.fori_loop(0, NU, finish, 0)
    F_o[...] = F[...]


def finish_kernel(
    F, lout, din, small, lout_o, din_o, n1_o, dq_o, bq_o, dk_o, bk_o, dv_o, bv_o, dout_o, n2_o, gate_o, up_o, down_o
):
    lout_o[...] = lout[...]
    din_o[...] = din[...]

    def tile(i, col):
        return F[i, col // UW, :, col % UW : col % UW + 128]

    for m, out in enumerate((gate_o, up_o, down_o)):
        for i in range(4):
            for n in range(1 if i == 3 else 0, 9):
                at = slice(OFFS[i] + 128 * n, OFFS[i] + 128 * (n + 1))
                out[:, at] = tile(i, m * FFW + 128 * n)
    base = 3 * FFW
    dk_o[...] = tile(0, base) + tile(2, base)
    dv_o[...] = tile(1, base) + tile(3, base)
    for n in range(HEADS):
        at = slice(128 * n, 128 * (n + 1))
        col = base + 128 * (n + 1)
        dq_o[:, at] = tile(0, col) + tile(2, col)
        dout_o[:, at] = tile(1, col) + tile(3, col)
        bq_o[n : n + 1, :] = small[2:3, at]
    bk_o[...] = small[2:3, QW : QW + WIDTH]
    bv_o[...] = small[2:3, QW + WIDTH : QW + 2 * WIDTH]
    lane = lax.broadcasted_iota(jnp.int32, (24, D), 1)
    row = lax.broadcasted_iota(jnp.int32, (24, D), 0)
    own = lane == row + lax.axis_index("dp") * 24
    n2_o[...] = jnp.sum(jnp.where(own, small[0:1, :], 0.0), axis=1)
    n1_o[...] = jnp.sum(jnp.where(own, small[1:2, :], 0.0), axis=1)


def finish(*args):
    shape = jax.ShapeDtypeStruct
    whole = pl.BlockSpec(memory_space=VM)
    return pl.pallas_call(
        finish_kernel,
        name="finish",
        out_shape=(
            shape((TOK, D), BF), shape((TOK, D), BF), shape((24,), F32), shape((24, QW), F32),
            shape((HEADS, WIDTH), F32), shape((24, WIDTH), F32), shape((1, WIDTH), F32),
            shape((24, WIDTH), F32), shape((1, WIDTH), F32), shape((24, QW), F32), shape((24,), F32),
            shape((24, FFL), F32), shape((24, FFL), F32), shape((24, FFL), F32),
        ),
        in_specs=[whole] * 4,
        out_specs=(whole,) * 14,
        compiler_params=pltpu.CompilerParams(vmem_limit_bytes=60 * 2**20),
    )(*args)


def back(*args):
    shape = jax.ShapeDtypeStruct
    whole = pl.BlockSpec(memory_space=VM)
    hbm = pl.BlockSpec(memory_space=pl.ANY)
    dma = pltpu.SemaphoreType.DMA
    regular = pltpu.SemaphoreType.REGULAR
    return pl.pallas_call(
        back_kernel,
        name="back",
        out_shape=(
            shape((4, NU, 24, UW), F32), shape((TOK, D), BF), shape((TOK, D), BF), shape((8, D), F32),
        ),
        in_specs=[hbm] * 4 + [whole] * 2 + [hbm] * 17,
        out_specs=(whole,) * 4,
        scratch_shapes=[
            VM((D, 4 * TOK), BF), VM((D, 4 * TOK), BF), VM((D, 2 * TOK), BF), VM((2 * TOK, QW), BF),
            VM((TOK, D), BF), VM((TOK, D), BF), VM((HALF, D), F32),
            VM((TOK, QW), BF), VM((TOK, WIDTH), BF), VM((TOK, WIDTH), BF),
            VM((TOK, TOK), F32), VM((TOK, WIDTH), F32), VM((TOK, WIDTH), F32),
            VM((D, QW), BF), VM((D, WIDTH), BF), VM((D, WIDTH), BF), VM((QW, D), BF),
            VM((4, NU, 24, UW), F32),
            VM((G_SLOTS, 2, 4, 2, 4, 24, UW), F32),
            VM((R_SLOTS, 2, 2, 4, 24, UW), F32), VM((R_SLOTS, 2, 2, 2, 4, 24, UW), F32),
            VM((R_SLOTS, 2, 2, 24, UW), F32), VM((R_SLOTS, 2, 2, 2, 24, UW), F32),
            VM((2, 4 * TOK, UW), BF),
            VM((4, HALF, D), F32), VM((4, HALF, D), F32),
            VM((2, HALF // 2, D), F32), VM((2, HALF, D), F32),
            VM((TOK, D), F32), VM((TOK, D), F32), VM((HALF, D), F32), VM((D, 2 * TOK), BF),
            VM((TOK, QW), BF), VM((TOK, QW), F32), VM((TOK, QW), F32), VM((2 * TOK, QW), BF),
            VM((2, TOK, WIDTH), F32), VM((2, TOK, WIDTH), F32), VM((2 * TOK, WIDTH), BF),
            VM((TOK, D), F32), VM((HALF, D), F32), VM((HALF, D), F32), VM((TOK, D), F32),
            VM((8, D), F32), VM((13, 8, D), F32),
            dma((R_SLOTS, 4, 2, 2)), dma((R_SLOTS, 4, 2, 2)), dma((NU, 3)), dma((NU, 3)),
            regular((4,)), dma((19,)), dma((19,)), regular((3,)), dma((1,)), dma((2,)),
            dma((10,)), dma((10,)), dma((17,)),
        ],
        compiler_params=pltpu.CompilerParams(
            collective_id=2, has_side_effects=True, vmem_limit_bytes=63 * 2**20
        ),
    )(*args)


def on_device(
    tokens, lengths, keep_mask, norm1_gain, w_query, b_query, w_key, b_key, w_value, b_value,
    w_out, norm2_gain, w_gate, w_up, w_down, cotangent,
):
    q, k, v, mask, cos, sin, h1, la, o2, n2t, dyt, dgu, a, dn2_part, out_part = front(
        lengths, keep_mask, norm1_gain, b_query, b_key, b_value, norm2_gain,
        tokens, cotangent, w_query, w_key, w_value, w_out, w_gate, w_up, w_down,
    )
    results = list(finish(*back(
        dgu, a, dn2_part, out_part, norm1_gain, norm2_gain, n2t, dyt, la, o2, tokens, cotangent, h1,
        q, k, v, mask, cos, sin, w_query, w_key, w_value, w_out,
    )))
    results[9], results[13] = results[9].T, results[13].T
    return tuple(results)


def solution(mesh):
    placed = (
        P("dp", None), P("dp", None), P("dp"), P(), P(None, "tensor"), P("tensor", None),
        P(None, "tensor"), P("tensor", None), P(None, "tensor"), P("tensor", None),
        P("tensor", None), P(), P(None, "tensor"), P(None, "tensor"), P("tensor", None), P("dp", None),
    )
    return jax.shard_map(
        on_device,
        mesh=mesh,
        in_specs=placed,
        out_specs=(
            P("dp", None), P("dp", None), P("dp"), P("dp", "tensor"), P("tensor", None),
            P("dp", "tensor"), P("tensor", None), P("dp", "tensor"), P("tensor", None),
            P("tensor", "dp"), P("dp"), P("dp", "tensor"), P("dp", "tensor"), P("tensor", "dp"),
        ),
        check_vma=False,
    )
```

```python
import math

import jax
import jax.numpy as jnp
from jax import lax
from jax.experimental import pallas as pl
from jax.experimental.pallas import tpu as pltpu
from jax.sharding import PartitionSpec as P

EPS = 1e-06
ROPE_BASE = 10000.0
NEG_FILL = -1e30
MESH = pl.DeviceIdType.MESH
BF = jnp.bfloat16
F32 = jnp.float32
VM = pltpu.VMEM

D = 1536
TOK = 256
HALF = 128
SUB = 64
HEADS = 6
WIDTH = 128
QW = HEADS * WIDTH
FFL = 4480
FFW = 1152
OFFS = (0, 1152, 2304, 3328)

UW = 256
NU = 17
GATE_UNITS = 9
G_SLOTS = 7
R_SLOTS = 3
N_TICK = NU + 4


def coords():
    dp = lax.axis_index("dp")
    t = lax.axis_index("tensor")
    return dp // 16, lax.rem(dp // 8, 2), lax.rem(dp // 2, 4), lax.rem(dp, 2), t


def device(y, xh, z, c, t):
    return (((y * 2 + xh) * 4 + z) * 2 + c, t)


def device_x(y, x, z, c):
    return device(y, x // 2, z, c, lax.rem(x, 2))


def remote(src, dst, send, recv, to):
    return pltpu.make_async_remote_copy(
        src_ref=src, dst_ref=dst, send_sem=send, recv_sem=recv, device_id=to, device_id_type=MESH
    )


def greet(devices):
    barrier = pltpu.get_barrier_semaphore()
    for to in devices:
        pl.semaphore_signal(barrier, inc=1, device_id=to, device_id_type=MESH)
    pl.semaphore_wait(barrier, len(devices))


def dot(left, right):
    return jnp.dot(left, right, preferred_element_type=F32)


def dot_nt(left, right):
    return lax.dot_general(left, right, (((1,), (1,)), ((), ())), preferred_element_type=F32)


def dot_tn(left, right):
    return lax.dot_general(left, right, (((0,), (0,)), ((), ())), preferred_element_type=F32)


def rope(v, cosine, sine):
    return v * cosine + pltpu.roll(v, WIDTH // 2, 1) * sine


def rope_back(w, cosine, sine):
    return w * cosine + pltpu.roll(w * sine, WIDTH // 2, 1)


def mean_last(v):
    return jnp.mean(v, axis=-1, keepdims=True)


def front_kernel(
    lengths, keep, g1, bq, bk, bv, g2, tokens_h, cot_h, wq_h, wk_h, wv_h, wo_h, wg_h, wu_h, wd_h,
    q_h, k_h, v_h, mask_h, cos_h, sin_h, h1_h, la_h, o2_h, n2t_h, dyt_h, dgu_h, a_h, dn2_h, out_h,
    tokens, cot, wq, wk, wv, wo, wgu, wd, q_o, k_o, v_o, mask_o, cos_o, sin_o, h1_o, la_o, o2_o,
    n2f, dyf, n1f, n1r, of, orr, part, prec, n2t_s, dyt_s, dgu_s, a_s, dn2_s, out_s,
    ss, rs, isem, ksem, osem, psem, tsem,
):
    y, xh, z, c, t = coords()
    x = 2 * xh + t
    x1, x2, x3 = lax.rem(x + 1, 4), lax.rem(x + 2, 4), lax.rem(x + 3, 4)
    right = device_x(y, x1, z, c)
    left = device_x(y, x3, z, c)
    core = device(y, xh, z, 1 - c, t)
    mate = device(y, xh, z, c, 1 - t)
    cross = device_x(y, 3 - x, z, c)
    me = 2 * xh + c
    hidden = pl.ds(pl.multiple_of((me * 9 - me // 3) * 128, 128), FFW)
    fetches = [
        pltpu.make_async_copy(src, dst, isem.at[i])
        for i, (src, dst) in enumerate((
            (cot_h, cot), (tokens_h, tokens), (wk_h, wk), (wv_h, wv), (wq_h, wq), (wo_h, wo),
            (wg_h.at[:, hidden], wgu.at[:, pl.ds(0, FFW)]), (wu_h.at[:, hidden], wgu.at[:, pl.ds(FFW, FFW)]),
            (wd_h.at[hidden, :], wd),
        ))
    ]
    for copy in fetches[:6]:
        copy.start()
    greet((right, left, core))
    mine = pl.ds(pl.multiple_of(t * HALF, HALF), HALF)
    other = pl.ds(pl.multiple_of((1 - t) * HALF, HALF), HALF)
    sent = []

    def send(src, dst, to):
        i = len(sent)
        copy = remote(src, dst, ss.at[i], rs.at[i], to)
        copy.start()
        sent.append(copy)
        return copy

    kept = []

    def keep_copy(src, dst):
        copy = pltpu.make_async_copy(src, dst, ksem.at[len(kept)])
        copy.start()
        kept.append(copy)

    near = pl.ds(2 * xh, 2)
    fetches[0].wait()
    dyf[near, c] = cot[...].astype(F32).reshape(2, HALF, D)
    dy_own = send(dyf.at[x, c], dyf.at[x, c], cross)
    x_mate = 2 * xh + 1 - t
    dy_core = send(dyf.at[near, c], dyf.at[near, c], core)

    rows = lax.broadcasted_iota(jnp.int32, (TOK, TOK), 0)
    cols = lax.broadcasted_iota(jnp.int32, (TOK, TOK), 1)
    row_id = lax.broadcasted_iota(jnp.int32, (TOK, WIDTH), 0)
    place = row_id
    seg_r = jnp.zeros((TOK, TOK), jnp.int32)
    seg_c = jnp.zeros((TOK, TOK), jnp.int32)
    end = jnp.int32(0)
    for i in range(4):
        span = lengths[0, i]
        end = end + span
        seg_r = seg_r + (rows >= end).astype(jnp.int32)
        seg_c = seg_c + (cols >= end).astype(jnp.int32)
        place = place - jnp.where(row_id >= end, span, 0)
    allowed = (seg_r == seg_c) & (cols <= rows) & ((keep[...][None, :] == 1) | (cols == rows))
    mask_o[...] = allowed.astype(F32)
    lane = lax.broadcasted_iota(jnp.int32, (TOK, WIDTH), 1)
    first = lane < WIDTH // 2
    step = jnp.where(first, lane, lane - WIDTH // 2).astype(F32)
    angle = place.astype(F32) * jnp.exp(step * (-2.0 * math.log(ROPE_BASE) / WIDTH))
    cosine = jnp.cos(angle)
    sine = jnp.sin(angle) * jnp.where(first, -1.0, 1.0)
    cos_o[...] = cosine
    sin_o[...] = sine

    fetches[1].wait()
    xf = tokens[...].astype(F32)
    r1 = lax.rsqrt(mean_last(xf * xf) + EPS)
    n1 = (xf * r1 * g1[...].astype(F32)[None, :]).astype(BF)
    n1f[...] = n1.astype(F32)
    n1_core = send(n1f, n1r, core)
    for copy in fetches[2:6]:
        copy.wait()
    for copy in fetches[6:]:
        copy.start()
    kp = dot(n1, wk[...]) + bk[...].astype(F32)
    k_o[...] = rope(kp, cosine, sine).astype(BF)
    v_o[...] = (dot(n1, wv[...]) + bv[...].astype(F32)).astype(BF)
    bias = bq[...].astype(F32)
    for h in range(HEADS):
        at = slice(h * WIDTH, (h + 1) * WIDTH)
        qp = dot(n1, wq[:, at]) + bias[h : h + 1]
        q_o[:, at] = (rope(qp, cosine, sine) * WIDTH**-0.5).astype(BF)

    def head(h, _):
        at = pl.ds(pl.multiple_of(h * WIDTH, WIDTH), WIDTH)
        s = jnp.where(mask_o[...] > 0.5, dot_nt(q_o[:, at], k_o[...]), NEG_FILL)
        e = jnp.exp(s - jnp.max(s, axis=-1, keepdims=True))
        soft = (e / jnp.sum(e, axis=-1, keepdims=True)).astype(BF)
        o = dot(soft, v_o[...]).astype(BF)
        o2_o[:TOK, at] = o
        of[:, at] = o.astype(F32)
        return 0

    lax.fori_loop(0, HEADS, head, 0)

    def quarter(n):
        return pl.ds(n * SUB, SUB)

    part[0] = dot(o2_o[other, :], wo[...])
    halves = [send(part.at[0, quarter(n)], prec.at[quarter(n)], mate) for n in range(2)]
    o_core = send(of, orr, core)
    part[1] = dot(o2_o[mine, :], wo[...])

    order = (
        ((x, 0, HALF),),
        ((x3, 0, SUB), (x1, 0, SUB)),
        ((x3, SUB, SUB), (x1, SUB, SUB)),
        ((x2, 0, HALF),),
    )

    def pieces(n):
        out, at = [], 0
        for xx, lo, size in order[n]:
            for cc in range(2):
                out.append((at, size, xx, cc, lo))
                at += size
        return out

    def gather(ref, n):
        if len(order[n]) == 1:
            return ref[order[n][0][0]].reshape(TOK, D).astype(BF)
        return jnp.concatenate([ref[xx, cc, lo : lo + size] for _, size, xx, cc, lo in pieces(n)], axis=0).astype(BF)

    def turned(n):
        return pltpu.make_async_copy(dyt_s.at[n % 2], dyt_h.at[:, pl.ds(n * TOK, TOK)], tsem.at[n % 2])

    def turn(n):
        if n >= 2:
            turned(n - 2).wait()
        dyt_s[n % 2] = gather(dyf, n).T
        turned(n).start()

    for src, dst in ((q_o, q_h), (k_o, k_h), (v_o, v_h), (mask_o, mask_h), (cos_o, cos_h), (sin_o, sin_h)):
        keep_copy(src, dst)
    la_o[:, :TOK] = n1.T
    n1_core.wait_recv()
    la_o[:, TOK:] = n1r[...].astype(BF).T
    keep_copy(la_o, la_h)
    o_core.wait_recv()
    o2_o[TOK:, :] = orr[...].astype(BF)
    keep_copy(o2_o, o2_h)
    dy_core.wait_recv()
    turn(0)

    def pass_on(xx, to, lo, size):
        at = n2f.at[xx, c, pl.ds(lo, size)]
        return send(at, at, to)

    to_right, to_left, to_core = [], [], []
    for n in range(2):
        halves[n].wait_recv()
        at = quarter(n)
        own = tokens[pl.ds(pl.multiple_of(t * HALF + n * SUB, SUB), SUB), :].astype(F32)
        h1 = own + part[1, at] + prec[at]
        h1_o[at] = h1
        r2 = lax.rsqrt(mean_last(h1 * h1) + EPS)
        n2f[x, c, at] = (h1 * r2 * g2[...].astype(F32)[None, :]).astype(BF).astype(F32)
        to_right.append(pass_on(x, right, n * SUB, SUB))
        to_left.append(pass_on(x, left, n * SUB, SUB))
        to_core.append(pass_on(x, core, n * SUB, SUB))
    keep_copy(h1_o, h1_h)

    unit = lax.broadcasted_iota(jnp.int32, (1, FFW), 1)
    live = jnp.where((unit < 128) & (me == 3), 0.0, 1.0)

    def results(n):
        slot, at = n % 2, pl.ds(n * TOK, TOK)
        moves = [(n2t_s.at[slot], n2t_h.at[:, at]), (dgu_s.at[slot], dgu_h.at[at]), (a_s.at[slot], a_h.at[at])]
        copies = [pltpu.make_async_copy(src, dst, osem.at[slot, i]) for i, (src, dst) in enumerate(moves)]
        for b, (staged, dst) in enumerate(((dn2_s, dn2_h), (out_s, out_h))):
            for i, (row, size, xx, cc, lo) in enumerate(pieces(n)):
                copies.append(
                    pltpu.make_async_copy(
                        staged.at[slot, pl.ds(row, size)], dst.at[xx, cc, pl.ds(lo, size)], psem.at[slot, b, i]
                    )
                )
        early = (0, 2) + tuple(range(3 + len(pieces(n)), len(copies)))
        return [copies[i] for i in early], [copy for i, copy in enumerate(copies) if i not in early]

    def feed(n):
        slot = n % 2
        here = gather(n2f, n)
        both = dot(here, wgu[...])
        g, u = both[:, :FFW], both[:, FFW:]
        if n >= 2:
            for copy in sum(results(n - 2), []):
                copy.wait()
        n2t_s[slot] = here.T
        sg = live / (1.0 + jnp.exp(-g))
        silu = g * sg
        a = (silu * u).astype(BF)
        a_s[slot] = a
        out_s[slot] = dot(a, wd[...])
        early, late = results(n)
        for copy in early:
            copy.start()
        da = dot_nt(gather(dyf, n), wd[...])
        dg = (da * u * sg * (1.0 + g * (1.0 - sg))).astype(BF)
        du = (da * silu).astype(BF)
        dgu_s[slot, :, :FFW] = dg
        dgu_s[slot, :, FFW:] = du
        dn2_s[slot] = dot_nt(dgu_s[slot], wgu[...])
        for copy in late:
            copy.start()

    passed, core_side, core_across = [], [], []

    dy_mate = send(dyf.at[x_mate, c, pl.ds(0, 96)], dyf.at[x_mate, c, pl.ds(0, 96)], cross)
    dy_own.wait_recv()
    dy_pass = send(dyf.at[3 - x, c, pl.ds(96, 32)], dyf.at[3 - x, c, pl.ds(96, 32)], mate)

    def step_one(n):
        to_right[n].wait_recv()
        passed.append(pass_on(x3, right, n * SUB, SUB // 2))
        core_side.append(pass_on(x3, core, n * SUB, SUB))
        to_left[n].wait_recv()
        passed.append(pass_on(x1, left, n * SUB + SUB // 2, SUB // 2))
        core_side.append(pass_on(x1, core, n * SUB, SUB))

    def step_two(n):
        for copy in passed[2 * n : 2 * n + 2]:
            copy.wait_recv()
        core_across.append(pass_on(x2, core, n * SUB, SUB))

    for copy in to_core:
        copy.wait_recv()
    for copy in fetches[6:]:
        copy.wait()
    feed(0)
    step_one(0)
    dy_side = send(dyf.at[3 - x, c], dyf.at[3 - x, c], core)
    dy_side.wait_recv()
    turn(1)
    for copy in core_side:
        copy.wait_recv()
    feed(1)
    step_one(1)
    turn(2)
    for copy in core_side[2:]:
        copy.wait_recv()
    feed(2)
    step_two(0)
    dy_mate.wait_recv()
    dy_pass.wait_recv()
    dy_across = send(dyf.at[x2, c], dyf.at[x2, c], core)
    step_two(1)
    dy_across.wait_recv()
    turn(3)
    for copy in core_across:
        copy.wait_recv()
    feed(3)
    for n in (2, 3):
        turned(n).wait()
        for copy in sum(results(n), []):
            copy.wait()
    for copy in kept:
        copy.wait()
    for copy in sent:
        copy.wait_send()


def front(*args):
    shape = jax.ShapeDtypeStruct
    whole = pl.BlockSpec(memory_space=VM)
    scalars = pl.BlockSpec(memory_space=pltpu.SMEM)
    hbm = pl.BlockSpec(memory_space=pl.ANY)
    dma = pltpu.SemaphoreType.DMA
    return pl.pallas_call(
        front_kernel,
        name="front",
        out_shape=(
            shape((TOK, QW), BF), shape((TOK, WIDTH), BF), shape((TOK, WIDTH), BF),
            shape((TOK, TOK), F32), shape((TOK, WIDTH), F32), shape((TOK, WIDTH), F32),
            shape((HALF, D), F32), shape((D, 2 * TOK), BF), shape((2 * TOK, QW), BF),
            shape((D, 4 * TOK), BF), shape((D, 4 * TOK), BF),
            shape((4 * TOK, 2 * FFW), BF), shape((4 * TOK, FFW), BF),
            shape((4, 2, HALF, D), F32), shape((4, 2, HALF, D), F32),
        ),
        in_specs=[scalars] + [whole] * 6 + [hbm] * 9,
        out_specs=(hbm,) * 15,
        scratch_shapes=[
            VM((TOK, D), BF), VM((TOK, D), BF),
            VM((D, QW), BF), VM((D, WIDTH), BF), VM((D, WIDTH), BF), VM((QW, D), BF),
            VM((D, 2 * FFW), BF), VM((FFW, D), BF),
            VM((TOK, QW), BF), VM((TOK, WIDTH), BF), VM((TOK, WIDTH), BF),
            VM((TOK, TOK), F32), VM((TOK, WIDTH), F32), VM((TOK, WIDTH), F32),
            VM((HALF, D), F32), VM((D, 2 * TOK), BF), VM((2 * TOK, QW), BF),
            VM((4, 2, HALF, D), F32), VM((4, 2, HALF, D), F32),
            VM((TOK, D), F32), VM((TOK, D), F32),
            VM((TOK, QW), F32), VM((TOK, QW), F32),
            VM((2, HALF, D), F32), VM((HALF, D), F32),
            VM((2, D, TOK), BF), VM((2, D, TOK), BF),
            VM((2, TOK, 2 * FFW), BF), VM((2, TOK, FFW), BF),
            VM((2, TOK, D), F32), VM((2, TOK, D), F32),
            dma((32,)), dma((32,)), dma((9,)), dma((9,)), dma((2, 3)), dma((2, 2, 4)), dma((2,)),
        ],
        compiler_params=pltpu.CompilerParams(
            collective_id=1, has_side_effects=True, vmem_limit_bytes=63 * 2**20
        ),
    )(*args)


def back_kernel(
    dgu_h, a_h, dn2_h, out_h, g1, g2, n2t_h, dyt_h, la_h, o2_h, tokens_h, cot_h, h1_h, q_h, k_h, v_h,
    mask_h, cos_h, sin_h, wq_h, wk_h, wv_h, wo_h,
    F_o, lout_o, din_o, small_o,
    n2t, dyt, la, o2, tokens, cot, h1, q, k, v, mask, cos, sin, wq, wk, wv, wo,
    F, G, R1, R2, R3, R4, RB, C, L, S1, S2, dhf, dhr, dh, lb, do, dqf, xqr, rq, dkvf, xkvr, rkv,
    dn1, dn1r, dir, lof, small, sb,
    ss, rs, fss, frs, credit, xss, xrs, free, lsem, bsem, sss, srs, isem,
):
    fetches = [
        pltpu.make_async_copy(src, dst, isem.at[i])
        for i, (src, dst) in enumerate((
            (n2t_h, n2t), (dyt_h, dyt), (cot_h, cot), (h1_h, h1), (wo_h, wo), (q_h, q), (k_h, k), (v_h, v),
            (mask_h, mask), (cos_h, cos), (sin_h, sin), (tokens_h, tokens), (wq_h, wq), (wk_h, wk),
            (wv_h, wv), (la_h, la), (o2_h, o2),
        ))
    ]
    for copy in fetches[:1]:
        copy.start()
    y, xh, z, c, t = coords()
    x = 2 * xh + t
    me = 2 * xh + c
    by_y = tuple(device(lax.rem(y + i, 4), xh, z, c, t) for i in (1, 2, 3))
    by_z = tuple(device(y, xh, lax.rem(z + i, 4), c, t) for i in (1, 2, 3))
    ring = {"y": (by_y[0], by_y[2]), "z": (by_z[0], by_z[2])}
    right = device_x(y, lax.rem(x + 1, 4), z, c)
    left = device_x(y, lax.rem(x + 3, 4), z, c)
    core = device(y, xh, z, 1 - c, t)
    mate = device(y, xh, z, c, 1 - t)
    over = device(y, 1 - xh, z, c, t)
    over_core = device(y, 1 - xh, z, 1 - c, t)
    peers = (None, core, over, over_core)
    greet(by_y + by_z + (right, left, core, over, over_core))
    mine = pl.ds(pl.multiple_of(t * HALF, HALF), HALF)
    other = pl.ds(pl.multiple_of((1 - t) * HALF, HALF), HALF)

    R = (R1, R2, R3, R4)

    def axis(j, s):
        return ("y", y) if (j == 0) == (s <= 2) else ("z", z)

    def part(g, j, s, i, way):
        own = z if j else y
        if s == 1:
            return G.at[g, j, i, way]
        if s == 2:
            return G.at[g, j, i]
        return G.at[g, j, own, way, i] if s == 3 else G.at[g, j, own, :, i]

    def step_copy(u, s, j, way):
        name, p = axis(j, s)
        g, r = lax.rem(u, G_SLOTS), lax.rem(u, R_SLOTS)
        to = lax.rem(p + (2 if s % 2 else (3 if way else 1)), 4)
        return remote(
            part(g, j, s, to, way),
            R[s - 1].at[r, j, way],
            ss.at[r, s - 1, j, way],
            rs.at[r, s - 1, j, way],
            ring[name][way],
        )

    def total(u, px, pc):
        return G.at[lax.rem(u, G_SLOTS), px, jnp.where(px == 0, y, z), pc, jnp.where(px == 0, z, y)]

    def last_copy(u, n):
        px = 1 - xh if n & 2 else xh
        pc = 1 - c if n & 1 else c
        return remote(total(u, px, pc), F.at[me, u], fss.at[u, n - 1], frs.at[u, n - 1], peers[n])

    def advance(u, s):
        g, r = lax.rem(u, G_SLOTS), lax.rem(u, R_SLOTS)
        for j in range(2):
            _, p = axis(j, s)
            for way in range(2):
                step_copy(u, s, j, way).wait_recv()
                if s % 2:
                    at = part(g, j, s, lax.rem(p + (3 if way else 1), 4), way)
                    at[...] = at[...] + R[s - 1][r, j, way]
                    step_copy(u, s + 1, j, way).start()
            if s % 2 == 0:
                at = part(g, j, s, p, 0)
                at[...] = at[...] + R[s - 1][r, j, 0] + R[s - 1][r, j, 1]
                if s == 2:
                    for way in range(2):
                        step_copy(u, 3, j, way).start()
            for way in range(2):
                step_copy(u, s, j, way).wait_send()
        if s == 4:
            for n in range(1, 4):
                last_copy(u, n).start()
            F[me, u] = total(u, xh, c)[...]

    def load(u, act):
        r = lax.rem(u, 2)

        @pl.when(u < 9)
        def _():
            at = pl.ds(pl.multiple_of(u * UW, UW), UW)
            act(pltpu.make_async_copy(dgu_h.at[:, at], RB.at[r], bsem.at[r]))

        @pl.when((u >= 9) & (u < 13))
        def _():
            at = pl.ds(pl.multiple_of((u - 9) * UW, UW), UW)
            act(pltpu.make_async_copy(a_h.at[:, at], RB.at[r], bsem.at[r]))

        @pl.when(u == 13)
        def _():
            act(pltpu.make_async_copy(a_h.at[:, pl.ds(1024, 128)], RB.at[r, :, pl.ds(0, 128)], bsem.at[r]))

    def product(g, left_ref, rhs, w, o0):
        def body(i, _):
            lhs = left_ref[pl.ds(pl.multiple_of(i * 384, 384), 384), :]
            res = dot(lhs, rhs).reshape(2, 4, 2, 24, w)
            for zz in range(4):
                for cc in range(2):
                    G[g, 0, i, cc, zz, :, o0 : o0 + w] = res[0, zz, cc]
                    G[g, 1, zz, cc, i, :, o0 : o0 + w] = res[1, zz, cc]
            return 0

        lax.fori_loop(0, 4, body, 0)

    def grads(u):
        g = lax.rem(u, G_SLOTS)

        @pl.when(u >= G_SLOTS)
        def _():
            for n in range(1, 4):
                last_copy(u - G_SLOTS, n).wait_send()

        load(u, lambda copy: copy.wait())

        @pl.when(u < 9)
        def _():
            product(g, n2t, RB[lax.rem(u, 2)], UW, 0)

        @pl.when((u >= 9) & (u < 13))
        def _():
            product(g, dyt, RB[lax.rem(u, 2)], UW, 0)

        @pl.when(u == 13)
        def _():
            product(g, dyt, RB[1, :, 0:128], 128, 0)
            product(g, la, rkv[...], 128, 128)

        @pl.when(u >= 14)
        def _():
            product(g, lb, rq[:, pl.ds(pl.multiple_of((u - 14) * UW, UW), UW)], UW, 0)

        load(u + 2, lambda copy: copy.start())

    def xcopy(i, src, dst, to):
        return remote(src, dst, xss.at[i], xrs.at[i], to)

    def core_copy(base, src):
        return xcopy(base, src.at[:, 1 - c], C, core)

    def local_copy(src):
        return pltpu.make_async_copy(src.at[:, c], L, lsem.at[0])

    def lrow(xx, lo, n):
        return L.at[xx, pl.ds(lo, n)]

    x1, x2, x3 = lax.rem(x + 1, 4), lax.rem(x + 2, 4), lax.rem(x + 3, 4)

    def ring1(base):
        return [
            xcopy(base + 2, lrow(x2, 0, 64), S1.at[0], right),
            xcopy(base + 3, lrow(x2, 64, 64), S1.at[1], left),
        ]

    def ring2(base):
        return [
            xcopy(base + 4, lrow(x1, 0, HALF), S2.at[0], right),
            xcopy(base + 5, lrow(x3, 0, HALF), S2.at[1], left),
        ]

    def x_begin(base, src, first):
        if not first:
            pl.semaphore_wait(free.at[0], 1)
        core_copy(base, src).start()
        local_copy(src).start()

    def x_ring1(base, src, first):
        core_copy(base, src).wait()
        local_copy(src).wait()

        def add(i, _):
            L[i] = L[i] + C[i]
            return 0

        lax.fori_loop(0, 4, add, 0)
        if first:
            pl.semaphore_signal(free.at[0], inc=1, device_id=core, device_id_type=MESH)
        else:
            pl.semaphore_wait(free.at[1], 1)
            pl.semaphore_wait(free.at[2], 1)
        for copy in ring1(base):
            copy.start()

    def x_ring2(base):
        for copy in ring1(base):
            copy.wait()
        low, high = lrow(x1, 0, 64), lrow(x3, 64, 64)
        low[...] = low[...] + S1[0]
        high[...] = high[...] + S1[1]
        for copy in ring2(base):
            copy.start()

    def x_end(base, first):
        for copy in ring2(base):
            copy.wait()
        total = lrow(x, 0, HALF)[...] + S2[0] + S2[1]
        if first:
            pl.semaphore_signal(free.at[1], inc=1, device_id=right, device_id_type=MESH)
            pl.semaphore_signal(free.at[2], inc=1, device_id=left, device_id_type=MESH)
        return total

    dh_copy = xcopy(12, dhf.at[mine], dhf.at[mine], mate)
    dh_core = xcopy(13, dhf, dhr, core)
    q_core = xcopy(14, dqf, xqr, core)
    kv_core = xcopy(15, dkvf, xkvr, core)
    dn1_copy = xcopy(16, dn1.at[other], dn1r, mate)
    lo_copy = xcopy(17, lof.at[mine], lof.at[mine], mate)
    di_copy = xcopy(18, dn1.at[mine], dir, mate)

    def second_norm():
        dn2 = x_end(0, True)
        hh = h1[...]
        r2 = lax.rsqrt(mean_last(hh * hh) + EPS)
        normed = hh * r2
        e = dn2 * g2[...].astype(F32)[None, :]
        grad = cot[mine, :].astype(F32) + r2 * (e - normed * mean_last(e * normed))
        dh[...] = grad
        dhf[mine, :] = grad.astype(BF).astype(F32)
        dh_copy.start()
        small[...] = jnp.zeros_like(small)
        small[0:1, :] = jnp.sum(dn2 * normed, axis=0, keepdims=True)

    def mix_grad():
        dh_copy.wait()
        dh_core.start()
        do[...] = dot_nt(dhf[...].astype(BF), wo[...]).astype(BF)
        dkvf[...] = jnp.zeros_like(dkvf)

    def heads(lo, hi):
        def body(h, _):
            at = pl.ds(pl.multiple_of(h * WIDTH, WIDTH), WIDTH)
            qh, doh = q[:, at], do[:, at]
            s = jnp.where(mask[...] > 0.5, dot_nt(qh, k[...]), NEG_FILL)
            e = jnp.exp(s - jnp.max(s, axis=-1, keepdims=True))
            soft = e / jnp.sum(e, axis=-1, keepdims=True)
            dp = dot_nt(doh, v[...])
            dz = (soft * (dp - jnp.sum(soft * dp, axis=-1, keepdims=True))).astype(BF)
            dq = dot(dz, k[...]) * WIDTH**-0.5
            dqf[:, at] = rope_back(dq, cos[...], sin[...]).astype(BF).astype(F32)
            dkvf[0] = dkvf[0] + dot_tn(dz, qh)
            dkvf[1] = dkvf[1] + dot_tn(soft.astype(BF), doh)
            return 0

        lax.fori_loop(lo, hi, body, 0)

    def head_end():
        dkvf[0] = rope_back(dkvf[0], cos[...], sin[...]).astype(BF).astype(F32)
        dkvf[1] = dkvf[1].astype(BF).astype(F32)
        q_core.start()
        kv_core.start()
        small[2:3, 0:QW] = jnp.sum(dqf[...], axis=0, keepdims=True)
        small[2:3, QW : QW + WIDTH] = jnp.sum(dkvf[0], axis=0, keepdims=True)
        small[2:3, QW + WIDTH : QW + 2 * WIDTH] = jnp.sum(dkvf[1], axis=0, keepdims=True)

    def input_grad():
        dn1[...] = (
            dot_nt(dqf[...].astype(BF), wq[...])
            + dot_nt(dkvf[0].astype(BF), wk[...])
            + dot_nt(dkvf[1].astype(BF), wv[...])
        )
        xf = tokens[...].astype(F32)
        normed = xf * lax.rsqrt(mean_last(xf * xf) + EPS)
        small[1:2, :] = jnp.sum(dn1[...] * normed, axis=0, keepdims=True)
        small_mate.start()
        dn1_copy.start()

    def exchange_end():
        q_core.wait()
        kv_core.wait()
        dh_core.wait()
        rkv[:TOK, :] = dkvf[c].astype(BF)
        rkv[TOK:, :] = xkvr[c].astype(BF)

        @pl.when(c == 0)
        def _():
            rq[:TOK, :] = dqf[...].astype(BF)
            rq[TOK:, :] = xqr[...].astype(BF)
            lb[...] = la[...]

        @pl.when(c == 1)
        def _():
            rq[...] = o2[...]
            lb[:, :TOK] = dhf[...].astype(BF).T
            lb[:, TOK:] = dhr[...].astype(BF).T

    def layer_end():
        lof[mine, :] = (h1[...] + x_end(6, False)).astype(BF).astype(F32)
        lo_copy.start()

    def input_end():
        dn1_copy.wait()
        total = dn1[mine, :] + dn1r[...]
        xf = tokens[mine, :].astype(F32)
        r1 = lax.rsqrt(mean_last(xf * xf) + EPS)
        normed = xf * r1
        e = total * g1[...].astype(F32)[None, :]
        grad = dh[...] + r1 * (e - normed * mean_last(e * normed))
        dn1[mine, :] = grad.astype(BF).astype(F32)
        di_copy.start()

    def small_copy(i, slot, to):
        return remote(small, sb.at[slot], sss.at[i], srs.at[i], to)

    small_mate = small_copy(0, 0, mate)
    quad_y = [small_copy(1 + i, 1 + y, by_y[i]) for i in range(3)]
    quad_z = [small_copy(4 + i, 5 + z, by_z[i]) for i in range(3)]
    quad_x = [small_copy(6 + i, 9 + me, peers[i]) for i in range(1, 4)]

    def small_add():
        small_mate.wait()
        gains = lax.broadcasted_iota(jnp.int32, small.shape, 0) < 2
        small[...] = small[...] + jnp.where(gains, sb[0], 0.0)

    def small_quad(copies, base, p):
        for copy in copies:
            copy.wait()
        sb[base + p] = small[...]
        small[...] = ((sb[base] + sb[base + 1]) + sb[base + 2]) + sb[base + 3]

    def start(copies):
        for copy in copies:
            copy.start()

    def fetched():
        for copy in fetches[1:]:
            copy.wait()

    extras = {
        0: [lambda: x_begin(0, dn2_h, True)],
        1: [lambda: x_ring1(0, dn2_h, True), fetched],
        3: [lambda: x_ring2(0)],
        5: [second_norm, lambda: x_begin(6, out_h, False)],
        7: [mix_grad, lambda: x_ring1(6, out_h, False)],
        8: [lambda: heads(0, 3)],
        9: [lambda: heads(3, 6), head_end, lambda: x_ring2(6)],
        10: [exchange_end],
        11: [input_grad],
        12: [small_add, lambda: start(quad_y)],
        13: [layer_end],
        14: [input_end, lambda: small_quad(quad_y, 1, y), lambda: start(quad_z)],
        16: [lambda: small_quad(quad_z, 5, z), lambda: start(quad_x)],
    }

    load(jnp.int32(0), lambda copy: copy.start())
    load(jnp.int32(1), lambda copy: copy.start())
    start(fetches[1:])
    fetches[0].wait()
    grads(jnp.int32(0))

    def tick(n, _):
        @pl.when((n >= R_SLOTS) & (n <= NU + 2))
        def _():
            for i in range(4):
                pl.semaphore_wait(credit.at[i], 1)

        @pl.when(n < NU)
        def _():
            for j in range(2):
                for way in range(2):
                    step_copy(n, 1, j, way).start()

        for s in range(1, 5):
            u = n - s

            @pl.when((u >= 0) & (u < NU))
            def _():
                advance(u, s)

        @pl.when((n >= 1) & (n <= NU + 3 - R_SLOTS))
        def _():
            for i, to in enumerate((ring["y"][1], ring["y"][0], ring["z"][1], ring["z"][0])):
                pl.semaphore_signal(credit.at[i], inc=1, device_id=to, device_id_type=MESH)

        @pl.when(n + 1 < NU)
        def _():
            grads(n + 1)

        for when, steps in extras.items():

            @pl.when(n == when)
            def _():
                for step in steps:
                    step()

        return 0

    lax.fori_loop(0, N_TICK, tick, 0)

    lo_copy.wait()
    lout_o[...] = lof[...].astype(BF)
    di_copy.wait()
    din_o[mine, :] = dn1[mine, :].astype(BF)
    din_o[other, :] = dir[...].astype(BF)
    small_quad(quad_x, 9, me)
    small_o[...] = small[...]

    def finish(u, _):
        for n in range(1, 4):
            last_copy(u, n).wait_recv()

            @pl.when(u >= NU - G_SLOTS)
            def _():
                last_copy(u, n).wait_send()

        return 0

    lax.fori_loop(0, NU, finish, 0)
    F_o[...] = F[...]


def finish_kernel(
    F, lout, din, small, lout_o, din_o, n1_o, dq_o, bq_o, dk_o, bk_o, dv_o, bv_o, dout_o, n2_o, gate_o, up_o, down_o
):
    lout_o[...] = lout[...]
    din_o[...] = din[...]

    def tile(i, col):
        return F[i, col // UW, :, col % UW : col % UW + 128]

    for m, out in enumerate((gate_o, up_o, down_o)):
        for i in range(4):
            for n in range(1 if i == 3 else 0, 9):
                at = slice(OFFS[i] + 128 * n, OFFS[i] + 128 * (n + 1))
                out[:, at] = tile(i, m * FFW + 128 * n)
    base = 3 * FFW
    dk_o[...] = tile(0, base) + tile(2, base)
    dv_o[...] = tile(1, base) + tile(3, base)
    for n in range(HEADS):
        at = slice(128 * n, 128 * (n + 1))
        col = base + 128 * (n + 1)
        dq_o[:, at] = tile(0, col) + tile(2, col)
        dout_o[:, at] = tile(1, col) + tile(3, col)
        bq_o[n : n + 1, :] = small[2:3, at]
    bk_o[...] = small[2:3, QW : QW + WIDTH]
    bv_o[...] = small[2:3, QW + WIDTH : QW + 2 * WIDTH]
    lane = lax.broadcasted_iota(jnp.int32, (24, D), 1)
    row = lax.broadcasted_iota(jnp.int32, (24, D), 0)
    own = lane == row + lax.axis_index("dp") * 24
    n2_o[...] = jnp.sum(jnp.where(own, small[0:1, :], 0.0), axis=1)
    n1_o[...] = jnp.sum(jnp.where(own, small[1:2, :], 0.0), axis=1)


def finish(*args):
    shape = jax.ShapeDtypeStruct
    whole = pl.BlockSpec(memory_space=VM)
    return pl.pallas_call(
        finish_kernel,
        name="finish",
        out_shape=(
            shape((TOK, D), BF), shape((TOK, D), BF), shape((24,), F32), shape((24, QW), F32),
            shape((HEADS, WIDTH), F32), shape((24, WIDTH), F32), shape((1, WIDTH), F32),
            shape((24, WIDTH), F32), shape((1, WIDTH), F32), shape((24, QW), F32), shape((24,), F32),
            shape((24, FFL), F32), shape((24, FFL), F32), shape((24, FFL), F32),
        ),
        in_specs=[whole] * 4,
        out_specs=(whole,) * 14,
        compiler_params=pltpu.CompilerParams(vmem_limit_bytes=60 * 2**20),
    )(*args)


def back(*args):
    shape = jax.ShapeDtypeStruct
    whole = pl.BlockSpec(memory_space=VM)
    hbm = pl.BlockSpec(memory_space=pl.ANY)
    dma = pltpu.SemaphoreType.DMA
    regular = pltpu.SemaphoreType.REGULAR
    return pl.pallas_call(
        back_kernel,
        name="back",
        out_shape=(
            shape((4, NU, 24, UW), F32), shape((TOK, D), BF), shape((TOK, D), BF), shape((8, D), F32),
        ),
        in_specs=[hbm] * 4 + [whole] * 2 + [hbm] * 17,
        out_specs=(whole,) * 4,
        scratch_shapes=[
            VM((D, 4 * TOK), BF), VM((D, 4 * TOK), BF), VM((D, 2 * TOK), BF), VM((2 * TOK, QW), BF),
            VM((TOK, D), BF), VM((TOK, D), BF), VM((HALF, D), F32),
            VM((TOK, QW), BF), VM((TOK, WIDTH), BF), VM((TOK, WIDTH), BF),
            VM((TOK, TOK), F32), VM((TOK, WIDTH), F32), VM((TOK, WIDTH), F32),
            VM((D, QW), BF), VM((D, WIDTH), BF), VM((D, WIDTH), BF), VM((QW, D), BF),
            VM((4, NU, 24, UW), F32),
            VM((G_SLOTS, 2, 4, 2, 4, 24, UW), F32),
            VM((R_SLOTS, 2, 2, 4, 24, UW), F32), VM((R_SLOTS, 2, 2, 2, 4, 24, UW), F32),
            VM((R_SLOTS, 2, 2, 24, UW), F32), VM((R_SLOTS, 2, 2, 2, 24, UW), F32),
            VM((2, 4 * TOK, UW), BF),
            VM((4, HALF, D), F32), VM((4, HALF, D), F32),
            VM((2, HALF // 2, D), F32), VM((2, HALF, D), F32),
            VM((TOK, D), F32), VM((TOK, D), F32), VM((HALF, D), F32), VM((D, 2 * TOK), BF),
            VM((TOK, QW), BF), VM((TOK, QW), F32), VM((TOK, QW), F32), VM((2 * TOK, QW), BF),
            VM((2, TOK, WIDTH), F32), VM((2, TOK, WIDTH), F32), VM((2 * TOK, WIDTH), BF),
            VM((TOK, D), F32), VM((HALF, D), F32), VM((HALF, D), F32), VM((TOK, D), F32),
            VM((8, D), F32), VM((13, 8, D), F32),
            dma((R_SLOTS, 4, 2, 2)), dma((R_SLOTS, 4, 2, 2)), dma((NU, 3)), dma((NU, 3)),
            regular((4,)), dma((19,)), dma((19,)), regular((3,)), dma((1,)), dma((2,)),
            dma((10,)), dma((10,)), dma((17,)),
        ],
        compiler_params=pltpu.CompilerParams(
            collective_id=2, has_side_effects=True, vmem_limit_bytes=63 * 2**20
        ),
    )(*args)


def on_device(
    tokens, lengths, keep_mask, norm1_gain, w_query, b_query, w_key, b_key, w_value, b_value,
    w_out, norm2_gain, w_gate, w_up, w_down, cotangent,
):
    q, k, v, mask, cos, sin, h1, la, o2, n2t, dyt, dgu, a, dn2_part, out_part = front(
        lengths, keep_mask, norm1_gain, b_query, b_key, b_value, norm2_gain,
        tokens, cotangent, w_query, w_key, w_value, w_out, w_gate, w_up, w_down,
    )
    results = list(finish(*back(
        dgu, a, dn2_part, out_part, norm1_gain, norm2_gain, n2t, dyt, la, o2, tokens, cotangent, h1,
        q, k, v, mask, cos, sin, w_query, w_key, w_value, w_out,
    )))
    results[9], results[13] = results[9].T, results[13].T
    return tuple(results)


def solution(mesh):
    placed = (
        P("dp", None), P("dp", None), P("dp"), P(), P(None, "tensor"), P("tensor", None),
        P(None, "tensor"), P("tensor", None), P(None, "tensor"), P("tensor", None),
        P("tensor", None), P(), P(None, "tensor"), P(None, "tensor"), P("tensor", None), P("dp", None),
    )
    return jax.shard_map(
        on_device,
        mesh=mesh,
        in_specs=placed,
        out_specs=(
            P("dp", None), P("dp", None), P("dp"), P("dp", "tensor"), P("tensor", None),
            P("dp", "tensor"), P("tensor", None), P("dp", "tensor"), P("tensor", None),
            P("tensor", "dp"), P("dp"), P("dp", "tensor"), P("dp", "tensor"), P("tensor", "dp"),
        ),
        check_vma=False,
    )
```

```python
import math

import jax
import jax.numpy as jnp
from jax import lax
from jax.experimental import pallas as pl
from jax.experimental.pallas import tpu as pltpu
from jax.sharding import PartitionSpec as P

EPS = 1e-06
ROPE_BASE = 10000.0
NEG_FILL = -1e30
MESH = pl.DeviceIdType.MESH
BF = jnp.bfloat16
F32 = jnp.float32
VM = pltpu.VMEM

D = 1536
TOK = 256
HALF = 128
SUB = 64
HEADS = 6
WIDTH = 128
QW = HEADS * WIDTH
FFL = 4480
FFW = 1152
OFFS = (0, 1152, 2304, 3328)

UW = 256
NU = 17
GATE_UNITS = 9
G_SLOTS = 7
R_SLOTS = 3
N_TICK = NU + 4


def coords():
    dp = lax.axis_index("dp")
    t = lax.axis_index("tensor")
    return dp // 16, lax.rem(dp // 8, 2), lax.rem(dp // 2, 4), lax.rem(dp, 2), t


def device(y, xh, z, c, t):
    return (((y * 2 + xh) * 4 + z) * 2 + c, t)


def device_x(y, x, z, c):
    return device(y, x // 2, z, c, lax.rem(x, 2))


def remote(src, dst, send, recv, to):
    return pltpu.make_async_remote_copy(
        src_ref=src, dst_ref=dst, send_sem=send, recv_sem=recv, device_id=to, device_id_type=MESH
    )


def greet(devices):
    barrier = pltpu.get_barrier_semaphore()
    for to in devices:
        pl.semaphore_signal(barrier, inc=1, device_id=to, device_id_type=MESH)
    pl.semaphore_wait(barrier, len(devices))


def dot(left, right):
    return jnp.dot(left, right, preferred_element_type=F32)


def dot_nt(left, right):
    return lax.dot_general(left, right, (((1,), (1,)), ((), ())), preferred_element_type=F32)


def dot_tn(left, right):
    return lax.dot_general(left, right, (((0,), (0,)), ((), ())), preferred_element_type=F32)


def rope(v, cosine, sine):
    return v * cosine + pltpu.roll(v, WIDTH // 2, 1) * sine


def rope_back(w, cosine, sine):
    return w * cosine + pltpu.roll(w * sine, WIDTH // 2, 1)


def mean_last(v):
    return jnp.mean(v, axis=-1, keepdims=True)


def front_kernel(
    lengths, keep, g1, bq, bk, bv, g2, tokens_h, cot_h, wq_h, wk_h, wv_h, wo_h, wg_h, wu_h, wd_h,
    q_h, k_h, v_h, mask_h, cos_h, sin_h, h1_h, la_h, o2_h, n2t_h, dyt_h, dgu_h, a_h, dn2_h, out_h,
    tokens, cot, wq, wk, wv, wo, wgu, wd, q_o, k_o, v_o, mask_o, cos_o, sin_o, h1_o, la_o, o2_o,
    n2f, dyf, n1f, n1r, of, orr, part, prec, n2t_s, dyt_s, dgu_s, a_s, dn2_s, out_s,
    ss, rs, isem, ksem, osem, psem, tsem,
):
    y, xh, z, c, t = coords()
    x = 2 * xh + t
    x1, x2, x3 = lax.rem(x + 1, 4), lax.rem(x + 2, 4), lax.rem(x + 3, 4)
    right = device_x(y, x1, z, c)
    left = device_x(y, x3, z, c)
    core = device(y, xh, z, 1 - c, t)
    mate = device(y, xh, z, c, 1 - t)
    cross = device_x(y, 3 - x, z, c)
    me = 2 * xh + c
    hidden = pl.ds(pl.multiple_of((me * 9 - me // 3) * 128, 128), FFW)
    fetches = [
        pltpu.make_async_copy(src, dst, isem.at[i])
        for i, (src, dst) in enumerate((
            (cot_h, cot), (tokens_h, tokens), (wk_h, wk), (wv_h, wv), (wq_h, wq), (wo_h, wo),
            (wg_h.at[:, hidden], wgu.at[:, pl.ds(0, FFW)]), (wu_h.at[:, hidden], wgu.at[:, pl.ds(FFW, FFW)]),
            (wd_h.at[hidden, :], wd),
        ))
    ]
    for copy in fetches[:6]:
        copy.start()
    greet((right, left, core))
    mine = pl.ds(pl.multiple_of(t * HALF, HALF), HALF)
    other = pl.ds(pl.multiple_of((1 - t) * HALF, HALF), HALF)
    sent = []

    def send(src, dst, to):
        i = len(sent)
        copy = remote(src, dst, ss.at[i], rs.at[i], to)
        copy.start()
        sent.append(copy)
        return copy

    kept = []

    def keep_copy(src, dst):
        copy = pltpu.make_async_copy(src, dst, ksem.at[len(kept)])
        copy.start()
        kept.append(copy)

    near = pl.ds(2 * xh, 2)
    fetches[0].wait()
    dyf[near, c] = cot[...].astype(F32).reshape(2, HALF, D)
    dy_own = send(dyf.at[x, c], dyf.at[x, c], cross)
    x_mate = 2 * xh + 1 - t
    dy_core = send(dyf.at[near, c], dyf.at[near, c], core)

    rows = lax.broadcasted_iota(jnp.int32, (TOK, TOK), 0)
    cols = lax.broadcasted_iota(jnp.int32, (TOK, TOK), 1)
    row_id = lax.broadcasted_iota(jnp.int32, (TOK, WIDTH), 0)
    place = row_id
    seg_r = jnp.zeros((TOK, TOK), jnp.int32)
    seg_c = jnp.zeros((TOK, TOK), jnp.int32)
    end = jnp.int32(0)
    for i in range(4):
        span = lengths[0, i]
        end = end + span
        seg_r = seg_r + (rows >= end).astype(jnp.int32)
        seg_c = seg_c + (cols >= end).astype(jnp.int32)
        place = place - jnp.where(row_id >= end, span, 0)
    allowed = (seg_r == seg_c) & (cols <= rows) & ((keep[...][None, :] == 1) | (cols == rows))
    mask_o[...] = allowed.astype(F32)
    lane = lax.broadcasted_iota(jnp.int32, (TOK, WIDTH), 1)
    first = lane < WIDTH // 2
    step = jnp.where(first, lane, lane - WIDTH // 2).astype(F32)
    angle = place.astype(F32) * jnp.exp(step * (-2.0 * math.log(ROPE_BASE) / WIDTH))
    cosine = jnp.cos(angle)
    sine = jnp.sin(angle) * jnp.where(first, -1.0, 1.0)
    cos_o[...] = cosine
    sin_o[...] = sine

    fetches[1].wait()
    xf = tokens[...].astype(F32)
    r1 = lax.rsqrt(mean_last(xf * xf) + EPS)
    n1 = (xf * r1 * g1[...].astype(F32)[None, :]).astype(BF)
    n1f[...] = n1.astype(F32)
    n1_core = send(n1f, n1r, core)
    for copy in fetches[2:6]:
        copy.wait()
    for copy in fetches[6:]:
        copy.start()
    kp = dot(n1, wk[...]) + bk[...].astype(F32)
    k_o[...] = rope(kp, cosine, sine).astype(BF)
    v_o[...] = (dot(n1, wv[...]) + bv[...].astype(F32)).astype(BF)
    bias = bq[...].astype(F32)
    for h in range(HEADS):
        at = slice(h * WIDTH, (h + 1) * WIDTH)
        qp = dot(n1, wq[:, at]) + bias[h : h + 1]
        q_o[:, at] = (rope(qp, cosine, sine) * WIDTH**-0.5).astype(BF)

    def attend(at_rows):
        def head(h, _):
            at = pl.ds(pl.multiple_of(h * WIDTH, WIDTH), WIDTH)
            s = jnp.where(mask_o[at_rows, :] > 0.5, dot_nt(q_o[at_rows, at], k_o[...]), NEG_FILL)
            e = jnp.exp(s - jnp.max(s, axis=-1, keepdims=True))
            soft = (e / jnp.sum(e, axis=-1, keepdims=True)).astype(BF)
            o = dot(soft, v_o[...]).astype(BF)
            o2_o[at_rows, at] = o
            of[at_rows, at] = o.astype(F32)
            return 0

        lax.fori_loop(0, HEADS, head, 0)

    def quarter(n):
        return pl.ds(n * SUB, SUB)

    attend(other)
    part[0] = dot(o2_o[other, :], wo[...])
    halves = [send(part.at[0, quarter(n)], prec.at[quarter(n)], mate) for n in range(2)]
    attend(mine)
    o_core = send(of, orr, core)
    part[1] = dot(o2_o[mine, :], wo[...])

    order = (
        ((x, 0, HALF),),
        ((x3, 0, SUB), (x1, 0, SUB)),
        ((x3, SUB, SUB), (x1, SUB, SUB)),
        ((x2, 0, HALF),),
    )

    def pieces(n):
        out, at = [], 0
        for xx, lo, size in order[n]:
            for cc in range(2):
                out.append((at, size, xx, cc, lo))
                at += size
        return out

    def gather(ref, n):
        if len(order[n]) == 1:
            return ref[order[n][0][0]].reshape(TOK, D).astype(BF)
        return jnp.concatenate([ref[xx, cc, lo : lo + size] for _, size, xx, cc, lo in pieces(n)], axis=0).astype(BF)

    def turned(n):
        return pltpu.make_async_copy(dyt_s.at[n % 2], dyt_h.at[:, pl.ds(n * TOK, TOK)], tsem.at[n % 2])

    def turn(n):
        if n >= 2:
            turned(n - 2).wait()
        dyt_s[n % 2] = gather(dyf, n).T
        turned(n).start()

    for src, dst in ((q_o, q_h), (k_o, k_h), (v_o, v_h), (mask_o, mask_h), (cos_o, cos_h), (sin_o, sin_h)):
        keep_copy(src, dst)
    la_o[:, :TOK] = n1.T
    n1_core.wait_recv()
    la_o[:, TOK:] = n1r[...].astype(BF).T
    keep_copy(la_o, la_h)
    o_core.wait_recv()
    o2_o[TOK:, :] = orr[...].astype(BF)
    keep_copy(o2_o, o2_h)
    dy_core.wait_recv()
    turn(0)

    def pass_on(xx, to, lo, size):
        at = n2f.at[xx, c, pl.ds(lo, size)]
        return send(at, at, to)

    to_right, to_left, to_core = [], [], []
    for n in range(2):
        halves[n].wait_recv()
        at = quarter(n)
        own = tokens[pl.ds(pl.multiple_of(t * HALF + n * SUB, SUB), SUB), :].astype(F32)
        h1 = own + part[1, at] + prec[at]
        h1_o[at] = h1
        r2 = lax.rsqrt(mean_last(h1 * h1) + EPS)
        n2f[x, c, at] = (h1 * r2 * g2[...].astype(F32)[None, :]).astype(BF).astype(F32)
        to_right.append(pass_on(x, right, n * SUB, SUB))
        to_left.append(pass_on(x, left, n * SUB, SUB))
        to_core.append(pass_on(x, core, n * SUB, SUB))
    keep_copy(h1_o, h1_h)

    unit = lax.broadcasted_iota(jnp.int32, (1, FFW), 1)
    live = jnp.where((unit < 128) & (me == 3), 0.0, 1.0)

    def results(n):
        slot, at = n % 2, pl.ds(n * TOK, TOK)
        moves = [(n2t_s.at[slot], n2t_h.at[:, at]), (dgu_s.at[slot], dgu_h.at[at]), (a_s.at[slot], a_h.at[at])]
        copies = [pltpu.make_async_copy(src, dst, osem.at[slot, i]) for i, (src, dst) in enumerate(moves)]
        for b, (staged, dst) in enumerate(((dn2_s, dn2_h), (out_s, out_h))):
            for i, (row, size, xx, cc, lo) in enumerate(pieces(n)):
                copies.append(
                    pltpu.make_async_copy(
                        staged.at[slot, pl.ds(row, size)], dst.at[xx, cc, pl.ds(lo, size)], psem.at[slot, b, i]
                    )
                )
        early = (0, 2) + tuple(range(3 + len(pieces(n)), len(copies)))
        return [copies[i] for i in early], [copy for i, copy in enumerate(copies) if i not in early]

    def feed(n):
        slot = n % 2
        here = gather(n2f, n)
        both = dot(here, wgu[...])
        g, u = both[:, :FFW], both[:, FFW:]
        if n >= 2:
            for copy in sum(results(n - 2), []):
                copy.wait()
        n2t_s[slot] = here.T
        sg = live / (1.0 + jnp.exp(-g))
        silu = g * sg
        a = (silu * u).astype(BF)
        a_s[slot] = a
        out_s[slot] = dot(a, wd[...])
        early, late = results(n)
        for copy in early:
            copy.start()
        if n == 3:
            dy_across.wait_recv()
            turn(3)
        da = dot_nt(gather(dyf, n), wd[...])
        dg = (da * u * sg * (1.0 + g * (1.0 - sg))).astype(BF)
        du = (da * silu).astype(BF)
        dgu_s[slot, :, :FFW] = dg
        dgu_s[slot, :, FFW:] = du
        dn2_s[slot] = dot_nt(dgu_s[slot], wgu[...])
        for copy in late:
            copy.start()

    passed, core_side, core_across = [], [], []

    dy_mate = send(dyf.at[x_mate, c, pl.ds(0, 96)], dyf.at[x_mate, c, pl.ds(0, 96)], cross)
    dy_own.wait_recv()
    dy_pass = send(dyf.at[3 - x, c, pl.ds(96, 32)], dyf.at[3 - x, c, pl.ds(96, 32)], mate)

    def step_one(n):
        to_right[n].wait_recv()
        passed.append(pass_on(x3, right, n * SUB, SUB // 2))
        core_side.append(pass_on(x3, core, n * SUB, SUB))
        to_left[n].wait_recv()
        passed.append(pass_on(x1, left, n * SUB + SUB // 2, SUB // 2))
        core_side.append(pass_on(x1, core, n * SUB, SUB))

    def step_two(n):
        for copy in passed[2 * n : 2 * n + 2]:
            copy.wait_recv()
        core_across.append(pass_on(x2, core, n * SUB, SUB))

    for copy in to_core:
        copy.wait_recv()
    for copy in fetches[6:]:
        copy.wait()
    feed(0)
    step_one(0)
    dy_side = send(dyf.at[3 - x, c], dyf.at[3 - x, c], core)
    dy_side.wait_recv()
    turn(1)
    for copy in core_side:
        copy.wait_recv()
    feed(1)
    step_one(1)
    turn(2)
    for copy in core_side[2:]:
        copy.wait_recv()
    feed(2)
    step_two(0)
    dy_mate.wait_recv()
    dy_pass.wait_recv()
    dy_across = send(dyf.at[x2, c], dyf.at[x2, c], core)
    step_two(1)
    for copy in core_across:
        copy.wait_recv()
    feed(3)
    for n in (2, 3):
        turned(n).wait()
        for copy in sum(results(n), []):
            copy.wait()
    for copy in kept:
        copy.wait()
    for copy in sent:
        copy.wait_send()


def front(*args):
    shape = jax.ShapeDtypeStruct
    whole = pl.BlockSpec(memory_space=VM)
    scalars = pl.BlockSpec(memory_space=pltpu.SMEM)
    hbm = pl.BlockSpec(memory_space=pl.ANY)
    dma = pltpu.SemaphoreType.DMA
    return pl.pallas_call(
        front_kernel,
        name="front",
        out_shape=(
            shape((TOK, QW), BF), shape((TOK, WIDTH), BF), shape((TOK, WIDTH), BF),
            shape((TOK, TOK), F32), shape((TOK, WIDTH), F32), shape((TOK, WIDTH), F32),
            shape((HALF, D), F32), shape((D, 2 * TOK), BF), shape((2 * TOK, QW), BF),
            shape((D, 4 * TOK), BF), shape((D, 4 * TOK), BF),
            shape((4 * TOK, 2 * FFW), BF), shape((4 * TOK, FFW), BF),
            shape((4, 2, HALF, D), F32), shape((4, 2, HALF, D), F32),
        ),
        in_specs=[scalars] + [whole] * 6 + [hbm] * 9,
        out_specs=(hbm,) * 15,
        scratch_shapes=[
            VM((TOK, D), BF), VM((TOK, D), BF),
            VM((D, QW), BF), VM((D, WIDTH), BF), VM((D, WIDTH), BF), VM((QW, D), BF),
            VM((D, 2 * FFW), BF), VM((FFW, D), BF),
            VM((TOK, QW), BF), VM((TOK, WIDTH), BF), VM((TOK, WIDTH), BF),
            VM((TOK, TOK), F32), VM((TOK, WIDTH), F32), VM((TOK, WIDTH), F32),
            VM((HALF, D), F32), VM((D, 2 * TOK), BF), VM((2 * TOK, QW), BF),
            VM((4, 2, HALF, D), F32), VM((4, 2, HALF, D), F32),
            VM((TOK, D), F32), VM((TOK, D), F32),
            VM((TOK, QW), F32), VM((TOK, QW), F32),
            VM((2, HALF, D), F32), VM((HALF, D), F32),
            VM((2, D, TOK), BF), VM((2, D, TOK), BF),
            VM((2, TOK, 2 * FFW), BF), VM((2, TOK, FFW), BF),
            VM((2, TOK, D), F32), VM((2, TOK, D), F32),
            dma((32,)), dma((32,)), dma((9,)), dma((9,)), dma((2, 3)), dma((2, 2, 4)), dma((2,)),
        ],
        compiler_params=pltpu.CompilerParams(
            collective_id=1, has_side_effects=True, vmem_limit_bytes=63 * 2**20
        ),
    )(*args)


def back_kernel(
    dgu_h, a_h, dn2_h, out_h, g1, g2, n2t_h, dyt_h, la_h, o2_h, tokens_h, cot_h, h1_h, q_h, k_h, v_h,
    mask_h, cos_h, sin_h, wq_h, wk_h, wv_h, wo_h,
    F_o, lout_o, din_o, small_o,
    n2t, dyt, la, o2, tokens, cot, h1, q, k, v, mask, cos, sin, wq, wk, wv, wo,
    F, G, R1, R2, R3, R4, RB, C, L, S1, S2, dhf, dhr, dh, lb, do, dqf, xqr, rq, dkvf, xkvr, rkv,
    dn1, dn1r, dir, lof, small, sb,
    ss, rs, fss, frs, credit, xss, xrs, free, lsem, bsem, sss, srs, isem,
):
    fetches = [
        pltpu.make_async_copy(src, dst, isem.at[i])
        for i, (src, dst) in enumerate((
            (n2t_h, n2t), (dyt_h, dyt), (cot_h, cot), (h1_h, h1), (wo_h, wo), (q_h, q), (k_h, k), (v_h, v),
            (mask_h, mask), (cos_h, cos), (sin_h, sin), (tokens_h, tokens), (wq_h, wq), (wk_h, wk),
            (wv_h, wv), (la_h, la), (o2_h, o2),
        ))
    ]
    for copy in fetches[:1]:
        copy.start()
    y, xh, z, c, t = coords()
    x = 2 * xh + t
    me = 2 * xh + c
    by_y = tuple(device(lax.rem(y + i, 4), xh, z, c, t) for i in (1, 2, 3))
    by_z = tuple(device(y, xh, lax.rem(z + i, 4), c, t) for i in (1, 2, 3))
    ring = {"y": (by_y[0], by_y[2]), "z": (by_z[0], by_z[2])}
    right = device_x(y, lax.rem(x + 1, 4), z, c)
    left = device_x(y, lax.rem(x + 3, 4), z, c)
    core = device(y, xh, z, 1 - c, t)
    mate = device(y, xh, z, c, 1 - t)
    over = device(y, 1 - xh, z, c, t)
    over_core = device(y, 1 - xh, z, 1 - c, t)
    peers = (None, core, over, over_core)
    greet(by_y + by_z + (right, left, core, over, over_core))
    mine = pl.ds(pl.multiple_of(t * HALF, HALF), HALF)
    other = pl.ds(pl.multiple_of((1 - t) * HALF, HALF), HALF)

    R = (R1, R2, R3, R4)

    def axis(j, s):
        return ("y", y) if (j == 0) == (s <= 2) else ("z", z)

    def part(g, j, s, i, way):
        own = z if j else y
        if s == 1:
            return G.at[g, j, i, way]
        if s == 2:
            return G.at[g, j, i]
        return G.at[g, j, own, way, i] if s == 3 else G.at[g, j, own, :, i]

    def step_copy(u, s, j, way):
        name, p = axis(j, s)
        g, r = lax.rem(u, G_SLOTS), lax.rem(u, R_SLOTS)
        to = lax.rem(p + (2 if s % 2 else (3 if way else 1)), 4)
        return remote(
            part(g, j, s, to, way),
            R[s - 1].at[r, j, way],
            ss.at[r, s - 1, j, way],
            rs.at[r, s - 1, j, way],
            ring[name][way],
        )

    def total(u, px, pc):
        return G.at[lax.rem(u, G_SLOTS), px, jnp.where(px == 0, y, z), pc, jnp.where(px == 0, z, y)]

    def last_copy(u, n):
        px = 1 - xh if n & 2 else xh
        pc = 1 - c if n & 1 else c
        return remote(total(u, px, pc), F.at[me, u], fss.at[u, n - 1], frs.at[u, n - 1], peers[n])

    def advance(u, s):
        g, r = lax.rem(u, G_SLOTS), lax.rem(u, R_SLOTS)
        for j in range(2):
            _, p = axis(j, s)
            for way in range(2):
                step_copy(u, s, j, way).wait_recv()
                if s % 2:
                    at = part(g, j, s, lax.rem(p + (3 if way else 1), 4), way)
                    at[...] = at[...] + R[s - 1][r, j, way]
                    step_copy(u, s + 1, j, way).start()
            if s % 2 == 0:
                at = part(g, j, s, p, 0)
                at[...] = at[...] + R[s - 1][r, j, 0] + R[s - 1][r, j, 1]
                if s == 2:
                    for way in range(2):
                        step_copy(u, 3, j, way).start()
            for way in range(2):
                step_copy(u, s, j, way).wait_send()
        if s == 4:
            for n in range(1, 4):
                last_copy(u, n).start()
            F[me, u] = total(u, xh, c)[...]

    def load(u, act):
        r = lax.rem(u, 2)

        @pl.when(u < 9)
        def _():
            at = pl.ds(pl.multiple_of(u * UW, UW), UW)
            act(pltpu.make_async_copy(dgu_h.at[:, at], RB.at[r], bsem.at[r]))

        @pl.when((u >= 9) & (u < 13))
        def _():
            at = pl.ds(pl.multiple_of((u - 9) * UW, UW), UW)
            act(pltpu.make_async_copy(a_h.at[:, at], RB.at[r], bsem.at[r]))

        @pl.when(u == 13)
        def _():
            act(pltpu.make_async_copy(a_h.at[:, pl.ds(1024, 128)], RB.at[r, :, pl.ds(0, 128)], bsem.at[r]))

    def product(g, left_ref, rhs, w, o0):
        def body(i, _):
            lhs = left_ref[pl.ds(pl.multiple_of(i * 384, 384), 384), :]
            res = dot(lhs, rhs).reshape(2, 4, 2, 24, w)
            for zz in range(4):
                for cc in range(2):
                    G[g, 0, i, cc, zz, :, o0 : o0 + w] = res[0, zz, cc]
                    G[g, 1, zz, cc, i, :, o0 : o0 + w] = res[1, zz, cc]
            return 0

        lax.fori_loop(0, 4, body, 0)

    def grads(u):
        g = lax.rem(u, G_SLOTS)

        @pl.when(u >= G_SLOTS)
        def _():
            for n in range(1, 4):
                last_copy(u - G_SLOTS, n).wait_send()

        load(u, lambda copy: copy.wait())

        @pl.when(u < 9)
        def _():
            product(g, n2t, RB[lax.rem(u, 2)], UW, 0)

        @pl.when((u >= 9) & (u < 13))
        def _():
            product(g, dyt, RB[lax.rem(u, 2)], UW, 0)

        @pl.when(u == 13)
        def _():
            product(g, dyt, RB[1, :, 0:128], 128, 0)
            product(g, la, rkv[...], 128, 128)

        @pl.when(u >= 14)
        def _():
            product(g, lb, rq[:, pl.ds(pl.multiple_of((u - 14) * UW, UW), UW)], UW, 0)

        load(u + 2, lambda copy: copy.start())

    def xcopy(i, src, dst, to):
        return remote(src, dst, xss.at[i], xrs.at[i], to)

    def core_copy(base, src):
        return xcopy(base, src.at[:, 1 - c], C, core)

    def local_copy(src):
        return pltpu.make_async_copy(src.at[:, c], L, lsem.at[0])

    def lrow(xx, lo, n):
        return L.at[xx, pl.ds(lo, n)]

    x1, x2, x3 = lax.rem(x + 1, 4), lax.rem(x + 2, 4), lax.rem(x + 3, 4)

    def ring1(base):
        return [
            xcopy(base + 2, lrow(x2, 0, 64), S1.at[0], right),
            xcopy(base + 3, lrow(x2, 64, 64), S1.at[1], left),
        ]

    def ring2(base):
        return [
            xcopy(base + 4, lrow(x1, 0, HALF), S2.at[0], right),
            xcopy(base + 5, lrow(x3, 0, HALF), S2.at[1], left),
        ]

    def x_begin(base, src, first):
        if not first:
            pl.semaphore_wait(free.at[0], 1)
        core_copy(base, src).start()
        local_copy(src).start()

    def x_ring1(base, src, first):
        core_copy(base, src).wait()
        local_copy(src).wait()

        def add(i, _):
            L[i] = L[i] + C[i]
            return 0

        lax.fori_loop(0, 4, add, 0)
        if first:
            pl.semaphore_signal(free.at[0], inc=1, device_id=core, device_id_type=MESH)
        else:
            pl.semaphore_wait(free.at[1], 1)
            pl.semaphore_wait(free.at[2], 1)
        for copy in ring1(base):
            copy.start()

    def x_ring2(base):
        for copy in ring1(base):
            copy.wait()
        low, high = lrow(x1, 0, 64), lrow(x3, 64, 64)
        low[...] = low[...] + S1[0]
        high[...] = high[...] + S1[1]
        for copy in ring2(base):
            copy.start()

    def x_end(base, first):
        for copy in ring2(base):
            copy.wait()
        total = lrow(x, 0, HALF)[...] + S2[0] + S2[1]
        if first:
            pl.semaphore_signal(free.at[1], inc=1, device_id=right, device_id_type=MESH)
            pl.semaphore_signal(free.at[2], inc=1, device_id=left, device_id_type=MESH)
        return total

    dh_copy = xcopy(12, dhf.at[mine], dhf.at[mine], mate)
    dh_core = xcopy(13, dhf, dhr, core)
    q_core = xcopy(14, dqf, xqr, core)
    kv_core = xcopy(15, dkvf, xkvr, core)
    dn1_copy = xcopy(16, dn1.at[other], dn1r, mate)
    lo_copy = xcopy(17, lof.at[mine], lof.at[mine], mate)
    di_copy = xcopy(18, dn1.at[mine], dir, mate)

    def second_norm():
        dn2 = x_end(0, True)
        hh = h1[...]
        r2 = lax.rsqrt(mean_last(hh * hh) + EPS)
        normed = hh * r2
        e = dn2 * g2[...].astype(F32)[None, :]
        grad = cot[mine, :].astype(F32) + r2 * (e - normed * mean_last(e * normed))
        dh[...] = grad
        dhf[mine, :] = grad.astype(BF).astype(F32)
        dh_copy.start()
        small[...] = jnp.zeros_like(small)
        small[0:1, :] = jnp.sum(dn2 * normed, axis=0, keepdims=True)

    def mix_grad():
        dh_copy.wait()
        dh_core.start()
        do[...] = dot_nt(dhf[...].astype(BF), wo[...]).astype(BF)
        dkvf[...] = jnp.zeros_like(dkvf)

    def heads(lo, hi):
        def body(h, _):
            at = pl.ds(pl.multiple_of(h * WIDTH, WIDTH), WIDTH)
            qh, doh = q[:, at], do[:, at]
            s = jnp.where(mask[...] > 0.5, dot_nt(qh, k[...]), NEG_FILL)
            e = jnp.exp(s - jnp.max(s, axis=-1, keepdims=True))
            soft = e / jnp.sum(e, axis=-1, keepdims=True)
            dp = dot_nt(doh, v[...])
            dz = (soft * (dp - jnp.sum(soft * dp, axis=-1, keepdims=True))).astype(BF)
            dq = dot(dz, k[...]) * WIDTH**-0.5
            dqf[:, at] = rope_back(dq, cos[...], sin[...]).astype(BF).astype(F32)
            dkvf[0] = dkvf[0] + dot_tn(dz, qh)
            dkvf[1] = dkvf[1] + dot_tn(soft.astype(BF), doh)
            return 0

        lax.fori_loop(lo, hi, body, 0)

    def head_end():
        dkvf[0] = rope_back(dkvf[0], cos[...], sin[...]).astype(BF).astype(F32)
        dkvf[1] = dkvf[1].astype(BF).astype(F32)
        q_core.start()
        kv_core.start()
        small[2:3, 0:QW] = jnp.sum(dqf[...], axis=0, keepdims=True)
        small[2:3, QW : QW + WIDTH] = jnp.sum(dkvf[0], axis=0, keepdims=True)
        small[2:3, QW + WIDTH : QW + 2 * WIDTH] = jnp.sum(dkvf[1], axis=0, keepdims=True)

    def input_grad():
        dn1[...] = (
            dot_nt(dqf[...].astype(BF), wq[...])
            + dot_nt(dkvf[0].astype(BF), wk[...])
            + dot_nt(dkvf[1].astype(BF), wv[...])
        )
        xf = tokens[...].astype(F32)
        normed = xf * lax.rsqrt(mean_last(xf * xf) + EPS)
        small[1:2, :] = jnp.sum(dn1[...] * normed, axis=0, keepdims=True)
        small_mate.start()
        dn1_copy.start()

    def exchange_end():
        q_core.wait()
        kv_core.wait()
        dh_core.wait()
        rkv[:TOK, :] = dkvf[c].astype(BF)
        rkv[TOK:, :] = xkvr[c].astype(BF)

        @pl.when(c == 0)
        def _():
            rq[:TOK, :] = dqf[...].astype(BF)
            rq[TOK:, :] = xqr[...].astype(BF)
            lb[...] = la[...]

        @pl.when(c == 1)
        def _():
            rq[...] = o2[...]
            lb[:, :TOK] = dhf[...].astype(BF).T
            lb[:, TOK:] = dhr[...].astype(BF).T

    def layer_end():
        lof[mine, :] = (h1[...] + x_end(6, False)).astype(BF).astype(F32)
        lo_copy.start()

    def input_end():
        dn1_copy.wait()
        total = dn1[mine, :] + dn1r[...]
        xf = tokens[mine, :].astype(F32)
        r1 = lax.rsqrt(mean_last(xf * xf) + EPS)
        normed = xf * r1
        e = total * g1[...].astype(F32)[None, :]
        grad = dh[...] + r1 * (e - normed * mean_last(e * normed))
        dn1[mine, :] = grad.astype(BF).astype(F32)
        di_copy.start()

    def small_copy(i, slot, to):
        return remote(small, sb.at[slot], sss.at[i], srs.at[i], to)

    small_mate = small_copy(0, 0, mate)
    quad_y = [small_copy(1 + i, 1 + y, by_y[i]) for i in range(3)]
    quad_z = [small_copy(4 + i, 5 + z, by_z[i]) for i in range(3)]
    quad_x = [small_copy(6 + i, 9 + me, peers[i]) for i in range(1, 4)]

    def small_add():
        small_mate.wait()
        gains = lax.broadcasted_iota(jnp.int32, small.shape, 0) < 2
        small[...] = small[...] + jnp.where(gains, sb[0], 0.0)

    def small_quad(copies, base, p):
        for copy in copies:
            copy.wait()
        sb[base + p] = small[...]
        small[...] = ((sb[base] + sb[base + 1]) + sb[base + 2]) + sb[base + 3]

    def start(copies):
        for copy in copies:
            copy.start()

    def fetched():
        for copy in fetches[1:]:
            copy.wait()

    extras = {
        0: [lambda: x_begin(0, dn2_h, True)],
        1: [lambda: x_ring1(0, dn2_h, True), fetched],
        3: [lambda: x_ring2(0)],
        5: [second_norm, lambda: x_begin(6, out_h, False)],
        7: [mix_grad, lambda: x_ring1(6, out_h, False)],
        8: [lambda: heads(0, 3)],
        9: [lambda: heads(3, 6), head_end, lambda: x_ring2(6)],
        10: [exchange_end],
        11: [input_grad],
        12: [small_add, lambda: start(quad_y)],
        13: [layer_end],
        14: [input_end, lambda: small_quad(quad_y, 1, y), lambda: start(quad_z)],
        16: [lambda: small_quad(quad_z, 5, z), lambda: start(quad_x)],
    }

    load(jnp.int32(0), lambda copy: copy.start())
    load(jnp.int32(1), lambda copy: copy.start())
    start(fetches[1:])
    fetches[0].wait()
    grads(jnp.int32(0))

    def tick(n, _):
        @pl.when((n >= R_SLOTS) & (n <= NU + 2))
        def _():
            for i in range(4):
                pl.semaphore_wait(credit.at[i], 1)

        @pl.when(n < NU)
        def _():
            for j in range(2):
                for way in range(2):
                    step_copy(n, 1, j, way).start()

        for s in range(1, 5):
            u = n - s

            @pl.when((u >= 0) & (u < NU))
            def _():
                advance(u, s)

        @pl.when((n >= 1) & (n <= NU + 3 - R_SLOTS))
        def _():
            for i, to in enumerate((ring["y"][1], ring["y"][0], ring["z"][1], ring["z"][0])):
                pl.semaphore_signal(credit.at[i], inc=1, device_id=to, device_id_type=MESH)

        @pl.when(n + 1 < NU)
        def _():
            grads(n + 1)

        for when, steps in extras.items():

            @pl.when(n == when)
            def _():
                for step in steps:
                    step()

        return 0

    lax.fori_loop(0, N_TICK, tick, 0)

    lo_copy.wait()
    lout_o[...] = lof[...].astype(BF)
    di_copy.wait()
    din_o[mine, :] = dn1[mine, :].astype(BF)
    din_o[other, :] = dir[...].astype(BF)
    small_quad(quad_x, 9, me)
    small_o[...] = small[...]

    def finish(u, _):
        for n in range(1, 4):
            last_copy(u, n).wait_recv()

            @pl.when(u >= NU - G_SLOTS)
            def _():
                last_copy(u, n).wait_send()

        return 0

    lax.fori_loop(0, NU, finish, 0)
    F_o[...] = F[...]


def finish_kernel(
    F, lout, din, small, lout_o, din_o, n1_o, dq_o, bq_o, dk_o, bk_o, dv_o, bv_o, dout_o, n2_o, gate_o, up_o, down_o
):
    lout_o[...] = lout[...]
    din_o[...] = din[...]

    def tile(i, col):
        return F[i, col // UW, :, col % UW : col % UW + 128]

    for m, out in enumerate((gate_o, up_o, down_o)):
        for i in range(4):
            for n in range(1 if i == 3 else 0, 9):
                at = slice(OFFS[i] + 128 * n, OFFS[i] + 128 * (n + 1))
                out[:, at] = tile(i, m * FFW + 128 * n)
    base = 3 * FFW
    dk_o[...] = tile(0, base) + tile(2, base)
    dv_o[...] = tile(1, base) + tile(3, base)
    for n in range(HEADS):
        at = slice(128 * n, 128 * (n + 1))
        col = base + 128 * (n + 1)
        dq_o[:, at] = tile(0, col) + tile(2, col)
        dout_o[:, at] = tile(1, col) + tile(3, col)
        bq_o[n : n + 1, :] = small[2:3, at]
    bk_o[...] = small[2:3, QW : QW + WIDTH]
    bv_o[...] = small[2:3, QW + WIDTH : QW + 2 * WIDTH]
    lane = lax.broadcasted_iota(jnp.int32, (24, D), 1)
    row = lax.broadcasted_iota(jnp.int32, (24, D), 0)
    own = lane == row + lax.axis_index("dp") * 24
    n2_o[...] = jnp.sum(jnp.where(own, small[0:1, :], 0.0), axis=1)
    n1_o[...] = jnp.sum(jnp.where(own, small[1:2, :], 0.0), axis=1)


def finish(*args):
    shape = jax.ShapeDtypeStruct
    whole = pl.BlockSpec(memory_space=VM)
    return pl.pallas_call(
        finish_kernel,
        name="finish",
        out_shape=(
            shape((TOK, D), BF), shape((TOK, D), BF), shape((24,), F32), shape((24, QW), F32),
            shape((HEADS, WIDTH), F32), shape((24, WIDTH), F32), shape((1, WIDTH), F32),
            shape((24, WIDTH), F32), shape((1, WIDTH), F32), shape((24, QW), F32), shape((24,), F32),
            shape((24, FFL), F32), shape((24, FFL), F32), shape((24, FFL), F32),
        ),
        in_specs=[whole] * 4,
        out_specs=(whole,) * 14,
        compiler_params=pltpu.CompilerParams(vmem_limit_bytes=60 * 2**20),
    )(*args)


def back(*args):
    shape = jax.ShapeDtypeStruct
    whole = pl.BlockSpec(memory_space=VM)
    hbm = pl.BlockSpec(memory_space=pl.ANY)
    dma = pltpu.SemaphoreType.DMA
    regular = pltpu.SemaphoreType.REGULAR
    return pl.pallas_call(
        back_kernel,
        name="back",
        out_shape=(
            shape((4, NU, 24, UW), F32), shape((TOK, D), BF), shape((TOK, D), BF), shape((8, D), F32),
        ),
        in_specs=[hbm] * 4 + [whole] * 2 + [hbm] * 17,
        out_specs=(whole,) * 4,
        scratch_shapes=[
            VM((D, 4 * TOK), BF), VM((D, 4 * TOK), BF), VM((D, 2 * TOK), BF), VM((2 * TOK, QW), BF),
            VM((TOK, D), BF), VM((TOK, D), BF), VM((HALF, D), F32),
            VM((TOK, QW), BF), VM((TOK, WIDTH), BF), VM((TOK, WIDTH), BF),
            VM((TOK, TOK), F32), VM((TOK, WIDTH), F32), VM((TOK, WIDTH), F32),
            VM((D, QW), BF), VM((D, WIDTH), BF), VM((D, WIDTH), BF), VM((QW, D), BF),
            VM((4, NU, 24, UW), F32),
            VM((G_SLOTS, 2, 4, 2, 4, 24, UW), F32),
            VM((R_SLOTS, 2, 2, 4, 24, UW), F32), VM((R_SLOTS, 2, 2, 2, 4, 24, UW), F32),
            VM((R_SLOTS, 2, 2, 24, UW), F32), VM((R_SLOTS, 2, 2, 2, 24, UW), F32),
            VM((2, 4 * TOK, UW), BF),
            VM((4, HALF, D), F32), VM((4, HALF, D), F32),
            VM((2, HALF // 2, D), F32), VM((2, HALF, D), F32),
            VM((TOK, D), F32), VM((TOK, D), F32), VM((HALF, D), F32), VM((D, 2 * TOK), BF),
            VM((TOK, QW), BF), VM((TOK, QW), F32), VM((TOK, QW), F32), VM((2 * TOK, QW), BF),
            VM((2, TOK, WIDTH), F32), VM((2, TOK, WIDTH), F32), VM((2 * TOK, WIDTH), BF),
            VM((TOK, D), F32), VM((HALF, D), F32), VM((HALF, D), F32), VM((TOK, D), F32),
            VM((8, D), F32), VM((13, 8, D), F32),
            dma((R_SLOTS, 4, 2, 2)), dma((R_SLOTS, 4, 2, 2)), dma((NU, 3)), dma((NU, 3)),
            regular((4,)), dma((19,)), dma((19,)), regular((3,)), dma((1,)), dma((2,)),
            dma((10,)), dma((10,)), dma((17,)),
        ],
        compiler_params=pltpu.CompilerParams(
            collective_id=2, has_side_effects=True, vmem_limit_bytes=63 * 2**20
        ),
    )(*args)


def on_device(
    tokens, lengths, keep_mask, norm1_gain, w_query, b_query, w_key, b_key, w_value, b_value,
    w_out, norm2_gain, w_gate, w_up, w_down, cotangent,
):
    q, k, v, mask, cos, sin, h1, la, o2, n2t, dyt, dgu, a, dn2_part, out_part = front(
        lengths, keep_mask, norm1_gain, b_query, b_key, b_value, norm2_gain,
        tokens, cotangent, w_query, w_key, w_value, w_out, w_gate, w_up, w_down,
    )
    results = list(finish(*back(
        dgu, a, dn2_part, out_part, norm1_gain, norm2_gain, n2t, dyt, la, o2, tokens, cotangent, h1,
        q, k, v, mask, cos, sin, w_query, w_key, w_value, w_out,
    )))
    results[9], results[13] = results[9].T, results[13].T
    return tuple(results)


def solution(mesh):
    placed = (
        P("dp", None), P("dp", None), P("dp"), P(), P(None, "tensor"), P("tensor", None),
        P(None, "tensor"), P("tensor", None), P(None, "tensor"), P("tensor", None),
        P("tensor", None), P(), P(None, "tensor"), P(None, "tensor"), P("tensor", None), P("dp", None),
    )
    return jax.shard_map(
        on_device,
        mesh=mesh,
        in_specs=placed,
        out_specs=(
            P("dp", None), P("dp", None), P("dp"), P("dp", "tensor"), P("tensor", None),
            P("dp", "tensor"), P("tensor", None), P("dp", "tensor"), P("tensor", None),
            P("tensor", "dp"), P("dp"), P("dp", "tensor"), P("dp", "tensor"), P("tensor", "dp"),
        ),
        check_vma=False,
    )
```
